32 devices in a mesh: seg: 8 (over z, x), tile: 4 (over y, core).
Axes of the slice: x: 2, y: 2, z: 4, core: 2. Of those that a mesh axis runs over, the one named last changes fastest.
Arguments:
- x_input: bfloat16 [64, 24, 16, 24], P('seg', 'tile'), may hold values from -6 to 6
- expand_w: bfloat16 [24, 144], replicated, may hold values from -1.25 to 1.25
- gain0: float32 [144], replicated, may hold values from 0.25 to 1.75
- bias0: float32 [144], replicated, may hold values from -3 to 3
- dw_kernel: bfloat16 [3, 3, 144], replicated, may hold values from -2 to 2
- gain1: float32 [144], replicated, may hold values from 0.25 to 1.75
- bias1: float32 [144], replicated, may hold values from -3 to 3
- reduce_w: float32 [144, 6], replicated, may hold values from -0.5 to 0.5
- reduce_b: float32 [6], replicated, may hold values from -3 to 3
- restore_w: float32 [6, 144], replicated, may hold values from -2.5 to 2.5
- restore_b: float32 [144], replicated, may hold values from -3 to 3
- project_w: bfloat16 [144, 24], replicated, may hold values from -0.5 to 0.5
- gain2: float32 [24], replicated, may hold values from 0.25 to 1.75
- bias2: float32 [24], replicated, may hold values from -3 to 3
- cotangent: bfloat16 [64, 24, 16, 24], P('seg', 'tile'), may hold values from -6 to 6
- seg_count: int32 [8], P('seg'), may hold values from 1 to 8, as said below
- seg_len: int32 [64], P('seg'), may hold values from 6 to 24, as said below
Outputs:
- block_out: bfloat16 [64, 24, 16, 24], P('seg', 'tile')
- x_grad: bfloat16 [64, 24, 16, 24], P('seg', 'tile')
- expand_w_grad: float32 [24, 144], replicated
- gain0_grad: float32 [144], replicated
- bias0_grad: float32 [144], replicated
- dw_kernel_grad: float32 [3, 3, 144], replicated
- gain1_grad: float32 [144], replicated
- bias1_grad: float32 [144], replicated
- reduce_w_grad: float32 [144, 6], replicated
- reduce_b_grad: float32 [6], replicated
- restore_w_grad: float32 [6, 144], replicated
- restore_b_grad: float32 [144], replicated
- project_w_grad: float32 [144, 24], replicated
- gain2_grad: float32 [24], replicated
- bias2_grad: float32 [24], replicated
- rms_values: float32 [5], replicated
The draws below stay inside these ranges and needn't reach their ends.
Inputs may be any that keep to these rules, and one draw needn't show every extreme that they name: Slots s with s mod 8 below seg_count of their index of seg hold segments, the others are empty; some index has all 8 live, some only one. `seg_len`: frames from the start of a segment; in every index of seg some live segment has all 24 frames.
All inputs are finite; a program needn't handle non-finite values.
Results may differ from the reference program's by a relative error of at most 0.007.
The reference program's roundings to bfloat16 on the way count: a program that leaves them out, or rounds other values in their place, can miss the bound.
Values may be sent and summed in bfloat16 or wider, within the bound.
No kernel may reach another device: no remote copies, remote signals or barrier semaphores. Data moves between devices by JAX's collectives and lax.ppermute only.
A program may use at most 64 MiB of HBM per device.

```python
import jax
import jax.numpy as jnp
from jax import lax

C = 24
E = 144
SQ = 6
TIME = 24
MEL = 16
SEG_DEV = 8
SEGS = 64
N_SEG = 8


def live_counts(key):
    base = jax.random.fold_in(key, 11)
    counts = jax.random.randint(jax.random.fold_in(base, 1), (N_SEG,), 1, SEG_DEV + 1)
    fullest = jax.random.randint(jax.random.fold_in(base, 2), (), 0, N_SEG)
    offset = jax.random.randint(jax.random.fold_in(base, 3), (), 1, N_SEG)
    emptiest = (fullest + offset) % N_SEG
    counts = counts.at[fullest].set(SEG_DEV)
    counts = counts.at[emptiest].set(1)
    return counts.astype(jnp.int32)


def draw_seg_count(key, part):
    return live_counts(key)


def draw_seg_len(key, part):
    counts = live_counts(key)
    key = jax.random.fold_in(key, 5)
    lengths = jax.random.randint(jax.random.fold_in(key, 1), (SEGS,), TIME // 4, TIME + 1)
    chosen = jax.random.randint(jax.random.fold_in(key, 2), (N_SEG,), 0, 1 << 20) % counts
    group_start = jnp.arange(N_SEG, dtype=jnp.int32) * SEG_DEV
    lengths = lengths.at[group_start + chosen].set(TIME)
    short_slot = group_start[0] + (chosen[0] + 1) % SEG_DEV
    lengths = lengths.at[short_slot].set(TIME // 4)
    return lengths.astype(jnp.int32)


def level_of(key, shape, split, least, largest):
    level = 1.0
    for axis_at, parts in split:
        draws = jax.random.uniform(jax.random.fold_in(jax.random.fold_in(key, 6), axis_at), (parts,), jnp.float32, least / len(split), largest / len(split))
        level = level * jnp.repeat(jnp.exp(draws), shape[axis_at] // parts).reshape((-1,) + (1,) * (len(shape) - 1 - axis_at))
    return level


def noise(rng, shape, deviation, reach, cuts=(), held_as=jnp.bfloat16):
    loudness = level_of(rng, shape, cuts, -0.22, 0.18) if cuts else 1.0
    array = jax.random.normal(rng, shape, jnp.float32) * deviation * loudness
    return jnp.minimum(jnp.maximum(array, -reach), reach).astype(held_as)


def setup_inputs(seed: int = 0) -> dict:
    key_of = jax.random.split(jax.random.key(seed), 18)
    return {
        "x_input": noise(key_of[0], (SEGS, TIME, MEL, C), 1.0, 6.0, ((0, 8), (1, 4))),
        "expand_w": noise(key_of[1], (C, E), C ** -0.5, 1.25),
        "gain0": jnp.clip(1.0 + 0.15 * jax.random.normal(key_of[2], (E,), jnp.float32), 0.25, 1.75),
        "bias0": noise(key_of[3], (E,), 0.5, 3.0, (), jnp.float32),
        "dw_kernel": noise(key_of[4], (3, 3, E), 9 ** -0.5, 2.0),
        "gain1": jnp.clip(1.0 + 0.15 * jax.random.normal(key_of[5], (E,), jnp.float32), 0.25, 1.75),
        "bias1": noise(key_of[6], (E,), 0.5, 3.0, (), jnp.float32),
        "reduce_w": noise(key_of[7], (E, SQ), E ** -0.5, 0.5, (), jnp.float32),
        "reduce_b": noise(key_of[8], (SQ,), 0.5, 3.0, (), jnp.float32),
        "restore_w": noise(key_of[9], (SQ, E), SQ ** -0.5, 2.5, (), jnp.float32),
        "restore_b": noise(key_of[10], (E,), 0.5, 3.0, (), jnp.float32),
        "project_w": noise(key_of[11], (E, C), E ** -0.5, 0.5),
        "gain2": jnp.clip(1.0 + 0.15 * jax.random.normal(key_of[12], (C,), jnp.float32), 0.25, 1.75),
        "bias2": noise(key_of[13], (C,), 0.5, 3.0, (), jnp.float32),
        "cotangent": noise(key_of[14], (SEGS, TIME, MEL, C), 1.0, 6.0, ((0, 8), (1, 4))),
        "seg_count": draw_seg_count(jax.random.fold_in(key_of[17], 71), 0),
        "seg_len": draw_seg_len(jax.random.fold_in(key_of[17], 71), 0),
    }


EPSILON = 0.001
PRECISE = lax.Precision.HIGHEST

@jax.custom_vjp
def low(v):
    return lax.optimization_barrier(v.astype(jnp.bfloat16)).astype(jnp.float32)

@jax.custom_vjp
def low_back(v):
    return v

def low_keep(v):
    return (low(v), None)

def low_pass(kept, grad):
    return (grad,)

def back_keep(v):
    return (v, None)

def back_low(kept, grad):
    return (low(grad),)
low.defvjp(low_keep, low_pass)
low_back.defvjp(back_keep, back_low)

def swish(values):
    return values * jax.nn.sigmoid(values)

def batch_norm(values, weights, total, gain, bias):
    mean_val = lax.optimization_barrier(jnp.sum(values * weights, axis=(0, 1, 2))) / total
    centred = values - mean_val
    variance = lax.optimization_barrier(jnp.sum(centred * centred * weights, axis=(0, 1, 2))) / total
    return centred * lax.rsqrt(variance + EPSILON) * gain + bias

def depthwise(field, kernel):
    padded = jnp.pad(field, ((0, 0), (1, 1), (1, 1), (0, 0)))
    result = jnp.zeros(field.shape, jnp.float32)
    for row in range(3):
        for col in range(3):
            result = result + padded[:, row:row + TIME, col:col + MEL, :] * kernel[row, col]
    return result

def reference(x_input, expand_w, gain0, bias0, dw_kernel, gain1, bias1, reduce_w, reduce_b, restore_w, restore_b, project_w, gain2, bias2, cotangent, seg_count, seg_len):
    slot_index = jnp.arange(SEGS, dtype=jnp.int32)
    is_live = slot_index % SEG_DEV < seg_count[slot_index // SEG_DEV]
    time_index = jnp.arange(TIME, dtype=jnp.int32)
    valid = is_live[:, None] & (time_index[None, :] < seg_len[:, None])
    frame_mask = valid.astype(jnp.float32)[:, :, None, None]
    total = jnp.sum(frame_mask) * MEL
    seg_frames = jnp.maximum(lax.optimization_barrier(jnp.sum(frame_mask, axis=(1, 2, 3))) * MEL, 1.0)

    def forward(x_val, ew, g0, b0, kern, g1, b1, rw, rb, sw, sb, pw, g2, b2):
        expanded = low_back(jnp.einsum('stmc,cd->stmd', x_val, ew, precision=PRECISE))
        act0 = low(swish(batch_norm(expanded, frame_mask, total, g0, b0)) * frame_mask)
        deep = low_back(depthwise(act0, kern))
        act1 = swish(batch_norm(deep, frame_mask, total, g1, b1)) * frame_mask
        pooled = lax.optimization_barrier(jnp.sum(act1, axis=(1, 2))) / seg_frames[:, None]
        squeezed = swish(jnp.dot(pooled, rw, precision=PRECISE) + rb)
        gate = jax.nn.sigmoid(jnp.dot(squeezed, sw, precision=PRECISE) + sb)
        act2 = low(act1 * gate[:, None, None, :])
        projected = low_back(jnp.einsum('stme,ec->stmc', act2, pw, precision=PRECISE))
        branch = batch_norm(projected, frame_mask, total, g2, b2) * frame_mask
        result = x_val + branch
        return (result, (act0, act1, act2, branch))
    params = (x_input.astype(jnp.float32), expand_w.astype(jnp.float32), gain0.astype(jnp.float32), bias0.astype(jnp.float32), dw_kernel.astype(jnp.float32), gain1.astype(jnp.float32), bias1.astype(jnp.float32), reduce_w.astype(jnp.float32), reduce_b.astype(jnp.float32), restore_w.astype(jnp.float32), restore_b.astype(jnp.float32), project_w.astype(jnp.float32), gain2.astype(jnp.float32), bias2.astype(jnp.float32))
    result, pullback, inner = jax.vjp(forward, *params, has_aux=True)
    act0, act1, act2, branch = inner
    grads = pullback(cotangent.astype(jnp.float32))

    def mean_square(values, chans):
        return jnp.sqrt(jnp.sum(frame_mask * values * values) / (total * chans))
    rms_values = jnp.stack([mean_square(result, C), mean_square(act0, E), mean_square(act1, E), mean_square(act2, E), mean_square(branch, C)])
    return (result.astype(jnp.bfloat16), grads[0].astype(jnp.bfloat16), grads[1], grads[2], grads[3], grads[4], grads[5], grads[6], grads[7], grads[8], grads[9], grads[10], grads[11], grads[12], grads[13], rms_values)
```

```python
import functools
from typing import NamedTuple

import jax
import jax.numpy as jnp
from jax import lax
from jax.experimental import pallas as pl
from jax.experimental.pallas import tpu as pltpu
from jax.sharding import PartitionSpec as P

EPSILON = 0.001
BOTH = ("seg", "tile")
LANES = 128
F32 = jnp.float32
BF16 = jnp.bfloat16
VMEM = pl.BlockSpec(memory_space=pltpu.VMEM)
SMEM = pl.BlockSpec(memory_space=pltpu.SMEM)
HBM = pl.BlockSpec(memory_space=pltpu.HBM)


class Sizes(NamedTuple):
    devices: int
    tiles: int
    segs: int
    own: int
    rows: int
    width: int
    chans: int
    wide: int
    squeeze: int


def iota(shape, dim):
    return lax.broadcasted_iota(jnp.int32, shape, dim)


def dot(left, right, left_dim, right_dim, precise=False):
    return lax.dot_general(
        left,
        right,
        (((left_dim,), (right_dim,)), ((), ())),
        precision=lax.Precision.HIGHEST if precise else None,
        preferred_element_type=F32,
    )


def eye(rows, cols, dtype=F32):
    return (iota((rows, cols), 0) == iota((rows, cols), 1)).astype(dtype)


def spread(column):
    return jnp.broadcast_to(column, (column.shape[0], LANES))


def lane_sum(values):
    return jnp.sum(values, axis=1, keepdims=True)


def sigmoid(values):
    return 0.5 * jnp.tanh(0.5 * values) + 0.5


def vector(ref):
    return ref[...].astype(F32).reshape(1, ref.shape[0])


def thirds(values):
    high = values.astype(BF16)
    rest = values - high.astype(F32)
    middle = rest.astype(BF16)
    return [high, middle, (rest - middle.astype(F32)).astype(BF16)]


def doubled(values):
    high = values.astype(BF16)
    return jnp.concatenate([high, (values - high.astype(F32)).astype(BF16)], axis=1)


def tripled(values):
    return jnp.concatenate(thirds(values), axis=1)


def row_sums(values):
    return dot(jnp.ones((8, 3 * LANES), BF16), tripled(values), 1, 1)[0:1]


def padded_rows(rows, count):
    spare = count - sum(row.shape[0] for row in rows)
    if spare:
        rows = rows + [jnp.zeros((spare, rows[0].shape[1]), F32)]
    return jnp.concatenate(rows, axis=0)


def spread_by(rows, unit):
    held = jnp.concatenate(thirds(rows), axis=0)
    return dot(held, jnp.concatenate([unit] * 3, axis=0), 0, 0)


def spread_rows(rows):
    count = len(rows)
    shape = (16, count * LANES)
    unit = jnp.where(iota(shape, 0) == lax.div(iota(shape, 1), LANES), 1.0, 0.0).astype(BF16)
    wide = spread_by(padded_rows(rows, 16), unit)
    return [wide[:, at * LANES : (at + 1) * LANES] for at in range(count)]


def columns_of(rows):
    held = padded_rows(rows, 8)
    width = held.shape[1]
    spare = (-width) % LANES
    if spare:
        held = jnp.concatenate([held, jnp.zeros((8, spare), F32)], axis=1)
    return held.T[:width]


def placed_cells(cells, first):
    rows = cells.shape[0]
    parts = [jnp.zeros((first, LANES), F32)] if first else []
    parts += [cells, jnp.zeros((LANES - first - rows, LANES), F32)]
    return jnp.concatenate(parts, axis=0).astype(BF16)


def placed_sums(acc_ref, count, start):
    lane = iota((2 * LANES, LANES), 1)
    result = 0.0
    for at in range(count):
        unit = jnp.where(lane == start + at, 1.0, 0.0).astype(BF16)
        result = result + dot(doubled(acc_ref[at]), unit, 1, 0)
    return result


def lane_at(sz):
    lane = iota((1, LANES), 1)
    step = sz.width * sz.own
    return lax.rem(lane, sz.width), lax.rem(lax.div(lane, sz.width), sz.own), lax.div(lane, step)


def seg_lanes(sz, rows):
    slot = lax.rem(lax.div(iota((rows, LANES), 1), sz.width), sz.own)
    return jnp.where(slot == iota((rows, LANES), 0), 1.0, 0.0).astype(BF16)


def seg_sums(sz, values):
    lanes = seg_lanes(sz, 16)
    return dot(jnp.concatenate([lanes] * 3, axis=1), tripled(values), 1, 1)[0:8]


def seg_spread(sz, rows):
    return spread_by(padded_rows([rows], 16), seg_lanes(sz, 16))


def mask_rows(sz, info):
    return [info[t : t + 1] for t in range(sz.rows)]


def half_of(ref, t, e):
    first = e - e % 16
    return ref[t, first : first + 16].astype(F32)[e - first : e - first + 8]


def shift_unit(sz):
    source = iota((LANES, 2 * LANES), 0)
    column = iota((LANES, 2 * LANES), 1)
    lane = lax.rem(column, LANES)
    spot = lax.rem(lane, sz.width)
    left = jnp.where((source == lane - 1) & (spot != 0), 1.0, 0.0)
    right = jnp.where((source == lane + 1) & (spot != sz.width - 1), 1.0, 0.0)
    return jnp.where(column < LANES, left, right).astype(BF16)


def block_unit(sz):
    source = iota((LANES, 2 * LANES), 0)
    column = iota((LANES, 2 * LANES), 1)
    lane = lax.rem(column, LANES)
    step = sz.width * sz.own
    before = jnp.where(source == lane - step, 1.0, 0.0)
    after = jnp.where(source == lane + step, 1.0, 0.0)
    return jnp.where(column < LANES, before, after).astype(BF16)


def field_shifts(sz, fields, sh_ref, unit_ref, exact):
    deep = LANES if exact else 2 * LANES

    def parts(values):
        return values.astype(BF16) if exact else doubled(values)

    before = dot(parts(fields[-1]), unit_ref[0:deep, 2 * LANES : 3 * LANES], 1, 0)
    after = dot(parts(fields[0]), unit_ref[0:deep, 3 * LANES :], 1, 0)
    rows = [before] + fields + [after]
    cells = parts(jnp.concatenate(rows, axis=0))
    sides = dot(cells, unit_ref[0:deep, 0 : 2 * LANES], 1, 0)
    for t, row in enumerate(rows):
        part = slice(t * sz.wide, (t + 1) * sz.wide)
        sh_ref[0, t] = sides[part, :LANES]
        sh_ref[1, t] = row
        sh_ref[2, t] = sides[part, LANES:]


def backward_parts(sz, sh_ref, tap_ref, part, acts, acc_ref):
    result = [0.0] * sz.rows
    for i in range(3):
        for j in range(3):
            tap = tap_ref[3 * i + j, part]
            held = 0.0
            for t in range(sz.rows):
                field = sh_ref[2 - j, t + 2 - i, part]
                result[t] = result[t] + field * tap
                if acts is not None:
                    held = held + field * acts[t]
            if acts is not None:
                acc_ref[3 * i + j, part] = held
    return result


def every(sz, ref, first, step):
    return ref[pl.ds(first, sz.devices, stride=step), :]


def wide_rows(first, second, half, last):
    tail = [first[:, LANES:], second[:, LANES:], jnp.zeros((1, LANES - 2 * half), F32)]
    tail = jnp.concatenate(tail, axis=1)
    return jnp.concatenate([first[:, :LANES], second[:, :LANES], tail, last], axis=0)


def wide_pair(block, half):
    first = jnp.concatenate([block[0:1], block[2:3, :half]], axis=1)
    second = jnp.concatenate([block[1:2], block[2:3, half : 2 * half]], axis=1)
    return first, second


def wide_moments(sz, ref, half):
    sums, squares, tails, counts = (every(sz, ref, at, 4) for at in range(4))
    total = jnp.sum(counts, axis=0, keepdims=True)
    inverse = 1.0 / jnp.maximum(counts, 1.0)
    means = []
    spares = []
    for held in (sums, tails):
        mean_val = jnp.sum(held, axis=0, keepdims=True) / total
        offset = held - counts * mean_val
        means.append(mean_val)
        spares.append(jnp.sum(offset * offset * inverse, axis=0, keepdims=True))
    low = jnp.sum(squares, axis=0, keepdims=True) + spares[0]
    high = jnp.sum(tails, axis=0, keepdims=True)[:, half : 2 * half] + spares[1][:, :half]
    square = jnp.concatenate([low, high], axis=1)
    mean_row = jnp.concatenate([means[0], means[1][:, :half]], axis=1)
    total_row = jnp.concatenate([total, total[:, :half]], axis=1)
    return mean_row, lax.rsqrt(square / total_row + EPSILON), total_row


def send_block(ref, block):
    count = block.shape[0]
    if count < 8:
        block = jnp.concatenate([block] * (8 // count), axis=0)
    for at in range(0, ref.shape[0], 8):
        ref[at : at + 8] = block


def partner(sz, step):
    return lax.rem(lax.axis_index("tile") + step, sz.tiles)


def entry_kernel(sz, x_hbm, w_hbm, len_hbm, count_hbm, pay_ref, *scratch):
    x_ref, w_ref, len_ref, count_ref, sems = scratch
    copies = [
        pltpu.make_async_copy(x_hbm, x_ref, sems.at[0]),
        pltpu.make_async_copy(w_hbm, w_ref, sems.at[1]),
        pltpu.make_async_copy(len_hbm, len_ref, sems.at[2]),
        pltpu.make_async_copy(count_hbm, count_ref, sems.at[3]),
    ]
    for copy in copies:
        copy.start()
    for copy in reversed(copies):
        copy.wait()
    tile_pos = lax.axis_index("tile")
    lane_seg = lax.div(iota((1, LANES), 1), sz.width)
    length = jnp.zeros((1, LANES), jnp.int32)
    count = jnp.zeros((), jnp.int32)
    for s in range(sz.segs):
        held = jnp.where(s < count_ref[0], len_ref[s], 0)
        length = jnp.where(lane_seg == s, held, length)
        count = count + jnp.clip(held - tile_pos * sz.rows, 0, sz.rows)
    count = (count * sz.width).astype(F32)
    masks = [(tile_pos * sz.rows + t < length).astype(F32) for t in range(sz.rows)]
    unit = eye(sz.chans, sz.chans, BF16)
    cells = [dot(unit, x_ref[:, t].reshape(LANES, sz.chans), 1, 1) for t in range(sz.rows)]
    sums = lane_sum(sum(cells[t] * masks[t] for t in range(sz.rows)))
    mean_val = spread(sums / jnp.maximum(count, 1.0))
    centred = [(cells[t] - mean_val) * masks[t] for t in range(sz.rows)]
    centred = jnp.concatenate(centred, axis=1)
    spare = dot(centred, centred, 1, 1, True)
    weights = w_ref[...].astype(F32)
    wide_sum = dot(jnp.broadcast_to(sums, (sz.chans, 8)), weights, 0, 0, True)[0:1]
    square = jnp.sum(dot(spare, weights, 1, 0, True) * weights, axis=0, keepdims=True)
    last = jnp.full((1, LANES), count, F32)
    send_block(pay_ref, wide_rows(wide_sum, square, sz.wide - LANES, last))


def send_kernel(sz, x_ref, c_ref, after_ref, *out_refs):
    del after_ref
    for step, out_ref in enumerate(out_refs):
        first = partner(sz, step) * sz.own
        out_ref[...] = jnp.zeros(out_ref.shape, BF16)
        for t in range(sz.rows):
            at = (t % 2) * 2 * sz.chans
            out_ref[:, t // 2, :, at : at + sz.chans] = x_ref[pl.ds(first, sz.own), t]
            at = at + sz.chans
            out_ref[:, t // 2, :, at : at + sz.chans] = c_ref[pl.ds(first, sz.own), t]


def setup_kernel(sz, *refs):
    wide_refs, small_refs, dw_ref, rw_ref, sw_ref, pw_in, w_in, len_ref, count_ref = (
        refs[0:5],
        refs[5:8],
        *refs[8:15],
    )
    par_ref, tap_ref, unit_ref, info_ref, pw_ref, w_ref = refs[15:]
    par_ref[...] = jnp.zeros(par_ref.shape, F32)
    for at, ref in enumerate(wide_refs):
        par_ref[at : at + 1] = vector(ref)
    for at, ref in enumerate(small_refs):
        par_ref[5 + at : 6 + at, 0 : ref.shape[0]] = vector(ref)
    par_ref[8 : 8 + sz.squeeze] = rw_ref[...]
    par_ref[16 : 16 + sz.squeeze] = sw_ref[...]
    pw_ref[...] = pw_in[...]
    w_ref[...] = w_in[...]
    taps = spread_rows([dw_ref[i, j : j + 1].astype(F32) for i in range(3) for j in range(3)])
    for at in range(9):
        tap_ref[at] = taps[at]
    for at, unit in enumerate([shift_unit(sz), block_unit(sz)]):
        part = slice(at * 2 * LANES, (at + 1) * 2 * LANES)
        unit_ref[0:LANES, part] = unit
        unit_ref[LANES:, part] = unit
    first = lax.axis_index("tile") * sz.own
    _, slot, block = lane_at(sz)
    length = jnp.zeros((1, LANES), jnp.int32)
    count = jnp.zeros((), jnp.int32)
    at = iota((8, LANES), 0)
    frames = jnp.ones((8, LANES), F32)
    for s in range(sz.own):
        held = jnp.where(first + s < count_ref[0], len_ref[first + s], 0)
        length = jnp.where(slot == s, held, length)
        count = count + jnp.minimum(held, sz.rows * sz.tiles)
        frame = jnp.maximum((held * sz.width).astype(F32), 1.0)
        frames = jnp.where(at == s, frame, frames)
    for t in range(sz.rows):
        info_ref[t : t + 1] = (block * sz.rows + t < length).astype(F32)
    info_ref[7:8] = jnp.full((1, LANES), (count * sz.width).astype(F32))
    info_ref[8:16] = frames


def gather_kernel(sz, *refs):
    own_refs, (w_ref, exp_ref, xc_ref, all_ref) = refs[: sz.tiles], refs[sz.tiles :]
    for step, ref in enumerate(own_refs):
        all_ref[partner(sz, sz.tiles - step)] = ref[...]
    unit = eye(LANES, LANES, BF16)
    weights = w_ref[...]
    for g in range(sz.rows // 2):
        flat = dot(unit, all_ref[:, :, g].reshape(LANES, LANES), 1, 1)
        for par in range(2):
            at = par * 2 * sz.chans
            t = 2 * g + par
            x_at = flat[at : at + sz.chans]
            xc_ref[t] = flat[at : at + 2 * sz.chans].astype(BF16)
            exp_ref[t] = dot(weights, x_at.astype(BF16), 0, 0)


def stage_one_kernel(sz, pay_ref, exp_ref, xc_ref, par_ref, tap_ref, unit_ref, info_ref, *refs):
    out_pay, act0_ref, deep_ref, ec_ref, s0_ref, row_ref, near_ref, part_ref = refs[:8]
    mat_ref, acc_ref, sh_ref, buf_ref = refs[8:]
    chans = sz.chans
    half = sz.wide - LANES
    mean0, inv0, total = wide_moments(sz, pay_ref, half)
    row_ref[0:1] = mean0
    row_ref[1:2] = inv0
    row_ref[2:3] = total
    info = info_ref[...]
    masks = mask_rows(sz, info)
    count = info[7:8]
    mean_c, slope_c, bias_c = spread_rows([mean0, inv0 * par_ref[0:1], par_ref[1:2]])
    acts = []
    squares = 0.0
    for t in range(sz.rows):
        centred = exp_ref[t] - mean_c
        pre = centred * slope_c + bias_c
        gate = sigmoid(pre)
        held = pre * gate
        ec_ref[t] = centred
        s0_ref[t] = (gate + held * (1.0 - gate)) * masks[t]
        act = (held * masks[t]).astype(BF16)
        act0_ref[t] = act
        act = act.astype(F32)
        squares = squares + act * act
        acts.append(act)
    field_shifts(sz, acts, sh_ref, unit_ref, True)
    step = sz.width * sz.own
    spot, _, block = lane_at(sz)
    full = [jnp.broadcast_to(mask, (8, LANES)) for mask in masks]
    before = jnp.where(block == 0, 0.0, pltpu.roll(full[-1], step, 1))
    after = jnp.where(block == sz.tiles - 1, 0.0, pltpu.roll(full[0], LANES - step, 1))
    full = [before] + full + [after]
    left = [jnp.where(spot == 0, 0.0, row) for row in full]
    right = [jnp.where(spot == sz.width - 1, 0.0, row) for row in full]
    moved = [right, full, left]
    total_sum = []
    for e in range(0, sz.wide, 8):
        part = slice(e, e + 8)
        taps = [tap_ref[at, part] for at in range(9)]
        acts = [half_of(act0_ref, t, e) for t in range(sz.rows)]
        sums = 0.0
        for t in range(sz.rows):
            deep = 0.0
            back = 0.0
            for i in range(3):
                for j in range(3):
                    deep = deep + sh_ref[j, t + i, part] * taps[3 * i + j]
                    back = back + moved[j][t + 2 - i] * taps[3 * i + j]
            deep_ref[t, part] = deep
            sums = sums + deep * masks[t]
            mat_ref[t, part] = back * s0_ref[t, part]
        total_sum.append(sums)
        for i in range(3):
            for j in range(3):
                held = sum(moved[j][t + 2 - i] * acts[t] for t in range(sz.rows))
                acc_ref[3 * i + j, part] = held
    total_sum = jnp.concatenate(total_sum, axis=0)
    mean_own = lane_sum(total_sum) / jnp.maximum(count[:, 0:1], 1.0)
    square = 0.0
    for t in range(sz.rows):
        centred = (deep_ref[t] - mean_own) * masks[t]
        square = square + centred * centred
    send_block(out_pay, wide_rows(row_sums(total_sum), row_sums(square), half, count))
    part_ref[...] = placed_sums(acc_ref, 9, 3 * chans + 9)
    held = jnp.zeros((sz.wide, LANES), F32)
    second = jnp.zeros((chans, chans), F32)
    x_sum = 0.0
    for t in range(sz.rows):
        x_at = xc_ref[t].astype(F32)[:chans]
        cells = placed_cells(x_at, 0)
        held = held + dot(doubled(mat_ref[t]), jnp.concatenate([cells, cells], axis=1), 1, 1)
        kept = x_at * masks[t]
        second = second + dot(kept.astype(BF16), x_at.astype(BF16), 1, 1)
        x_sum = x_sum + kept
    near_ref[...] = jnp.zeros(near_ref.shape, F32)
    buf_ref[...] = held
    for k in range(5):
        rows = min(32, sz.wide - 32 * k)
        near_ref[0:rows, chans * k : chans * (k + 1)] = buf_ref[32 * k : 32 * k + rows, 0:chans]
    near_ref[16:32, 4 * chans : 5 * chans] = second[0:16]
    near_ref[0:chans, 5 * chans : LANES] = second[:, 16:]
    x_row = row_sums(x_sum)
    for k in range(3):
        near_ref[chans + k : chans + k + 1, 5 * chans : LANES] = x_row[:, 8 * k : 8 * k + 8]
    squares = jnp.sum(squares.reshape(sz.wide // 8, 8, LANES), axis=0)
    squares = jnp.sum(lane_sum(squares), axis=0, keepdims=True)
    near_ref[chans + 3 : chans + 4, 5 * chans : 5 * chans + 1] = squares


def stage_two_kernel(
    sz,
    pay_ref,
    deep_ref,
    xc_ref,
    par_ref,
    tap_ref,
    unit_ref,
    info_ref,
    pw_ref,
    near_ref,
    act0_ref,
    s0_ref,
    part_ref,
    out_pay,
    act1_ref,
    dc_ref,
    s1_ref,
    proj_ref,
    gate_ref,
    seg_ref,
    row_ref,
    buf_ref,
    sq_ref,
    mat_ref,
    acc_ref,
    sh_ref,
):
    chans = sz.chans
    half = sz.wide - LANES
    mean1, inv1, _ = wide_moments(sz, pay_ref, half)
    row_ref[0:1] = mean1
    row_ref[1:2] = inv1
    info = info_ref[...]
    masks = mask_rows(sz, info)
    count = info[7:8]
    mean_c, slope_c, bias_c = spread_rows([mean1, inv1 * par_ref[2:3], par_ref[3:4]])
    pool = 0.0
    squares = 0.0
    fields = []
    for t in range(sz.rows):
        centred = deep_ref[t] - mean_c
        pre = centred * slope_c + bias_c
        gate = sigmoid(pre)
        held = pre * gate
        dc_ref[t] = centred
        s1_ref[t] = (gate + held * (1.0 - gate)) * masks[t]
        act = held * masks[t]
        act1_ref[t] = act
        pool = pool + act
        squares = squares + act * act
        fields.append(centred * masks[t])
    pooled = seg_sums(sz, pool) / info[8:16, 0:1]
    rw = par_ref[8:16]
    sw = par_ref[16:24]
    squeeze_pre = dot(pooled, rw, 1, 1, True) + par_ref[7:8, 0:8]
    squeezed = squeeze_pre * sigmoid(squeeze_pre)
    gate = sigmoid(dot(squeezed, sw, 1, 0, True) + par_ref[4:5])
    seg_ref[0] = pooled
    seg_ref[1] = gate
    seg_ref[2, :, 0:8] = squeeze_pre
    gate_wide = seg_spread(sz, gate)
    gate_ref[...] = gate_wide
    sums = 0.0
    sum_g = 0.0
    gated = 0.0
    for t in range(sz.rows):
        act = (act1_ref[t] * gate_wide).astype(BF16)
        cells = dot(pw_ref[...], act, 1, 0)
        proj_ref[t] = cells
        sums = sums + cells * masks[t]
        sum_g = sum_g + xc_ref[t].astype(F32)[chans:] * masks[t]
        act = act.astype(F32)
        gated = gated + act * act
    sq_ref[0:8] = jnp.sum(squares.reshape(sz.wide // 8, 8, LANES), axis=0)
    sq_ref[8:16] = jnp.sum(gated.reshape(sz.wide // 8, 8, LANES), axis=0)
    mean_own = lane_sum(sums) / jnp.maximum(count[:, 0:1], 1.0)
    square = 0.0
    sum_gp = 0.0
    for t in range(sz.rows):
        centred = (proj_ref[t] - mean_own) * masks[t]
        square = square + centred * centred
        sum_gp = sum_gp + centred * xc_ref[t].astype(F32)[chans:]
    row = row_sums(jnp.concatenate([sums, square, sum_g, sum_gp], axis=0))
    row = jnp.concatenate([row, count[:, 4 * chans :]], axis=1)
    each = near_ref.shape[0] // sz.devices
    out_pay[pl.ds(0, sz.devices, stride=2), :] = jnp.broadcast_to(row, (sz.devices, LANES))
    out_pay[pl.ds(1, sz.devices, stride=2), :] = near_ref[...]
    field_shifts(sz, fields, sh_ref, unit_ref, False)
    for e in range(0, sz.wide, 8):
        part = slice(e, e + 8)
        acts = [half_of(act0_ref, t, e) for t in range(sz.rows)]
        back = backward_parts(sz, sh_ref, tap_ref, part, acts, acc_ref)
        for t in range(sz.rows):
            mat_ref[t, part] = back[t] * s0_ref[t, part]
    buf = part_ref[...] + placed_sums(acc_ref, 9, 3 * chans + 18)
    for t in range(sz.rows):
        cells = placed_cells(xc_ref[t].astype(F32)[:chans], chans)
        buf = buf + dot(doubled(mat_ref[t]), jnp.concatenate([cells, cells], axis=1), 1, 1)
    buf_ref[...] = buf


def stage_three_kernel(
    sz,
    pay_ref,
    proj_ref,
    xc_ref,
    act0_ref,
    act1_ref,
    s0_ref,
    dc_ref,
    s1_ref,
    gate_ref,
    seg_ref,
    par_ref,
    tap_ref,
    unit_ref,
    info_ref,
    pw_ref,
    part_ref,
    sq_ref,
    row_ref,
    out_pay,
    res_ref,
    scaled_ref,
    bg2_ref,
    gg2_ref,
    ga_ref,
    mat_ref,
    acc_ref,
    sh_ref,
    buf_ref,
):
    chans = sz.chans
    half = sz.wide - LANES
    info = info_ref[...]
    masks = mask_rows(sz, info)
    parts = every(sz, pay_ref, 0, 2)
    near = every(sz, pay_ref, 1, 2)
    sums = jnp.sum(parts, axis=0, keepdims=True)
    counts = pltpu.roll(parts, LANES - 4 * chans, 1)
    grads = pltpu.roll(parts, LANES - 2 * chans, 1)
    total = sums[:, 4 * chans : 4 * chans + 1]
    mean_row = sums / total
    offset = parts - counts * mean_row
    scaled = offset / jnp.maximum(counts, 1.0)
    spare = jnp.sum(offset * scaled, axis=0, keepdims=True)
    cross = jnp.sum(scaled * grads, axis=0, keepdims=True)
    square = sums[:, chans : 2 * chans] + spare[:, :chans]
    inv2 = lax.rsqrt(square / total + EPSILON)
    bias_grad = sums[:, 2 * chans : 3 * chans]
    gain_grad = inv2 * (sums[:, 3 * chans : 4 * chans] + cross[:, :chans])
    bg2_ref[...] = bias_grad.reshape(chans)
    gg2_ref[...] = gain_grad.reshape(chans)
    rows = [mean_row[:, :chans], inv2, bias_grad / total, gain_grad / total]
    rows += [par_ref[5:6, :chans], par_ref[6:7, :chans]]
    columns = columns_of(rows)
    mean_c, inv_c, bg_c, gg_c, gain_c, bias_c = (
        spread(columns[:, at : at + 1]) for at in range(6)
    )
    scale = inv_c * gain_c
    gate_wide = gate_ref[...]
    branch_sq = 0.0
    result_sq = 0.0
    gate_sum = 0.0
    buf = part_ref[...]
    for t in range(sz.rows):
        both = xc_ref[t].astype(F32)
        normed = (proj_ref[t] - mean_c) * inv_c
        branch = (normed * gain_c + bias_c) * masks[t]
        result = both[:chans] + branch
        res_ref[t] = result
        branch_sq = branch_sq + branch * branch
        result_sq = result_sq + result * result * masks[t]
        grad = scale * (both[chans:] - (bg_c + normed * gg_c)) * masks[t]
        wide_grad = dot(pw_ref[...], grad.astype(BF16), 0, 0)
        ga_ref[t] = wide_grad
        act = act1_ref[t]
        gate_sum = gate_sum + wide_grad * act
        act = (act * gate_wide).astype(BF16)
        buf = buf + dot(act, placed_cells(grad, 2 * chans), 1, 1)
    rw = par_ref[8:16]
    sw = par_ref[16:24]
    pooled = seg_ref[0]
    gate = seg_ref[1]
    squeeze_pre = seg_ref[2, :, 0:8]
    slope = sigmoid(squeeze_pre)
    squeezed = squeeze_pre * slope
    slope = slope + squeezed * (1.0 - slope)
    live = (iota((8, 1), 0) < sz.own).astype(F32)
    gate_pre = seg_sums(sz, gate_sum) * gate * (1.0 - gate)
    squeeze_grad = dot(gate_pre, sw, 1, 1, True) * slope * live
    back = dot(squeeze_grad, rw, 1, 0, True) / info[8:16, 0:1]
    back_wide = seg_spread(sz, back)
    (scale_c,) = spread_rows([row_ref[1:2] * par_ref[2:3]])
    sum_b = 0.0
    sum_g = 0.0
    fields = []
    for t in range(sz.rows):
        grad = (ga_ref[t] * gate_wide + back_wide) * s1_ref[t]
        scaled_ref[t] = grad * scale_c
        sum_b = sum_b + grad
        sum_g = sum_g + grad * dc_ref[t]
        fields.append(grad)
    sum_b = row_sums(sum_b)
    sum_g = row_sums(sum_g) * row_ref[1:2]
    field_shifts(sz, fields, sh_ref, unit_ref, False)
    for e in range(0, sz.wide, 8):
        part = slice(e, e + 8)
        acts = [half_of(act0_ref, t, e) for t in range(sz.rows)]
        back = backward_parts(sz, sh_ref, tap_ref, part, acts, acc_ref)
        for t in range(sz.rows):
            mat_ref[t, part] = back[t] * s0_ref[t, part]
    buf = buf + placed_sums(acc_ref, 9, 3 * chans)
    for t in range(sz.rows):
        cells = placed_cells(xc_ref[t].astype(F32)[:chans], 0)
        buf = buf + dot(doubled(mat_ref[t]), jnp.concatenate([cells, cells], axis=1), 1, 1)
    at = 3 * chans + 27
    small = [dot(squeezed, gate_pre, 0, 0, True)[: sz.squeeze]]
    small.append(dot(squeeze_grad, pooled, 0, 0, True)[: sz.squeeze])
    small.append(jnp.sum(gate_pre, axis=0, keepdims=True))
    shape = (16, LANES)
    unit = jnp.where(iota(shape, 0) + at == iota(shape, 1), 1.0, 0.0).astype(BF16)
    buf_ref[...] = buf + spread_by(padded_rows(small, 16), unit)
    at = at + 2 * sz.squeeze + 1
    spots = iota((8, 1), 0)
    held = jnp.sum(squeeze_grad, axis=0, keepdims=True)
    column = jnp.zeros((8, 1), F32)
    for k in range(sz.squeeze):
        column = jnp.where(spots == k, held[:, k : k + 1], column)
    buf_ref[0:8, at : at + 1] = column
    column = jnp.zeros((8, 1), F32)
    squares = [
        jnp.sum(result_sq.reshape(chans // 8, 8, LANES), axis=0),
        sq_ref[0:8],
        sq_ref[8:16],
        jnp.sum(branch_sq.reshape(chans // 8, 8, LANES), axis=0),
    ]
    for k, square in enumerate(squares):
        value = jnp.sum(lane_sum(square), axis=0, keepdims=True)
        column = jnp.where(spots == k, value, column)
    buf_ref[8:16, at : at + 1] = column
    used = at + 1
    piece = LANES - used
    for k in range(-(-used // piece)):
        take = min(piece, used - k * piece)
        buf_ref[k * half : (k + 1) * half, used : used + take] = buf_ref[
            LANES : LANES + half, k * piece : k * piece + take
        ]
    each = LANES // sz.devices
    last = jnp.sum(near, axis=0, keepdims=True)
    block = wide_rows(sum_b, sum_g, half, last)
    send_block(out_pay, jnp.concatenate([block, jnp.zeros((4, LANES), F32)], axis=0))
    for k in range(each):
        held = buf_ref[pl.ds(k, sz.devices, stride=each), :]
        out_pay[pl.ds(4 + k, sz.devices, stride=8), :] = held


def stage_four_kernel(
    sz, pay_ref, scaled_ref, dc_ref, ec_ref, s0_ref, row0_ref, row1_ref, par_ref, *refs
):
    tap_ref, unit_ref, info_ref, out_pay, gp0_ref, bg1_ref, gg1_ref, mid_ref, sh_ref = refs
    half = sz.wide - LANES
    masks = mask_rows(sz, info_ref[...])
    block = jnp.sum(pay_ref[...].reshape(sz.devices, 8, LANES), axis=0)
    bias_grad, gain_grad = wide_pair(block, half)
    bg1_ref[...] = bias_grad.reshape(sz.wide)
    gg1_ref[...] = gain_grad.reshape(sz.wide)
    mid_ref[0:1] = bias_grad
    mid_ref[1:2] = gain_grad
    inv1 = row1_ref[1:2]
    scale = inv1 * par_ref[2:3] / row0_ref[2:3]
    bg_c, gg_c = spread_rows([bias_grad * scale, gain_grad * inv1 * scale])
    fields = []
    for t in range(sz.rows):
        grad = scaled_ref[t] - masks[t] * (bg_c + dc_ref[t] * gg_c)
        fields.append(grad.astype(BF16).astype(F32))
    field_shifts(sz, fields, sh_ref, unit_ref, True)
    total_b = []
    total_g = []
    for e in range(0, sz.wide, 8):
        part = slice(e, e + 8)
        back = backward_parts(sz, sh_ref, tap_ref, part, None, None)
        sum_b = 0.0
        sum_g = 0.0
        for t in range(sz.rows):
            grad = back[t] * s0_ref[t, part]
            gp0_ref[t, part] = grad
            sum_b = sum_b + grad
            sum_g = sum_g + grad * ec_ref[t, part]
        total_b.append(sum_b)
        total_g.append(sum_g)
    sum_b = row_sums(jnp.concatenate(total_b, axis=0))
    sum_g = row_sums(jnp.concatenate(total_g, axis=0)) * row0_ref[1:2]
    top = wide_rows(sum_b, sum_g, half, jnp.zeros((1, LANES), F32))
    send_block(out_pay, jnp.concatenate([top, block[4:8]], axis=0))


def back_kernel(sz, gp0_ref, res_ref, row0_ref, par_ref, w_ref, *refs):
    out_refs, all_ref = refs[:-1], refs[-1]
    chans = sz.chans
    (scale,) = spread_rows([row0_ref[1:2] * par_ref[0:1]])
    weights = w_ref[...]
    for g in range(sz.rows // 2):
        pieces = []
        for par in range(2):
            t = 2 * g + par
            pieces += [res_ref[t], dot(weights, (gp0_ref[t] * scale).astype(BF16), 1, 0)]
        pieces.append(jnp.zeros((LANES - 4 * chans, LANES), F32))
        turned = jnp.concatenate(pieces, axis=0).T.astype(BF16)
        all_ref[:, :, g] = turned.reshape(sz.tiles, sz.own, sz.width, LANES)
    for step, out_ref in enumerate(out_refs):
        out_ref[...] = all_ref[partner(sz, step)]


def far_kernel(sz, pay_ref, row0_ref, w_ref, after_ref, far_ref, buf_ref, near_ref):
    del after_ref
    chans = sz.chans
    held = every(sz, pay_ref, 3, 8)
    near_ref[...] = held[0:32]
    buf_ref[...] = jnp.zeros(buf_ref.shape, F32)
    for k in range(5):
        rows = min(32, sz.wide - 32 * k)
        buf_ref[32 * k : 32 * k + rows, 0:chans] = near_ref[0:rows, chans * k : chans * (k + 1)]
    far_ref[0:chans] = dot(eye(chans, LANES), buf_ref[...], 1, 1, True)
    x_row = [near_ref[chans + k : chans + k + 1, 5 * chans : LANES] for k in range(3)]
    x_row = jnp.concatenate(x_row, axis=1)
    x_column = columns_of([x_row])[:, 0:1]
    right = near_ref[0:chans, 5 * chans : LANES]
    below = right.T[0:8, 0:16]
    below = jnp.concatenate([below, right[16:chans]], axis=1)
    second = jnp.concatenate([near_ref[16:32, 4 * chans : 5 * chans], below], axis=0)
    second = second - x_column * x_row / row0_ref[2:3, :chans]
    wide = dot(second, w_ref[...].astype(F32), 1, 0, True)
    far_ref[chans : 2 * chans] = wide * row0_ref[1:2]
    far_ref[2 * chans : 3 * chans, 0:1] = x_column
    far_ref[3 * chans : 3 * chans + 1, 0:1] = near_ref[
        chans + 3 : chans + 4, 5 * chans : 5 * chans + 1
    ]


def return_kernel(sz, *refs):
    got_refs = refs[: sz.tiles]
    c_ref, out_ref, pre_ref = refs[sz.tiles :]
    chans = sz.chans
    for step, ref in enumerate(got_refs):
        first = partner(sz, sz.tiles - step) * sz.own
        for t in range(sz.rows):
            at = (t % 2) * 2 * chans
            out_ref[pl.ds(first, sz.own), t] = ref[:, t // 2, :, at : at + chans]
            back = ref[:, t // 2, :, at + chans : at + 2 * chans].astype(F32)
            pre_ref[pl.ds(first, sz.own), t] = back + c_ref[pl.ds(first, sz.own), t].astype(F32)


def last_kernel(
    sz,
    pay_ref,
    pre_ref,
    x_ref,
    far_ref,
    row0_ref,
    row1_ref,
    mid_ref,
    par_ref,
    w_ref,
    len_ref,
    count_ref,
    xg_ref,
    ew_ref,
    gg0_ref,
    bg0_ref,
    dw_ref,
    rw_ref,
    rb_ref,
    sw_ref,
    sb_ref,
    pw_ref,
    rms_ref,
    buf_ref,
):
    chans = sz.chans
    half = sz.wide - LANES
    each = LANES // sz.devices
    block = [jnp.sum(every(sz, pay_ref, at, 8), axis=0, keepdims=True) for at in range(3)]
    bias_grad, gain_grad = wide_pair(jnp.concatenate(block, axis=0), half)
    bg0_ref[...] = bias_grad.reshape(sz.wide)
    gg0_ref[...] = gain_grad.reshape(sz.wide)
    mean0 = row0_ref[0:1]
    inv0 = row0_ref[1:2]
    total = row0_ref[2:3]
    scale0 = inv0 * par_ref[0:1]
    bias_row = bias_grad / total
    gain_row = gain_grad / total
    weights = w_ref[...].astype(F32)
    factor = scale0 * gain_row * inv0
    matrix = dot(weights * factor, weights, 1, 1, True)
    offset = jnp.broadcast_to(scale0 * bias_row - factor * mean0, (8, sz.wide))
    offset = dot(offset, weights, 1, 1, True)[0:1]
    high = matrix.astype(BF16)
    low = (matrix - high.astype(F32)).astype(BF16)
    first = lax.axis_index("tile") * sz.rows
    for t in range(sz.rows):
        cells = x_ref[:, t].reshape(sz.segs * sz.width, chans)
        back = dot(cells, high, 1, 0) + dot(cells, low, 1, 0) + offset
        for s in range(sz.segs):
            length = jnp.where(s < count_ref[0], len_ref[s], 0)
            live = jnp.where(first + t < length, 1.0, 0.0)
            held = back[s * sz.width : (s + 1) * sz.width] * live
            xg_ref[s, t] = (pre_ref[s, t] - held).astype(BF16)
    used = 3 * chans + 29 + 2 * sz.squeeze
    piece = LANES - used
    for k in range(each):
        buf_ref[pl.ds(k, sz.devices, stride=each), :] = every(sz, pay_ref, 4 + k, 8)
    buf_ref[LANES:] = jnp.zeros((half, LANES), F32)
    for k in range(-(-used // piece)):
        take = min(piece, used - k * piece)
        buf_ref[LANES : LANES + half, k * piece : k * piece + take] = buf_ref[
            k * half : (k + 1) * half, used : used + take
        ]
    rows = dot(eye(LANES, LANES), buf_ref[...], 1, 1, True)
    inv1 = row1_ref[1:2]
    scale1 = inv1 * par_ref[2:3]
    bias1 = mid_ref[0:1] / total
    gain1 = mid_ref[1:2] * inv1 / total
    inner = rows[0:chans] - far_ref[0:chans] * bias1 - rows[chans : 2 * chans] * gain1
    x_sum = far_ref[2 * chans : 3 * chans, 0:1]
    ew_ref[...] = scale0 * (
        scale1 * inner - x_sum * bias_row - far_ref[chans : 2 * chans] * gain_row
    )
    pw_ref[...] = rows[2 * chans : 3 * chans]
    spot = 3 * chans
    held = rows[spot : spot + 9] - rows[spot + 9 : spot + 18] * bias1
    held = scale1 * (held - rows[spot + 18 : spot + 27] * gain1)
    for i in range(3):
        dw_ref[i] = held[3 * i : 3 * i + 3]
    spot = spot + 27
    sw_ref[...] = rows[spot : spot + sz.squeeze]
    spot = spot + sz.squeeze
    rw_ref[...] = rows[spot : spot + sz.squeeze]
    spot = spot + sz.squeeze
    sb_ref[...] = rows[spot : spot + 1].reshape(sz.wide)
    misc = rows[spot + 1 : spot + 2]
    rb_ref[...] = misc[:, : sz.squeeze].reshape(sz.squeeze)
    act0_sq = far_ref[3 * chans : 3 * chans + 1, 0:1]
    squares = jnp.concatenate(
        [misc[:, 8:9], act0_sq, misc[:, 9:10], misc[:, 10:11], misc[:, 11:12]], axis=1
    )
    chan_row = jnp.where(
        (iota((1, 5), 1) == 0) | (iota((1, 5), 1) == 4), float(chans), float(sz.wide)
    )
    rms_ref[...] = jnp.sqrt(squares / (total[:, :5] * chan_row)).reshape(5)


def call(kernel, sz, args, kinds, outs, scratch=(), cost=1.0, room=16):
    spaces = {"v": VMEM, "s": SMEM, "h": HBM, "a": pl.BlockSpec(memory_space=pl.ANY)}
    kinds = kinds + "v" * (len(args) - len(kinds))
    return pl.pallas_call(
        functools.partial(kernel, sz),
        out_shape=tuple(jax.ShapeDtypeStruct(shape, kind) for shape, kind in outs),
        in_specs=[spaces[kind] for kind in kinds],
        out_specs=tuple(VMEM for _ in outs),
        scratch_shapes=[pltpu.VMEM(*held) if isinstance(held, tuple) else held for held in scratch],
        compiler_params=pltpu.CompilerParams(vmem_limit_bytes=room * 1024 * 1024),
        cost_estimate=pl.CostEstimate(
            flops=int(cost * 1e9), bytes_accessed=int(cost * 3e6), transcendentals=0
        ),
        name=kernel.__name__,
    )(*args)


def everywhere(values):
    return lax.all_to_all(values, BOTH, 0, 0, tiled=True)


def passed(sz, parts):
    result = [parts[0]]
    for step in range(1, sz.tiles):
        pairs = [(i, (i + step) % sz.tiles) for i in range(sz.tiles)]
        result.append(lax.ppermute(parts[step], "tile", pairs))
    return result


def shards(
    x_input,
    expand_w,
    gain0,
    bias0,
    dw_kernel,
    gain1,
    bias1,
    reduce_w,
    reduce_b,
    restore_w,
    restore_b,
    project_w,
    gain2,
    bias2,
    cotangent,
    seg_count,
    seg_len,
):
    segs, rows, width, chans = x_input.shape
    wide, squeeze = reduce_w.shape
    tiles = lax.axis_size("tile")
    devices = lax.axis_size("seg") * tiles
    own = segs // tiles
    sz = Sizes(devices, tiles, segs, own, rows, width, chans, wide, squeeze)
    big = ((rows, wide, LANES), F32)
    small = ((rows, chans, LANES), F32)
    block = ((own, rows // 2, width, LANES), BF16)
    packed = ((rows, wide, LANES), BF16)
    both = ((rows, 2 * chans, LANES), BF16)
    column = ((wide, LANES), F32)
    taps = ((9, wide, LANES), F32)
    shifts = ((3, rows + 2, wide, LANES), F32)

    def pay_of(count):
        return ((devices * count, LANES), F32)

    (pay,) = call(
        entry_kernel,
        sz,
        [x_input, expand_w, seg_len, seg_count],
        "hhhh",
        [pay_of(4)],
        [
            (x_input.shape, BF16),
            (expand_w.shape, BF16),
            pltpu.SMEM(seg_len.shape, jnp.int32),
            pltpu.SMEM(seg_count.shape, jnp.int32),
            pltpu.SemaphoreType.DMA((4,)),
        ],
        room=60,
    )
    parts = call(send_kernel, sz, [x_input, cotangent, pay], "vva", [block] * tiles)
    par, tap, unit, info, pw_near, w_near = call(
        setup_kernel,
        sz,
        [gain0, bias0, gain1, bias1, restore_b, gain2, bias2, reduce_b, dw_kernel, reduce_w.T]
        + [restore_w, project_w.T, expand_w, seg_len, seg_count],
        "v" * 13 + "ss",
        [
            ((24, wide), F32),
            taps,
            ((2 * LANES, 4 * LANES), BF16),
            ((16, LANES), F32),
            ((chans, wide), BF16),
            ((chans, wide), BF16),
        ],
    )
    pay = everywhere(pay)
    parts = passed(sz, parts)
    exp, x_c = call(
        gather_kernel, sz, parts + [w_near], "", [big, both], [((tiles,) + block[0], BF16)]
    )
    pay, act0, deep, ec, s0, row0, near, part = call(
        stage_one_kernel,
        sz,
        [pay, exp, x_c, par, tap, unit, info],
        "",
        [pay_of(4), packed, big, big, big, ((3, wide), F32)]
        + [((max(32, devices), LANES), F32), column],
        [big, taps, shifts, column],
    )
    pay = everywhere(pay)
    pay, act1, dc, s1, proj, gate, seg_rows, row1, part, squares = call(
        stage_two_kernel,
        sz,
        [pay, deep, x_c, par, tap, unit, info, pw_near, near, act0, s0, part],
        "",
        [pay_of(2), big, big, big, small, column, ((3, 8, wide), F32), ((2, wide), F32)]
        + [column, ((16, LANES), F32)],
        [big, taps, shifts],
    )
    pay = everywhere(pay)
    pay, res, scaled, bg2, gg2 = call(
        stage_three_kernel,
        sz,
        [pay, proj, x_c, act0, act1, s0, dc, s1, gate, seg_rows, par, tap, unit, info]
        + [pw_near, part, squares, row1],
        "",
        [pay_of(8), small, big, ((chans,), F32), ((chans,), F32)],
        [big, big, taps, shifts, column],
    )
    far_pay = everywhere(pay)
    pay, gp0, bg1, gg1, mid = call(
        stage_four_kernel,
        sz,
        [far_pay, scaled, dc, ec, s0, row0, row1, par, tap, unit, info],
        "",
        [pay_of(8), big, ((wide,), F32), ((wide,), F32), ((2, wide), F32)],
        [shifts],
    )
    sent = call(
        back_kernel,
        sz,
        [gp0, res, row0, par, w_near],
        "",
        [block] * tiles,
        [((tiles,) + block[0], BF16)],
    )
    pay = everywhere(pay)
    (far,) = call(
        far_kernel,
        sz,
        [far_pay, row0, w_near, gp0],
        "vvva",
        [((3 * chans + 8, wide), F32)],
        [column, ((32, LANES), F32)],
    )
    sent = passed(sz, sent)
    block_out, pre = call(
        return_kernel,
        sz,
        sent + [cotangent],
        "",
        [(x_input.shape, BF16), (x_input.shape, F32)],
    )
    x_grad, ew, gg0, bg0, dw, rw, rb, sw, sb, pw, rms = call(
        last_kernel,
        sz,
        [pay, pre, x_input, far, row0, row1, mid, par, w_near, seg_len, seg_count],
        "v" * 9 + "ss",
        [
            (x_input.shape, BF16),
            ((chans, wide), F32),
            ((wide,), F32),
            ((wide,), F32),
            (dw_kernel.shape, F32),
            ((squeeze, wide), F32),
            ((squeeze,), F32),
            ((squeeze, wide), F32),
            ((wide,), F32),
            ((chans, wide), F32),
            ((5,), F32),
        ],
        [column],
    )
    return (
        block_out,
        x_grad,
        ew,
        gg0,
        bg0,
        dw,
        gg1,
        bg1,
        rw.T,
        rb,
        sw,
        sb,
        pw.T,
        gg2,
        bg2,
        rms,
    )


def solution(mesh):
    split = P("seg", "tile", None, None)
    return jax.shard_map(
        shards,
        mesh=mesh,
        in_specs=(split,) + (P(),) * 13 + (split, P("seg"), P("seg")),
        out_specs=(split, split) + (P(),) * 14,
        check_vma=False,
    )
```

```python
import functools
from typing import NamedTuple

import jax
import jax.numpy as jnp
from jax import lax
from jax.experimental import pallas as pl
from jax.experimental.pallas import tpu as pltpu
from jax.sharding import PartitionSpec as P

EPSILON = 0.001
BOTH = ("seg", "tile")
LANES = 128
F32 = jnp.float32
BF16 = jnp.bfloat16
VMEM = pl.BlockSpec(memory_space=pltpu.VMEM)
SMEM = pl.BlockSpec(memory_space=pltpu.SMEM)
HBM = pl.BlockSpec(memory_space=pltpu.HBM)


class Sizes(NamedTuple):
    devices: int
    tiles: int
    segs: int
    own: int
    rows: int
    width: int
    chans: int
    wide: int
    squeeze: int


def iota(shape, dim):
    return lax.broadcasted_iota(jnp.int32, shape, dim)


def dot(left, right, left_dim, right_dim, precise=False):
    return lax.dot_general(
        left,
        right,
        (((left_dim,), (right_dim,)), ((), ())),
        precision=lax.Precision.HIGHEST if precise else None,
        preferred_element_type=F32,
    )


def eye(rows, cols, dtype=F32):
    return (iota((rows, cols), 0) == iota((rows, cols), 1)).astype(dtype)


def spread(column):
    return jnp.broadcast_to(column, (column.shape[0], LANES))


def lane_sum(values):
    return jnp.sum(values, axis=1, keepdims=True)


def sigmoid(values):
    return 0.5 * jnp.tanh(0.5 * values) + 0.5


def vector(ref):
    return ref[...].astype(F32).reshape(1, ref.shape[0])


def thirds(values):
    high = values.astype(BF16)
    rest = values - high.astype(F32)
    middle = rest.astype(BF16)
    return [high, middle, (rest - middle.astype(F32)).astype(BF16)]


def doubled(values):
    high = values.astype(BF16)
    return jnp.concatenate([high, (values - high.astype(F32)).astype(BF16)], axis=1)


def tripled(values):
    return jnp.concatenate(thirds(values), axis=1)


def row_sums(values):
    return dot(jnp.ones((8, 3 * LANES), BF16), tripled(values), 1, 1)[0:1]


def padded_rows(rows, count):
    spare = count - sum(row.shape[0] for row in rows)
    if spare:
        rows = rows + [jnp.zeros((spare, rows[0].shape[1]), F32)]
    return jnp.concatenate(rows, axis=0)


def spread_by(rows, unit):
    held = jnp.concatenate(thirds(rows), axis=0)
    return dot(held, jnp.concatenate([unit] * 3, axis=0), 0, 0)


def spread_rows(rows):
    count = len(rows)
    shape = (16, count * LANES)
    unit = jnp.where(iota(shape, 0) == lax.div(iota(shape, 1), LANES), 1.0, 0.0).astype(BF16)
    wide = spread_by(padded_rows(rows, 16), unit)
    return [wide[:, at * LANES : (at + 1) * LANES] for at in range(count)]


def columns_of(rows):
    held = padded_rows(rows, 8)
    width = held.shape[1]
    spare = (-width) % LANES
    if spare:
        held = jnp.concatenate([held, jnp.zeros((8, spare), F32)], axis=1)
    return held.T[:width]


def turned(cells):
    rows, width = cells.shape
    spare = (-width) % LANES
    held = jnp.concatenate([cells.astype(F32), jnp.zeros((rows, spare), F32)], axis=1)
    return held.T[:width].astype(cells.dtype)


def placed_cells(cells, first):
    rows = cells.shape[0]
    parts = [jnp.zeros((first, LANES), F32)] if first else []
    parts += [cells, jnp.zeros((LANES - first - rows, LANES), F32)]
    return jnp.concatenate(parts, axis=0).astype(BF16)


def placed_sums(acc_ref, count, start):
    lane = iota((2 * LANES, LANES), 1)
    result = 0.0
    for at in range(count):
        unit = jnp.where(lane == start + at, 1.0, 0.0).astype(BF16)
        result = result + dot(doubled(acc_ref[at]), unit, 1, 0)
    return result


def lane_at(sz):
    lane = iota((1, LANES), 1)
    step = sz.width * sz.own
    return lax.rem(lane, sz.width), lax.rem(lax.div(lane, sz.width), sz.own), lax.div(lane, step)


def seg_lanes(sz, rows):
    slot = lax.rem(lax.div(iota((rows, LANES), 1), sz.width), sz.own)
    return jnp.where(slot == iota((rows, LANES), 0), 1.0, 0.0).astype(BF16)


def seg_sums(sz, values):
    lanes = seg_lanes(sz, 16)
    return dot(jnp.concatenate([lanes] * 3, axis=1), tripled(values), 1, 1)[0:8]


def seg_spread(sz, rows):
    return spread_by(padded_rows([rows], 16), seg_lanes(sz, 16))


def mask_rows(sz, info):
    return [info[t : t + 1] for t in range(sz.rows)]


def half_of(ref, t, e):
    first = e - e % 16
    return ref[t, first : first + 16].astype(F32)[e - first : e - first + 8]


def shift_unit(sz):
    source = iota((LANES, 2 * LANES), 0)
    column = iota((LANES, 2 * LANES), 1)
    lane = lax.rem(column, LANES)
    spot = lax.rem(lane, sz.width)
    left = jnp.where((source == lane - 1) & (spot != 0), 1.0, 0.0)
    right = jnp.where((source == lane + 1) & (spot != sz.width - 1), 1.0, 0.0)
    return jnp.where(column < LANES, left, right).astype(BF16)


def block_unit(sz):
    source = iota((LANES, 2 * LANES), 0)
    column = iota((LANES, 2 * LANES), 1)
    lane = lax.rem(column, LANES)
    step = sz.width * sz.own
    before = jnp.where(source == lane - step, 1.0, 0.0)
    after = jnp.where(source == lane + step, 1.0, 0.0)
    return jnp.where(column < LANES, before, after).astype(BF16)


def field_shifts(sz, fields, sh_ref, unit_ref, exact):
    deep = LANES if exact else 2 * LANES

    def parts(values):
        return values.astype(BF16) if exact else doubled(values)

    before = dot(parts(fields[-1]), unit_ref[0:deep, 2 * LANES : 3 * LANES], 1, 0)
    after = dot(parts(fields[0]), unit_ref[0:deep, 3 * LANES :], 1, 0)
    rows = [before] + fields + [after]
    cells = parts(jnp.concatenate(rows, axis=0))
    sides = dot(cells, unit_ref[0:deep, 0 : 2 * LANES], 1, 0)
    for t, row in enumerate(rows):
        part = slice(t * sz.wide, (t + 1) * sz.wide)
        sh_ref[0, t] = sides[part, :LANES]
        sh_ref[1, t] = row
        sh_ref[2, t] = sides[part, LANES:]


def backward_parts(sz, sh_ref, tap_ref, part, acts, acc_ref):
    result = [0.0] * sz.rows
    for i in range(3):
        for j in range(3):
            tap = tap_ref[3 * i + j, part]
            held = 0.0
            for t in range(sz.rows):
                field = sh_ref[2 - j, t + 2 - i, part]
                result[t] = result[t] + field * tap
                if acts is not None:
                    held = held + field * acts[t]
            if acts is not None:
                acc_ref[3 * i + j, part] = held
    return result


def every(sz, ref, first, step):
    return ref[pl.ds(first, sz.devices, stride=step), :]


def wide_rows(first, second, half, last):
    tail = [first[:, LANES:], second[:, LANES:], jnp.zeros((1, LANES - 2 * half), F32)]
    tail = jnp.concatenate(tail, axis=1)
    return jnp.concatenate([first[:, :LANES], second[:, :LANES], tail, last], axis=0)


def wide_pair(block, half):
    first = jnp.concatenate([block[0:1], block[2:3, :half]], axis=1)
    second = jnp.concatenate([block[1:2], block[2:3, half : 2 * half]], axis=1)
    return first, second


def wide_moments(sz, ref, half):
    sums, squares, tails, counts = (every(sz, ref, at, 4) for at in range(4))
    total = jnp.sum(counts, axis=0, keepdims=True)
    inverse = 1.0 / jnp.maximum(counts, 1.0)
    means = []
    spares = []
    for held in (sums, tails):
        mean_val = jnp.sum(held, axis=0, keepdims=True) / total
        offset = held - counts * mean_val
        means.append(mean_val)
        spares.append(jnp.sum(offset * offset * inverse, axis=0, keepdims=True))
    low = jnp.sum(squares, axis=0, keepdims=True) + spares[0]
    high = jnp.sum(tails, axis=0, keepdims=True)[:, half : 2 * half] + spares[1][:, :half]
    square = jnp.concatenate([low, high], axis=1)
    mean_row = jnp.concatenate([means[0], means[1][:, :half]], axis=1)
    total_row = jnp.concatenate([total, total[:, :half]], axis=1)
    return mean_row, lax.rsqrt(square / total_row + EPSILON), total_row


def send_block(ref, block):
    count = block.shape[0]
    if count < 8:
        block = jnp.concatenate([block] * (8 // count), axis=0)
    for at in range(0, ref.shape[0], 8):
        ref[at : at + 8] = block


def partner(step):
    return lax.bitwise_xor(lax.axis_index("tile"), step)


def entry_kernel(sz, x_hbm, w_hbm, len_hbm, count_hbm, pay_ref, *scratch):
    x_ref, w_ref, len_ref, count_ref, sems = scratch
    copies = [
        pltpu.make_async_copy(len_hbm, len_ref, sems.at[0]),
        pltpu.make_async_copy(count_hbm, count_ref, sems.at[1]),
        pltpu.make_async_copy(w_hbm, w_ref, sems.at[2]),
    ]
    for s in range(sz.segs):
        copies.append(pltpu.make_async_copy(x_hbm.at[s], x_ref.at[s], sems.at[3 + s]))
    for copy in copies:
        copy.start()
    for copy in copies[:3]:
        copy.wait()
    tile_pos = lax.axis_index("tile")
    lane_seg = lax.div(iota((1, LANES), 1), sz.width)
    length = jnp.zeros((1, LANES), jnp.int32)
    count = jnp.zeros((), jnp.int32)
    for s in range(sz.segs):
        held = jnp.where(s < count_ref[0], len_ref[s], 0)
        length = jnp.where(lane_seg == s, held, length)
        count = count + jnp.clip(held - tile_pos * sz.rows, 0, sz.rows)
    count = (count * sz.width).astype(F32)
    masks = [(tile_pos * sz.rows + t < length).astype(F32) for t in range(sz.rows)]
    weights = w_ref[...]
    for copy in copies[3:]:
        copy.wait()
    unit = eye(sz.chans, sz.chans, BF16)
    cells = [dot(unit, x_ref[:, t].reshape(LANES, sz.chans), 1, 1) for t in range(sz.rows)]
    total = 0.0
    for t in range(sz.rows):
        total = total + cells[t] * masks[t]
    x_row = padded_rows([row_sums(total)], 16)
    wide_sum = dot(jnp.concatenate(thirds(x_row), axis=0), weights, 1, 0)
    wide_sum = wide_sum[0:1] + wide_sum[16:17] + wide_sum[32:33]
    mean_val = lane_sum(total) / jnp.maximum(count, 1.0)
    centred = [(cells[t] - mean_val) * masks[t] for t in range(sz.rows)]
    centred = jnp.concatenate(centred, axis=1)
    spare = dot(centred, centred, 1, 1, True)
    wide = sum(dot(held, weights, 1, 0) for held in thirds(spare))
    square = jnp.sum(wide * weights.astype(F32), axis=0, keepdims=True)
    last = jnp.full((1, LANES), count, F32)
    send_block(pay_ref, wide_rows(wide_sum, square, sz.wide - LANES, last))


def send_kernel(sz, x_ref, c_ref, after_ref, *out_refs):
    del after_ref
    for step, out_ref in enumerate(out_refs):
        first = partner(step) * sz.own
        out_ref[...] = jnp.zeros(out_ref.shape, BF16)
        for t in range(sz.rows):
            at = (t % 2) * 2 * sz.chans
            out_ref[:, t // 2, :, at : at + sz.chans] = x_ref[pl.ds(first, sz.own), t]
            at = at + sz.chans
            out_ref[:, t // 2, :, at : at + sz.chans] = c_ref[pl.ds(first, sz.own), t]


def setup_kernel(sz, *refs):
    wide_refs, small_refs, dw_ref, rw_ref, sw_ref, pw_in, w_in, len_ref, count_ref = (
        refs[0:5],
        refs[5:8],
        *refs[8:15],
    )
    par_ref, tap_ref, unit_ref, info_ref, pw_ref, pwt_ref, w_ref, wt_ref, far_info = refs[15:]
    par_ref[...] = jnp.zeros(par_ref.shape, F32)
    for at, ref in enumerate(wide_refs):
        par_ref[at : at + 1] = vector(ref)
    for at, ref in enumerate(small_refs):
        par_ref[5 + at : 6 + at, 0 : ref.shape[0]] = vector(ref)
    par_ref[8 : 8 + sz.squeeze] = rw_ref[...]
    par_ref[16 : 16 + sz.squeeze] = sw_ref[...]
    pw_ref[...] = pw_in[...]
    pwt_ref[...] = turned(pw_in[...])
    w_ref[...] = w_in[...]
    wt_ref[...] = turned(w_in[...])
    taps = spread_rows([dw_ref[i, j : j + 1].astype(F32) for i in range(3) for j in range(3)])
    for at in range(9):
        tap_ref[at] = taps[at]
    for at, unit in enumerate([shift_unit(sz), block_unit(sz)]):
        part = slice(at * 2 * LANES, (at + 1) * 2 * LANES)
        unit_ref[0:LANES, part] = unit
        unit_ref[LANES:, part] = unit
    first = lax.axis_index("tile") * sz.own
    _, slot, block = lane_at(sz)
    length = jnp.zeros((1, LANES), jnp.int32)
    count = jnp.zeros((), jnp.int32)
    at = iota((8, LANES), 0)
    frames = jnp.ones((8, LANES), F32)
    for s in range(sz.own):
        held = jnp.where(first + s < count_ref[0], len_ref[first + s], 0)
        length = jnp.where(slot == s, held, length)
        count = count + jnp.minimum(held, sz.rows * sz.tiles)
        frame = jnp.maximum((held * sz.width).astype(F32), 1.0)
        frames = jnp.where(at == s, frame, frames)
    for t in range(sz.rows):
        info_ref[t : t + 1] = (block * sz.rows + t < length).astype(F32)
    info_ref[7:8] = jnp.full((1, LANES), (count * sz.width).astype(F32))
    info_ref[8:16] = frames
    lane_seg = lax.div(iota((1, LANES), 1), sz.width)
    length = jnp.zeros((1, LANES), jnp.int32)
    for s in range(sz.segs):
        held = jnp.where(s < count_ref[0], len_ref[s], 0)
        length = jnp.where(lane_seg == s, held, length)
    far_info[...] = jnp.zeros(far_info.shape, F32)
    first = lax.axis_index("tile") * sz.rows
    for t in range(sz.rows):
        far_info[t : t + 1] = (first + t < length).astype(F32)


def stage_one_kernel(sz, pay_ref, *refs):
    own_refs = refs[: sz.tiles]
    wt_ref, par_ref, tap_ref, unit_ref, info_ref = refs[sz.tiles : sz.tiles + 5]
    refs = refs[sz.tiles + 5 :]
    out_pay, xc_ref, act0_ref, deep_ref, ec_ref, s0_ref, row_ref, near_ref, part_ref = refs[:9]
    mat_ref, acc_ref, sh_ref, buf_ref, all_ref = refs[9:]
    for step, ref in enumerate(own_refs):
        all_ref[partner(step)] = ref[...]
    unit = eye(LANES, LANES, BF16)
    expanded = []
    for g in range(sz.rows // 2):
        flat = dot(unit, all_ref[:, :, g].reshape(LANES, LANES), 1, 1)
        for par in range(2):
            at = par * 2 * sz.chans
            xc_ref[2 * g + par] = flat[at : at + 2 * sz.chans].astype(BF16)
            cells = flat[at : at + sz.chans].astype(BF16)
            expanded.append(dot(wt_ref[...], cells, 1, 0))
    chans = sz.chans
    half = sz.wide - LANES
    mean0, inv0, total = wide_moments(sz, pay_ref, half)
    row_ref[0:1] = mean0
    row_ref[1:2] = inv0
    row_ref[2:3] = total
    info = info_ref[...]
    masks = mask_rows(sz, info)
    count = info[7:8]
    mean_c, slope_c, bias_c = spread_rows([mean0, inv0 * par_ref[0:1], par_ref[1:2]])
    acts = []
    squares = 0.0
    for t in range(sz.rows):
        centred = expanded[t] - mean_c
        pre = centred * slope_c + bias_c
        gate = sigmoid(pre)
        held = pre * gate
        ec_ref[t] = centred
        s0_ref[t] = (gate + held * (1.0 - gate)) * masks[t]
        act = (held * masks[t]).astype(BF16)
        act0_ref[t] = act
        act = act.astype(F32)
        squares = squares + act * act
        acts.append(act)
    field_shifts(sz, acts, sh_ref, unit_ref, True)
    step = sz.width * sz.own
    spot, _, block = lane_at(sz)
    full = [jnp.broadcast_to(mask, (8, LANES)) for mask in masks]
    before = jnp.where(block == 0, 0.0, pltpu.roll(full[-1], step, 1))
    after = jnp.where(block == sz.tiles - 1, 0.0, pltpu.roll(full[0], LANES - step, 1))
    full = [before] + full + [after]
    left = jnp.broadcast_to(jnp.where(spot == 0, 0.0, 1.0), (8, LANES))
    right = jnp.broadcast_to(jnp.where(spot == sz.width - 1, 0.0, 1.0), (8, LANES))
    total_sum = []
    for e in range(0, sz.wide, 8):
        part = slice(e, e + 8)
        taps = [tap_ref[at, part] for at in range(9)]
        acts = [half_of(act0_ref, t, e) for t in range(sz.rows)]
        sums = 0.0
        edged = [taps[3 * i] * right + taps[3 * i + 1] + taps[3 * i + 2] * left for i in range(3)]
        for t in range(sz.rows):
            deep = 0.0
            back = 0.0
            for i in range(3):
                back = back + full[t + 2 - i] * edged[i]
                for j in range(3):
                    deep = deep + sh_ref[j, t + i, part] * taps[3 * i + j]
            deep_ref[t, part] = deep
            sums = sums + deep * masks[t]
            mat_ref[t, part] = back * s0_ref[t, part]
        total_sum.append(sums)
        for i in range(3):
            held = sum(full[t + 2 - i] * acts[t] for t in range(sz.rows))
            acc_ref[3 * i, part] = held * right
            acc_ref[3 * i + 1, part] = held
            acc_ref[3 * i + 2, part] = held * left
    total_sum = jnp.concatenate(total_sum, axis=0)
    mean_own = lane_sum(total_sum) / jnp.maximum(count[:, 0:1], 1.0)
    square = 0.0
    for t in range(sz.rows):
        centred = (deep_ref[t] - mean_own) * masks[t]
        square = square + centred * centred
    send_block(out_pay, wide_rows(row_sums(total_sum), row_sums(square), half, count))
    part_ref[...] = placed_sums(acc_ref, 9, 3 * chans + 9)
    held = jnp.zeros((sz.wide, LANES), F32)
    second = jnp.zeros((chans, chans), F32)
    x_sum = 0.0
    for t in range(sz.rows):
        x_at = xc_ref[t].astype(F32)[:chans]
        cells = placed_cells(x_at, 0)
        held = held + dot(doubled(mat_ref[t]), jnp.concatenate([cells, cells], axis=1), 1, 1)
        kept = x_at * masks[t]
        second = second + dot(kept.astype(BF16), x_at.astype(BF16), 1, 1)
        x_sum = x_sum + kept
    near_ref[...] = jnp.zeros(near_ref.shape, F32)
    buf_ref[...] = held
    for k in range(5):
        rows = min(32, sz.wide - 32 * k)
        near_ref[0:rows, chans * k : chans * (k + 1)] = buf_ref[32 * k : 32 * k + rows, 0:chans]
    near_ref[16:32, 4 * chans : 5 * chans] = second[0:16]
    near_ref[0:chans, 5 * chans : LANES] = second[:, 16:]
    x_row = row_sums(x_sum)
    for k in range(3):
        near_ref[chans + k : chans + k + 1, 5 * chans : LANES] = x_row[:, 8 * k : 8 * k + 8]
    squares = jnp.sum(squares.reshape(sz.wide // 8, 8, LANES), axis=0)
    squares = jnp.sum(lane_sum(squares), axis=0, keepdims=True)
    near_ref[chans + 3 : chans + 4, 5 * chans : 5 * chans + 1] = squares


def stage_two_kernel(
    sz,
    pay_ref,
    deep_ref,
    xc_ref,
    par_ref,
    tap_ref,
    unit_ref,
    info_ref,
    pw_ref,
    near_ref,
    act0_ref,
    s0_ref,
    part_ref,
    out_pay,
    act1_ref,
    dc_ref,
    s1_ref,
    proj_ref,
    gate_ref,
    seg_ref,
    row_ref,
    buf_ref,
    sq_ref,
    mat_ref,
    acc_ref,
    sh_ref,
):
    chans = sz.chans
    half = sz.wide - LANES
    mean1, inv1, _ = wide_moments(sz, pay_ref, half)
    row_ref[0:1] = mean1
    row_ref[1:2] = inv1
    info = info_ref[...]
    masks = mask_rows(sz, info)
    count = info[7:8]
    mean_c, slope_c, bias_c = spread_rows([mean1, inv1 * par_ref[2:3], par_ref[3:4]])
    pool = 0.0
    squares = 0.0
    fields = []
    for t in range(sz.rows):
        centred = deep_ref[t] - mean_c
        pre = centred * slope_c + bias_c
        gate = sigmoid(pre)
        held = pre * gate
        dc_ref[t] = centred
        s1_ref[t] = (gate + held * (1.0 - gate)) * masks[t]
        act = held * masks[t]
        act1_ref[t] = act
        pool = pool + act
        squares = squares + act * act
        fields.append(centred * masks[t])
    pooled = seg_sums(sz, pool) / info[8:16, 0:1]
    rw = par_ref[8:16]
    sw = par_ref[16:24]
    squeeze_pre = dot(pooled, rw, 1, 1, True) + par_ref[7:8, 0:8]
    squeezed = squeeze_pre * sigmoid(squeeze_pre)
    gate = sigmoid(dot(squeezed, sw, 1, 0, True) + par_ref[4:5])
    seg_ref[0] = pooled
    seg_ref[1] = gate
    seg_ref[2, :, 0:8] = squeeze_pre
    gate_wide = seg_spread(sz, gate)
    gate_ref[...] = gate_wide
    sums = 0.0
    sum_g = 0.0
    gated = 0.0
    for t in range(sz.rows):
        act = (act1_ref[t] * gate_wide).astype(BF16)
        cells = dot(pw_ref[...], act, 1, 0)
        proj_ref[t] = cells
        sums = sums + cells * masks[t]
        sum_g = sum_g + xc_ref[t].astype(F32)[chans:] * masks[t]
        act = act.astype(F32)
        gated = gated + act * act
    sq_ref[0:8] = jnp.sum(squares.reshape(sz.wide // 8, 8, LANES), axis=0)
    sq_ref[8:16] = jnp.sum(gated.reshape(sz.wide // 8, 8, LANES), axis=0)
    mean_own = lane_sum(sums) / jnp.maximum(count[:, 0:1], 1.0)
    square = 0.0
    sum_gp = 0.0
    for t in range(sz.rows):
        centred = (proj_ref[t] - mean_own) * masks[t]
        square = square + centred * centred
        sum_gp = sum_gp + centred * xc_ref[t].astype(F32)[chans:]
    row = row_sums(jnp.concatenate([sums, square, sum_g, sum_gp], axis=0))
    row = jnp.concatenate([row, count[:, 4 * chans :]], axis=1)
    each = near_ref.shape[0] // sz.devices
    out_pay[pl.ds(0, sz.devices, stride=2), :] = jnp.broadcast_to(row, (sz.devices, LANES))
    out_pay[pl.ds(1, sz.devices, stride=2), :] = near_ref[...]
    field_shifts(sz, fields, sh_ref, unit_ref, False)
    for e in range(0, sz.wide, 8):
        part = slice(e, e + 8)
        acts = [half_of(act0_ref, t, e) for t in range(sz.rows)]
        back = backward_parts(sz, sh_ref, tap_ref, part, acts, acc_ref)
        for t in range(sz.rows):
            mat_ref[t, part] = back[t] * s0_ref[t, part]
    buf = part_ref[...] + placed_sums(acc_ref, 9, 3 * chans + 18)
    for t in range(sz.rows):
        cells = placed_cells(xc_ref[t].astype(F32)[:chans], chans)
        buf = buf + dot(doubled(mat_ref[t]), jnp.concatenate([cells, cells], axis=1), 1, 1)
    buf_ref[...] = buf


def stage_three_kernel(
    sz,
    pay_ref,
    proj_ref,
    xc_ref,
    act0_ref,
    act1_ref,
    s0_ref,
    dc_ref,
    s1_ref,
    gate_ref,
    seg_ref,
    par_ref,
    tap_ref,
    unit_ref,
    info_ref,
    pwt_ref,
    part_ref,
    sq_ref,
    row_ref,
    out_pay,
    res_ref,
    scaled_ref,
    bg2_ref,
    gg2_ref,
    ga_ref,
    mat_ref,
    acc_ref,
    sh_ref,
    buf_ref,
):
    chans = sz.chans
    half = sz.wide - LANES
    info = info_ref[...]
    masks = mask_rows(sz, info)
    parts = every(sz, pay_ref, 0, 2)
    near = every(sz, pay_ref, 1, 2)
    sums = jnp.sum(parts, axis=0, keepdims=True)
    counts = pltpu.roll(parts, LANES - 4 * chans, 1)
    grads = pltpu.roll(parts, LANES - 2 * chans, 1)
    total = sums[:, 4 * chans : 4 * chans + 1]
    mean_row = sums / total
    offset = parts - counts * mean_row
    scaled = offset / jnp.maximum(counts, 1.0)
    spare = jnp.sum(offset * scaled, axis=0, keepdims=True)
    cross = jnp.sum(scaled * grads, axis=0, keepdims=True)
    square = sums[:, chans : 2 * chans] + spare[:, :chans]
    inv2 = lax.rsqrt(square / total + EPSILON)
    bias_grad = sums[:, 2 * chans : 3 * chans]
    gain_grad = inv2 * (sums[:, 3 * chans : 4 * chans] + cross[:, :chans])
    bg2_ref[...] = bias_grad.reshape(chans)
    gg2_ref[...] = gain_grad.reshape(chans)
    rows = [mean_row[:, :chans], inv2, bias_grad / total, gain_grad / total]
    rows += [par_ref[5:6, :chans], par_ref[6:7, :chans]]
    columns = columns_of(rows)
    mean_c, inv_c, bg_c, gg_c, gain_c, bias_c = (
        spread(columns[:, at : at + 1]) for at in range(6)
    )
    scale = inv_c * gain_c
    gate_wide = gate_ref[...]
    branch_sq = 0.0
    result_sq = 0.0
    gate_sum = 0.0
    buf = part_ref[...]
    for t in range(sz.rows):
        both = xc_ref[t].astype(F32)
        normed = (proj_ref[t] - mean_c) * inv_c
        branch = (normed * gain_c + bias_c) * masks[t]
        result = both[:chans] + branch
        res_ref[t] = result
        branch_sq = branch_sq + branch * branch
        result_sq = result_sq + result * result * masks[t]
        grad = scale * (both[chans:] - (bg_c + normed * gg_c)) * masks[t]
        wide_grad = dot(pwt_ref[...], grad.astype(BF16), 1, 0)
        ga_ref[t] = wide_grad
        act = act1_ref[t]
        gate_sum = gate_sum + wide_grad * act
        act = (act * gate_wide).astype(BF16)
        buf = buf + dot(act, placed_cells(grad, 2 * chans), 1, 1)
    rw = par_ref[8:16]
    sw = par_ref[16:24]
    pooled = seg_ref[0]
    gate = seg_ref[1]
    squeeze_pre = seg_ref[2, :, 0:8]
    slope = sigmoid(squeeze_pre)
    squeezed = squeeze_pre * slope
    slope = slope + squeezed * (1.0 - slope)
    live = (iota((8, 1), 0) < sz.own).astype(F32)
    gate_pre = seg_sums(sz, gate_sum) * gate * (1.0 - gate)
    squeeze_grad = dot(gate_pre, sw, 1, 1, True) * slope * live
    back = dot(squeeze_grad, rw, 1, 0, True) / info[8:16, 0:1]
    back_wide = seg_spread(sz, back)
    (scale_c,) = spread_rows([row_ref[1:2] * par_ref[2:3]])
    sum_b = 0.0
    sum_g = 0.0
    fields = []
    for t in range(sz.rows):
        grad = (ga_ref[t] * gate_wide + back_wide) * s1_ref[t]
        scaled_ref[t] = grad * scale_c
        sum_b = sum_b + grad
        sum_g = sum_g + grad * dc_ref[t]
        fields.append(grad)
    sum_b = row_sums(sum_b)
    sum_g = row_sums(sum_g) * row_ref[1:2]
    field_shifts(sz, fields, sh_ref, unit_ref, False)
    for e in range(0, sz.wide, 8):
        part = slice(e, e + 8)
        acts = [half_of(act0_ref, t, e) for t in range(sz.rows)]
        back = backward_parts(sz, sh_ref, tap_ref, part, acts, acc_ref)
        for t in range(sz.rows):
            mat_ref[t, part] = back[t] * s0_ref[t, part]
    buf = buf + placed_sums(acc_ref, 9, 3 * chans)
    for t in range(sz.rows):
        cells = placed_cells(xc_ref[t].astype(F32)[:chans], 0)
        buf = buf + dot(doubled(mat_ref[t]), jnp.concatenate([cells, cells], axis=1), 1, 1)
    at = 3 * chans + 27
    small = [dot(squeezed, gate_pre, 0, 0, True)[: sz.squeeze]]
    small.append(dot(squeeze_grad, pooled, 0, 0, True)[: sz.squeeze])
    small.append(jnp.sum(gate_pre, axis=0, keepdims=True))
    shape = (16, LANES)
    unit = jnp.where(iota(shape, 0) + at == iota(shape, 1), 1.0, 0.0).astype(BF16)
    buf_ref[...] = buf + spread_by(padded_rows(small, 16), unit)
    at = at + 2 * sz.squeeze + 1
    spots = iota((8, 1), 0)
    held = jnp.sum(squeeze_grad, axis=0, keepdims=True)
    column = jnp.zeros((8, 1), F32)
    for k in range(sz.squeeze):
        column = jnp.where(spots == k, held[:, k : k + 1], column)
    buf_ref[0:8, at : at + 1] = column
    column = jnp.zeros((8, 1), F32)
    squares = [
        jnp.sum(result_sq.reshape(chans // 8, 8, LANES), axis=0),
        sq_ref[0:8],
        sq_ref[8:16],
        jnp.sum(branch_sq.reshape(chans // 8, 8, LANES), axis=0),
    ]
    for k, square in enumerate(squares):
        value = jnp.sum(lane_sum(square), axis=0, keepdims=True)
        column = jnp.where(spots == k, value, column)
    buf_ref[8:16, at : at + 1] = column
    used = at + 1
    piece = LANES - used
    for k in range(-(-used // piece)):
        take = min(piece, used - k * piece)
        buf_ref[k * half : (k + 1) * half, used : used + take] = buf_ref[
            LANES : LANES + half, k * piece : k * piece + take
        ]
    each = LANES // sz.devices
    last = jnp.sum(near, axis=0, keepdims=True)
    block = wide_rows(sum_b, sum_g, half, last)
    send_block(out_pay, jnp.concatenate([block, jnp.zeros((4, LANES), F32)], axis=0))
    for k in range(each):
        held = buf_ref[pl.ds(k, sz.devices, stride=each), :]
        out_pay[pl.ds(4 + k, sz.devices, stride=8), :] = held


def stage_four_kernel(
    sz, pay_ref, scaled_ref, dc_ref, ec_ref, s0_ref, row0_ref, row1_ref, par_ref, *refs
):
    tap_ref, unit_ref, info_ref, out_pay, gp0_ref, bg1_ref, gg1_ref, mid_ref, sh_ref = refs
    half = sz.wide - LANES
    masks = mask_rows(sz, info_ref[...])
    block = jnp.sum(pay_ref[...].reshape(sz.devices, 8, LANES), axis=0)
    bias_grad, gain_grad = wide_pair(block, half)
    bg1_ref[...] = bias_grad.reshape(sz.wide)
    gg1_ref[...] = gain_grad.reshape(sz.wide)
    mid_ref[0:1] = bias_grad
    mid_ref[1:2] = gain_grad
    inv1 = row1_ref[1:2]
    scale = inv1 * par_ref[2:3] / row0_ref[2:3]
    bg_c, gg_c = spread_rows([bias_grad * scale, gain_grad * inv1 * scale])
    fields = []
    for t in range(sz.rows):
        grad = scaled_ref[t] - masks[t] * (bg_c + dc_ref[t] * gg_c)
        fields.append(grad.astype(BF16).astype(F32))
    field_shifts(sz, fields, sh_ref, unit_ref, True)
    total_b = []
    total_g = []
    for e in range(0, sz.wide, 8):
        part = slice(e, e + 8)
        back = backward_parts(sz, sh_ref, tap_ref, part, None, None)
        sum_b = 0.0
        sum_g = 0.0
        for t in range(sz.rows):
            grad = back[t] * s0_ref[t, part]
            gp0_ref[t, part] = grad
            sum_b = sum_b + grad
            sum_g = sum_g + grad * ec_ref[t, part]
        total_b.append(sum_b)
        total_g.append(sum_g)
    sum_b = row_sums(jnp.concatenate(total_b, axis=0))
    sum_g = row_sums(jnp.concatenate(total_g, axis=0)) * row0_ref[1:2]
    top = wide_rows(sum_b, sum_g, half, jnp.zeros((1, LANES), F32))
    send_block(out_pay, jnp.concatenate([top, block[4:8]], axis=0))


def back_kernel(sz, gp0_ref, res_ref, row0_ref, par_ref, w_ref, *refs):
    out_refs, all_ref = refs[:-1], refs[-1]
    chans = sz.chans
    (scale,) = spread_rows([row0_ref[1:2] * par_ref[0:1]])
    weights = w_ref[...]
    for g in range(sz.rows // 2):
        pieces = []
        for par in range(2):
            t = 2 * g + par
            pieces += [res_ref[t], dot(weights, (gp0_ref[t] * scale).astype(BF16), 1, 0)]
        pieces.append(jnp.zeros((LANES - 4 * chans, LANES), F32))
        turned = jnp.concatenate(pieces, axis=0).T.astype(BF16)
        all_ref[:, :, g] = turned.reshape(sz.tiles, sz.own, sz.width, LANES)
    for step, out_ref in enumerate(out_refs):
        out_ref[...] = all_ref[partner(step)]


def far_parts(sz, pay_ref, row0_ref, weights, buf_ref, near_ref):
    chans = sz.chans
    near_ref[...] = every(sz, pay_ref, 3, 8)[0:32]
    buf_ref[...] = jnp.zeros(buf_ref.shape, F32)
    for k in range(5):
        rows = min(32, sz.wide - 32 * k)
        buf_ref[32 * k : 32 * k + rows, 0:chans] = near_ref[0:rows, chans * k : chans * (k + 1)]
    two = picked_rows(buf_ref[...], chans)
    x_row = [near_ref[chans + k : chans + k + 1, 5 * chans : LANES] for k in range(3)]
    x_row = jnp.concatenate(x_row, axis=1)
    x_column = columns_of([x_row])[:, 0:1]
    right = near_ref[0:chans, 5 * chans : LANES]
    below = jnp.concatenate([right.T[0:8, 0:16], right[16:chans]], axis=1)
    second = jnp.concatenate([near_ref[16:32, 4 * chans : 5 * chans], below], axis=0)
    second = second - x_column * x_row / row0_ref[2:3, :chans]
    wide = dot(second, weights, 1, 0, True) * row0_ref[1:2]
    spot = chans + 3
    return two, wide, x_column, near_ref[spot : spot + 1, 5 * chans : 5 * chans + 1]


def picked_rows(columns, count):
    unit = eye(max(count, 16), LANES, BF16)
    return dot(jnp.concatenate([unit] * 3, axis=1), tripled(columns), 1, 1)[0:count]


def last_kernel(
    sz,
    pay_ref,
    far_pay,
    x_ref,
    c_ref,
    far_info,
    row0_ref,
    row1_ref,
    mid_ref,
    par_ref,
    w_ref,
    *refs,
):
    got_refs = refs[: sz.tiles]
    out_ref, xg_ref, ew_ref, gg0_ref, bg0_ref, dw_ref, rw_ref, rb_ref = refs[
        sz.tiles : sz.tiles + 8
    ]
    sw_ref, sb_ref, pw_ref, rms_ref, buf_ref, near_ref, corr_ref = refs[sz.tiles + 8 :]
    chans = sz.chans
    half = sz.wide - LANES
    each = LANES // sz.devices
    block = [jnp.sum(every(sz, pay_ref, at, 8), axis=0, keepdims=True) for at in range(3)]
    bias_grad, gain_grad = wide_pair(jnp.concatenate(block, axis=0), half)
    bg0_ref[...] = bias_grad.reshape(sz.wide)
    gg0_ref[...] = gain_grad.reshape(sz.wide)
    mean0 = row0_ref[0:1]
    inv0 = row0_ref[1:2]
    total = row0_ref[2:3]
    scale0 = inv0 * par_ref[0:1]
    bias_row = bias_grad / total
    gain_row = gain_grad / total
    weights = w_ref[...].astype(F32)
    factor = scale0 * gain_row * inv0
    matrix = dot(weights * factor, weights, 1, 1, True)
    offset = jnp.broadcast_to(scale0 * bias_row - factor * mean0, (8, sz.wide))
    offset = dot(offset, weights, 1, 1, True)[0:1]
    high = matrix.astype(BF16)
    low = (matrix - high.astype(F32)).astype(BF16)
    shape = (16, sz.rows * LANES)
    unit = jnp.where(iota(shape, 0) == lax.div(iota(shape, 1), LANES), 1.0, 0.0).astype(BF16)
    live = dot(far_info[...].astype(BF16), unit, 0, 0)
    for t in range(sz.rows):
        cells = x_ref[:, t].reshape(sz.segs * sz.width, chans)
        back = dot(cells, high, 1, 0) + dot(cells, low, 1, 0) + offset
        corr_ref[t] = back * live[:, t * LANES : t * LANES + chans]
    shape = (LANES, 4 * LANES)
    column = iota(shape, 1)
    spot = lax.rem(column, LANES)
    source = spot + chans * lax.div(column, LANES)
    unit = jnp.where((iota(shape, 0) == source) & (spot < chans), 1.0, 0.0).astype(BF16)
    size = sz.own * sz.width
    shape = (sz.own, sz.width, chans)
    for step, ref in enumerate(got_refs):
        first = partner(step) * sz.own
        for g in range(sz.rows // 2):
            cells = dot(ref[:, g].reshape(size, LANES), unit, 1, 0)
            for par in range(2):
                t = 2 * g + par
                at = 2 * par * LANES
                held = cells[:, at : at + chans]
                out_ref[pl.ds(first, sz.own), t] = held.astype(BF16).reshape(shape)
                at = at + LANES
                held = cells[:, at : at + chans] - corr_ref[t, pl.ds(first * sz.width, size)]
                held = held.reshape(shape) + c_ref[pl.ds(first, sz.own), t].astype(F32)
                xg_ref[pl.ds(first, sz.own), t] = held.astype(BF16)
    two, wide, x_sum, act0_sq = far_parts(sz, far_pay, row0_ref, weights, buf_ref, near_ref)
    used = 3 * chans + 29 + 2 * sz.squeeze
    piece = LANES - used
    for k in range(each):
        buf_ref[pl.ds(k, sz.devices, stride=each), :] = every(sz, pay_ref, 4 + k, 8)
    buf_ref[LANES:] = jnp.zeros((half, LANES), F32)
    for k in range(-(-used // piece)):
        take = min(piece, used - k * piece)
        buf_ref[LANES : LANES + half, k * piece : k * piece + take] = buf_ref[
            k * half : (k + 1) * half, used : used + take
        ]
    rows = picked_rows(buf_ref[...], LANES)
    inv1 = row1_ref[1:2]
    scale1 = inv1 * par_ref[2:3]
    bias1 = mid_ref[0:1] / total
    gain1 = mid_ref[1:2] * inv1 / total
    inner = rows[0:chans] - two * bias1 - rows[chans : 2 * chans] * gain1
    ew_ref[...] = scale0 * (scale1 * inner - x_sum * bias_row - wide * gain_row)
    pw_ref[...] = rows[2 * chans : 3 * chans]
    spot = 3 * chans
    held = rows[spot : spot + 9] - rows[spot + 9 : spot + 18] * bias1
    held = scale1 * (held - rows[spot + 18 : spot + 27] * gain1)
    for i in range(3):
        dw_ref[i] = held[3 * i : 3 * i + 3]
    spot = spot + 27
    sw_ref[...] = rows[spot : spot + sz.squeeze]
    spot = spot + sz.squeeze
    rw_ref[...] = rows[spot : spot + sz.squeeze]
    spot = spot + sz.squeeze
    sb_ref[...] = rows[spot : spot + 1].reshape(sz.wide)
    misc = rows[spot + 1 : spot + 2]
    rb_ref[...] = misc[:, : sz.squeeze].reshape(sz.squeeze)
    squares = jnp.concatenate(
        [misc[:, 8:9], act0_sq, misc[:, 9:10], misc[:, 10:11], misc[:, 11:12]], axis=1
    )
    chan_row = jnp.where(
        (iota((1, 5), 1) == 0) | (iota((1, 5), 1) == 4), float(chans), float(sz.wide)
    )
    rms_ref[...] = jnp.sqrt(squares / (total[:, :5] * chan_row)).reshape(5)


def call(kernel, sz, args, kinds, outs, scratch=(), cost=1.0, room=16):
    spaces = {"v": VMEM, "s": SMEM, "h": HBM, "a": pl.BlockSpec(memory_space=pl.ANY)}
    kinds = kinds + "v" * (len(args) - len(kinds))
    return pl.pallas_call(
        functools.partial(kernel, sz),
        out_shape=tuple(jax.ShapeDtypeStruct(shape, kind) for shape, kind in outs),
        in_specs=[spaces[kind] for kind in kinds],
        out_specs=tuple(VMEM for _ in outs),
        scratch_shapes=[pltpu.VMEM(*held) if isinstance(held, tuple) else held for held in scratch],
        compiler_params=pltpu.CompilerParams(vmem_limit_bytes=room * 1024 * 1024),
        cost_estimate=pl.CostEstimate(
            flops=int(cost * 1e9), bytes_accessed=int(cost * 3e6), transcendentals=0
        ),
        name=kernel.__name__,
    )(*args)


def everywhere(values):
    return lax.all_to_all(values, BOTH, 0, 0, tiled=True)


def passed(sz, parts):
    result = list(parts)
    for step in list(range(2, sz.tiles)) + [1]:
        pairs = [(i, i ^ step) for i in range(sz.tiles)]
        result[step] = lax.ppermute(parts[step], "tile", pairs)
    return result


def shards(
    x_input,
    expand_w,
    gain0,
    bias0,
    dw_kernel,
    gain1,
    bias1,
    reduce_w,
    reduce_b,
    restore_w,
    restore_b,
    project_w,
    gain2,
    bias2,
    cotangent,
    seg_count,
    seg_len,
):
    segs, rows, width, chans = x_input.shape
    wide, squeeze = reduce_w.shape
    tiles = lax.axis_size("tile")
    devices = lax.axis_size("seg") * tiles
    own = segs // tiles
    sz = Sizes(devices, tiles, segs, own, rows, width, chans, wide, squeeze)
    big = ((rows, wide, LANES), F32)
    small = ((rows, chans, LANES), F32)
    block = ((own, rows // 2, width, LANES), BF16)
    packed = ((rows, wide, LANES), BF16)
    both = ((rows, 2 * chans, LANES), BF16)
    column = ((wide, LANES), F32)
    taps = ((9, wide, LANES), F32)
    shifts = ((3, rows + 2, wide, LANES), F32)

    def pay_of(count):
        return ((devices * count, LANES), F32)

    (pay,) = call(
        entry_kernel,
        sz,
        [x_input, expand_w, seg_len, seg_count],
        "hhhh",
        [pay_of(4)],
        [
            (x_input.shape, BF16),
            (expand_w.shape, BF16),
            pltpu.SMEM(seg_len.shape, jnp.int32),
            pltpu.SMEM(seg_count.shape, jnp.int32),
            pltpu.SemaphoreType.DMA((3 + segs,)),
        ],
        room=60,
    )
    parts = call(send_kernel, sz, [x_input, cotangent, pay], "vva", [block] * tiles)
    par, tap, unit, info, pw_near, pw_turned, w_near, w_turned, far_info = call(
        setup_kernel,
        sz,
        [gain0, bias0, gain1, bias1, restore_b, gain2, bias2, reduce_b, dw_kernel, reduce_w.T]
        + [restore_w, project_w.T, expand_w, seg_len, seg_count],
        "v" * 13 + "ss",
        [
            ((24, wide), F32),
            taps,
            ((2 * LANES, 4 * LANES), BF16),
            ((16, LANES), F32),
            ((chans, wide), BF16),
            ((wide, chans), BF16),
            ((chans, wide), BF16),
            ((wide, chans), BF16),
            ((16, LANES), F32),
        ],
    )
    pay = everywhere(pay)
    parts = passed(sz, parts)
    pay, x_c, act0, deep, ec, s0, row0, near, part = call(
        stage_one_kernel,
        sz,
        [pay] + parts + [w_turned, par, tap, unit, info],
        "",
        [pay_of(4), both, packed, big, big, big, ((3, wide), F32)]
        + [((max(32, devices), LANES), F32), column],
        [big, taps, shifts, column, ((tiles,) + block[0], BF16)],
    )
    pay = everywhere(pay)
    pay, act1, dc, s1, proj, gate, seg_rows, row1, part, squares = call(
        stage_two_kernel,
        sz,
        [pay, deep, x_c, par, tap, unit, info, pw_near, near, act0, s0, part],
        "",
        [pay_of(2), big, big, big, small, column, ((3, 8, wide), F32), ((2, wide), F32)]
        + [column, ((16, LANES), F32)],
        [big, taps, shifts],
    )
    pay = everywhere(pay)
    pay, res, scaled, bg2, gg2 = call(
        stage_three_kernel,
        sz,
        [pay, proj, x_c, act0, act1, s0, dc, s1, gate, seg_rows, par, tap, unit, info]
        + [pw_turned, part, squares, row1],
        "",
        [pay_of(8), small, big, ((chans,), F32), ((chans,), F32)],
        [big, big, taps, shifts, column],
    )
    far_pay = everywhere(pay)
    pay, gp0, bg1, gg1, mid = call(
        stage_four_kernel,
        sz,
        [far_pay, scaled, dc, ec, s0, row0, row1, par, tap, unit, info],
        "",
        [pay_of(8), big, ((wide,), F32), ((wide,), F32), ((2, wide), F32)],
        [shifts],
    )
    sent = call(
        back_kernel,
        sz,
        [gp0, res, row0, par, w_near],
        "",
        [block] * tiles,
        [((tiles,) + block[0], BF16)],
    )
    pay = everywhere(pay)
    sent = passed(sz, sent)
    block_out, x_grad, ew, gg0, bg0, dw, rw, rb, sw, sb, pw, rms = call(
        last_kernel,
        sz,
        [pay, far_pay, x_input, cotangent, far_info, row0, row1, mid, par, w_near] + sent,
        "",
        [
            (x_input.shape, BF16),
            (x_input.shape, BF16),
            ((chans, wide), F32),
            ((wide,), F32),
            ((wide,), F32),
            (dw_kernel.shape, F32),
            ((squeeze, wide), F32),
            ((squeeze,), F32),
            ((squeeze, wide), F32),
            ((wide,), F32),
            ((chans, wide), F32),
            ((5,), F32),
        ],
        [column, ((32, LANES), F32), ((rows, LANES, chans), F32)],
    )
    return (
        block_out,
        x_grad,
        ew,
        gg0,
        bg0,
        dw,
        gg1,
        bg1,
        rw.T,
        rb,
        sw,
        sb,
        pw.T,
        gg2,
        bg2,
        rms,
    )


def solution(mesh):
    split = P("seg", "tile", None, None)
    return jax.shard_map(
        shards,
        mesh=mesh,
        in_specs=(split,) + (P(),) * 13 + (split, P("seg"), P("seg")),
        out_specs=(split, split) + (P(),) * 14,
        check_vma=False,
    )
```

```python
import functools
from typing import NamedTuple

import jax
import jax.numpy as jnp
from jax import lax
from jax.experimental import pallas as pl
from jax.experimental.pallas import tpu as pltpu
from jax.sharding import PartitionSpec as P

EPSILON = 0.001
BOTH = ("seg", "tile")
LANES = 128
F32 = jnp.float32
BF16 = jnp.bfloat16
VMEM = pl.BlockSpec(memory_space=pltpu.VMEM)
SMEM = pl.BlockSpec(memory_space=pltpu.SMEM)
HBM = pl.BlockSpec(memory_space=pltpu.HBM)


class Sizes(NamedTuple):
    devices: int
    tiles: int
    segs: int
    own: int
    rows: int
    width: int
    chans: int
    wide: int
    squeeze: int


def iota(shape, dim):
    return lax.broadcasted_iota(jnp.int32, shape, dim)


def dot(left, right, left_dim, right_dim, precise=False):
    return lax.dot_general(
        left,
        right,
        (((left_dim,), (right_dim,)), ((), ())),
        precision=lax.Precision.HIGHEST if precise else None,
        preferred_element_type=F32,
    )


def fine_dot(left, right):
    high = left.astype(BF16).astype(F32)
    left = jnp.concatenate([high, left - high, high], axis=0).astype(BF16)
    high = right.astype(BF16).astype(F32)
    right = jnp.concatenate([high, high, right - high], axis=0).astype(BF16)
    held = dot(left, right, 1, 1)
    return held[0:8, 0:8] + held[8:16, 8:16] + held[16:24, 16:24]


def eye(rows, cols, dtype=F32):
    return (iota((rows, cols), 0) == iota((rows, cols), 1)).astype(dtype)


def spread(column):
    return jnp.broadcast_to(column, (column.shape[0], LANES))


def lane_sum(values):
    return jnp.sum(values, axis=1, keepdims=True)


def sigmoid(values):
    return 0.5 * jnp.tanh(0.5 * values) + 0.5


def vector(ref):
    return ref[...].astype(F32).reshape(1, ref.shape[0])


def thirds(values):
    high = values.astype(BF16)
    rest = values - high.astype(F32)
    middle = rest.astype(BF16)
    return [high, middle, (rest - middle.astype(F32)).astype(BF16)]


def doubled(values):
    high = values.astype(BF16)
    return jnp.concatenate([high, (values - high.astype(F32)).astype(BF16)], axis=1)


def tripled(values):
    return jnp.concatenate(thirds(values), axis=1)


def row_sums(values):
    return dot(jnp.ones((8, 3 * LANES), BF16), tripled(values), 1, 1)[0:1]


def padded_rows(rows, count):
    spare = count - sum(row.shape[0] for row in rows)
    if spare:
        rows = rows + [jnp.zeros((spare, rows[0].shape[1]), F32)]
    return jnp.concatenate(rows, axis=0)


def spread_by(rows, unit):
    held = jnp.concatenate(thirds(rows), axis=0)
    return dot(held, jnp.concatenate([unit] * 3, axis=0), 0, 0)


def spread_rows(rows):
    count = len(rows)
    shape = (16, count * LANES)
    unit = jnp.where(iota(shape, 0) == lax.div(iota(shape, 1), LANES), 1.0, 0.0).astype(BF16)
    wide = spread_by(padded_rows(rows, 16), unit)
    return [wide[:, at * LANES : (at + 1) * LANES] for at in range(count)]


def columns_of(rows):
    held = padded_rows(rows, 8)
    width = held.shape[1]
    spare = (-width) % LANES
    if spare:
        held = jnp.concatenate([held, jnp.zeros((8, spare), F32)], axis=1)
    return held.T[:width]


def turned(cells):
    rows, width = cells.shape
    spare = (-width) % LANES
    held = jnp.concatenate([cells.astype(F32), jnp.zeros((rows, spare), F32)], axis=1)
    return held.T[:width].astype(cells.dtype)


def placed_sums(acc_ref, count, start):
    lane = iota((2 * LANES, LANES), 1)
    result = 0.0
    for at in range(count):
        unit = jnp.where(lane == start + at, 1.0, 0.0).astype(BF16)
        result = result + dot(doubled(acc_ref[at]), unit, 1, 0)
    return result


def lane_at(sz):
    lane = iota((1, LANES), 1)
    step = sz.width * sz.own
    return lax.rem(lane, sz.width), lax.rem(lax.div(lane, sz.width), sz.own), lax.div(lane, step)


def seg_lanes(sz, rows):
    slot = lax.rem(lax.div(iota((rows, LANES), 1), sz.width), sz.own)
    return jnp.where(slot == iota((rows, LANES), 0), 1.0, 0.0).astype(BF16)


def seg_sums(sz, values):
    lanes = seg_lanes(sz, 16)
    return dot(jnp.concatenate([lanes] * 3, axis=1), tripled(values), 1, 1)[0:8]


def seg_spread(sz, rows):
    return spread_by(padded_rows([rows], 16), seg_lanes(sz, 16))


def mask_rows(sz, info):
    return [info[t : t + 1] for t in range(sz.rows)]


def half_of(ref, t, e):
    first = e - e % 16
    return ref[t, first : first + 16].astype(F32)[e - first : e - first + 8]


def shift_unit(sz):
    source = iota((LANES, 2 * LANES), 0)
    column = iota((LANES, 2 * LANES), 1)
    lane = lax.rem(column, LANES)
    spot = lax.rem(lane, sz.width)
    left = jnp.where((source == lane - 1) & (spot != 0), 1.0, 0.0)
    right = jnp.where((source == lane + 1) & (spot != sz.width - 1), 1.0, 0.0)
    return jnp.where(column < LANES, left, right).astype(BF16)


def block_unit(sz):
    source = iota((LANES, 2 * LANES), 0)
    column = iota((LANES, 2 * LANES), 1)
    lane = lax.rem(column, LANES)
    step = sz.width * sz.own
    before = jnp.where(source == lane - step, 1.0, 0.0)
    after = jnp.where(source == lane + step, 1.0, 0.0)
    return jnp.where(column < LANES, before, after).astype(BF16)


def field_shifts(sz, fields, sh_ref, unit_ref, exact):
    deep = LANES if exact else 2 * LANES

    def parts(values):
        return values.astype(BF16) if exact else doubled(values)

    before = dot(parts(fields[-1]), unit_ref[0:deep, 2 * LANES : 3 * LANES], 1, 0)
    after = dot(parts(fields[0]), unit_ref[0:deep, 3 * LANES :], 1, 0)
    rows = [before] + fields + [after]
    cells = parts(jnp.concatenate(rows, axis=0))
    sides = dot(cells, unit_ref[0:deep, 0 : 2 * LANES], 1, 0)
    for t, row in enumerate(rows):
        part = slice(t * sz.wide, (t + 1) * sz.wide)
        sh_ref[0, t] = sides[part, :LANES]
        sh_ref[1, t] = row
        sh_ref[2, t] = sides[part, LANES:]


def pixel_product(values, pix_ref):
    cells = pix_ref[...].reshape(-1, LANES)
    even = jnp.concatenate(values[0::2], axis=1)
    odd = jnp.concatenate(values[1::2], axis=1)
    if even.dtype == F32:
        cells = jnp.concatenate([cells, cells], axis=0)
        even = doubled(even)
        odd = doubled(odd)
    return dot(even, cells, 1, 0), dot(odd, cells, 1, 0)


def backward_parts(sz, sh_ref, tap_ref, part, acts, acc_ref):
    result = [0.0] * sz.rows
    for j in range(3):
        taps = [tap_ref[3 * i + j, part] for i in range(3)]
        held = [0.0] * 3
        for at in range(sz.rows + 2):
            field = sh_ref[2 - j, at, part]
            for i in range(3):
                t = at - 2 + i
                if 0 <= t < sz.rows:
                    result[t] = result[t] + field * taps[i]
                    if acts is not None:
                        held[i] = held[i] + field * acts[t]
        if acts is not None:
            for i in range(3):
                acc_ref[3 * i + j, part] = held[i]
    return result


def every(sz, ref, first, step):
    return ref[pl.ds(first, sz.devices, stride=step), :]


def wide_rows(first, second, half, last):
    tail = [first[:, LANES:], second[:, LANES:], jnp.zeros((1, LANES - 2 * half), F32)]
    tail = jnp.concatenate(tail, axis=1)
    return jnp.concatenate([first[:, :LANES], second[:, :LANES], tail, last], axis=0)


def wide_pair(block, half):
    first = jnp.concatenate([block[0:1], block[2:3, :half]], axis=1)
    second = jnp.concatenate([block[1:2], block[2:3, half : 2 * half]], axis=1)
    return first, second


def wide_moments(sz, ref, half):
    sums, squares, tails, counts = (every(sz, ref, at, 4) for at in range(4))
    total = jnp.sum(counts, axis=0, keepdims=True)
    inverse = 1.0 / jnp.maximum(counts, 1.0)
    means = []
    spares = []
    for held in (sums, tails):
        mean_val = jnp.sum(held, axis=0, keepdims=True) / total
        offset = held - counts * mean_val
        means.append(mean_val)
        spares.append(jnp.sum(offset * offset * inverse, axis=0, keepdims=True))
    low = jnp.sum(squares, axis=0, keepdims=True) + spares[0]
    high = jnp.sum(tails, axis=0, keepdims=True)[:, half : 2 * half] + spares[1][:, :half]
    square = jnp.concatenate([low, high], axis=1)
    mean_row = jnp.concatenate([means[0], means[1][:, :half]], axis=1)
    total_row = jnp.concatenate([total, total[:, :half]], axis=1)
    return mean_row, lax.rsqrt(square / total_row + EPSILON), total_row


def send_block(ref, block):
    count = block.shape[0]
    if count < 8:
        block = jnp.concatenate([block] * (8 // count), axis=0)
    for at in range(0, ref.shape[0], 8):
        ref[at : at + 8] = block


def partner(step):
    return lax.bitwise_xor(lax.axis_index("tile"), step)


def entry_kernel(sz, x_hbm, w_hbm, len_hbm, count_hbm, pay_ref, info_ref, far_info, *scratch):
    x_ref, w_ref, len_ref, count_ref, sems = scratch
    copies = [
        pltpu.make_async_copy(len_hbm, len_ref, sems.at[0]),
        pltpu.make_async_copy(count_hbm, count_ref, sems.at[1]),
        pltpu.make_async_copy(w_hbm, w_ref, sems.at[2]),
        pltpu.make_async_copy(x_hbm, x_ref, sems.at[3]),
    ]
    for copy in copies:
        copy.start()
    for copy in copies[:2]:
        copy.wait()
    tile_pos = lax.axis_index("tile")
    lane_seg = lax.div(iota((1, LANES), 1), sz.width)
    lengths = []
    far_length = jnp.zeros((1, LANES), jnp.int32)
    count = jnp.zeros((), jnp.int32)
    for s in range(sz.segs):
        held = jnp.where(s < count_ref[0], len_ref[s], 0)
        far_length = jnp.where(lane_seg == s, held, far_length)
        count = count + jnp.clip(held - tile_pos * sz.rows, 0, sz.rows)
    count = jnp.full((1, LANES), (count * sz.width).astype(F32))
    masks = [(tile_pos * sz.rows + t < far_length).astype(F32) for t in range(sz.rows)]
    far_info[...] = jnp.zeros(far_info.shape, F32)
    for t in range(sz.rows):
        far_info[t : t + 1] = masks[t]
    first = tile_pos * sz.own
    _, slot, block = lane_at(sz)
    length = jnp.zeros((1, LANES), jnp.int32)
    own_count = jnp.zeros((), jnp.int32)
    at = iota((8, LANES), 0)
    frames = jnp.ones((8, LANES), F32)
    for s in range(sz.own):
        held = jnp.where(first + s < count_ref[0], len_ref[first + s], 0)
        length = jnp.where(slot == s, held, length)
        own_count = own_count + jnp.minimum(held, sz.rows * sz.tiles)
        frame = jnp.maximum((held * sz.width).astype(F32), 1.0)
        frames = jnp.where(at == s, frame, frames)
    info_ref[...] = jnp.zeros(info_ref.shape, F32)
    for t in range(sz.rows):
        info_ref[t : t + 1] = (block * sz.rows + t < length).astype(F32)
    info_ref[7:8] = jnp.full((1, LANES), (own_count * sz.width).astype(F32))
    info_ref[8:16] = frames
    unit = eye(sz.chans, sz.chans, BF16)
    for copy in copies[2:]:
        copy.wait()
    weights = w_ref[...]
    cells = [dot(unit, x_ref[:, t].reshape(LANES, sz.chans), 1, 1) for t in range(sz.rows)]
    centre = cells[0][:, 0:1]
    cells = jnp.concatenate([(cells[t] - centre) * masks[t] for t in range(sz.rows)], axis=1)
    high = cells.astype(BF16)
    low = (cells - high.astype(F32)).astype(BF16)
    left = jnp.concatenate([high, low, high, low], axis=1)
    right = jnp.concatenate([high, high, low, low], axis=1)
    ones = jnp.ones((sz.chans, left.shape[1]), BF16)
    second = dot(left, right, 1, 1)
    halves = jnp.concatenate([high, low], axis=1)
    ones = ones[:, : halves.shape[1]]
    across = dot(ones, halves, 1, 1)
    down = dot(halves, ones, 1, 1)
    divided = jnp.maximum(count[:, : sz.chans], 1.0)
    spare = second - down * (across / divided)
    wide = sum(dot(held, weights, 1, 0) for held in thirds(spare))
    square = jnp.sum(wide * weights.astype(F32), axis=0, keepdims=True)
    total = down + centre * count[:, : sz.chans]
    wide_sum = jnp.concatenate([total[:, 0:1]] * 8, axis=1)
    wide_sum = dot(wide_sum, weights.astype(F32), 0, 0, True)[0:1]
    send_block(pay_ref, wide_rows(wide_sum, square, sz.wide - LANES, count))


def send_kernel(sz, x_ref, c_ref, after_ref, *out_refs):
    del after_ref
    for step, out_ref in enumerate(out_refs):
        first = partner(step) * sz.own
        out_ref[...] = jnp.zeros(out_ref.shape, BF16)
        for t in range(sz.rows):
            at = (t % 2) * 2 * sz.chans
            out_ref[:, t // 2, :, at : at + sz.chans] = x_ref[pl.ds(first, sz.own), t]
            at = at + sz.chans
            out_ref[:, t // 2, :, at : at + sz.chans] = c_ref[pl.ds(first, sz.own), t]


def setup_kernel(sz, *refs):
    wide_refs, small_refs, dw_ref, rw_ref, sw_ref, pw_in, w_in = (
        refs[0:5],
        refs[5:8],
        *refs[8:13],
    )
    info_in, far_in, par_ref, tap_ref, unit_ref, pw_ref, pwt_ref, w_ref, wt_ref = refs[13:22]
    info_ref, far_info = refs[22:]
    info_ref[...] = info_in[...]
    far_info[...] = far_in[...]
    par_ref[...] = jnp.zeros(par_ref.shape, F32)
    for at, ref in enumerate(wide_refs):
        par_ref[at : at + 1] = vector(ref)
    for at, ref in enumerate(small_refs):
        par_ref[5 + at : 6 + at, 0 : ref.shape[0]] = vector(ref)
    par_ref[8 : 8 + sz.squeeze] = rw_ref[...]
    par_ref[16 : 16 + sz.squeeze] = sw_ref[...]
    pw_ref[...] = pw_in[...]
    pwt_ref[...] = turned(pw_in[...])
    w_ref[...] = w_in[...]
    wt_ref[...] = turned(w_in[...])
    taps = spread_rows([dw_ref[i, j : j + 1].astype(F32) for i in range(3) for j in range(3)])
    for at in range(9):
        tap_ref[at] = taps[at]
    for at, unit in enumerate([shift_unit(sz), block_unit(sz)]):
        part = slice(at * 2 * LANES, (at + 1) * 2 * LANES)
        unit_ref[0:LANES, part] = unit
        unit_ref[LANES:, part] = unit


def moment_kernel(sz, pay_ref, par_ref, row_ref, wide_ref):
    mean0, inv0, total = wide_moments(sz, pay_ref, sz.wide - LANES)
    row_ref[0:1] = mean0
    row_ref[1:2] = inv0
    row_ref[2:3] = total
    for at, held in enumerate(spread_rows([mean0, inv0 * par_ref[0:1], par_ref[1:2]])):
        wide_ref[at] = held


def stage_one_kernel(sz, wide_ref, *refs):
    own_refs = refs[: sz.tiles]
    wt_ref, tap_ref, unit_ref, info_ref = refs[sz.tiles : sz.tiles + 4]
    refs = refs[sz.tiles + 4 :]
    out_pay, xc_ref, pix_ref, act0_ref, deep_ref, ec_ref, s0_ref, near_ref, part_ref = refs[:9]
    mat_ref, acc_ref, sh_ref, buf_ref = refs[9:]
    chans = sz.chans
    half = sz.wide - LANES
    size = sz.own * sz.width
    for step, ref in enumerate(own_refs):
        source = partner(step)
        for g in range(sz.rows // 2):
            pix_ref[g, source] = ref[:, g].reshape(size, LANES)
    unit = eye(LANES, LANES, BF16)
    expanded = []
    for g in range(sz.rows // 2):
        flat = dot(unit, pix_ref[g].reshape(LANES, LANES), 1, 1)
        for par in range(2):
            at = par * 2 * chans
            xc_ref[2 * g + par] = flat[at : at + 2 * chans].astype(BF16)
            cells = flat[at : at + chans].astype(BF16)
            expanded.append(dot(wt_ref[...], cells, 1, 0))
    info = info_ref[...]
    masks = mask_rows(sz, info)
    count = info[7:8]
    mean_c, slope_c, bias_c = (wide_ref[at] for at in range(3))
    acts = []
    squares = 0.0
    for t in range(sz.rows):
        centred = expanded[t] - mean_c
        pre = centred * slope_c + bias_c
        gate = sigmoid(pre)
        held = pre * gate
        ec_ref[t] = centred
        s0_ref[t] = (gate + held * (1.0 - gate)) * masks[t]
        act = (held * masks[t]).astype(BF16)
        act0_ref[t] = act
        act = act.astype(F32)
        squares = squares + act * act
        acts.append(act)
    field_shifts(sz, acts, sh_ref, unit_ref, True)
    step = sz.width * sz.own
    spot, _, block = lane_at(sz)
    full = [jnp.broadcast_to(mask, (8, LANES)) for mask in masks]
    before = jnp.where(block == 0, 0.0, pltpu.roll(full[-1], step, 1))
    after = jnp.where(block == sz.tiles - 1, 0.0, pltpu.roll(full[0], LANES - step, 1))
    full = [before] + full + [after]
    left = jnp.broadcast_to(jnp.where(spot == 0, 0.0, 1.0), (8, LANES))
    right = jnp.broadcast_to(jnp.where(spot == sz.width - 1, 0.0, 1.0), (8, LANES))
    total_sum = []
    for e in range(0, sz.wide, 8):
        part = slice(e, e + 8)
        taps = [tap_ref[at, part] for at in range(9)]
        acts = [half_of(act0_ref, t, e) for t in range(sz.rows)]
        sums = 0.0
        edged = [taps[3 * i] * right + taps[3 * i + 1] + taps[3 * i + 2] * left for i in range(3)]
        deep = [0.0] * sz.rows
        for j in range(3):
            for at in range(sz.rows + 2):
                field = sh_ref[j, at, part]
                for i in range(3):
                    if 0 <= at - i < sz.rows:
                        deep[at - i] = deep[at - i] + field * taps[3 * i + j]
        for t in range(sz.rows):
            back = 0.0
            for i in range(3):
                back = back + full[t + 2 - i] * edged[i]
            deep_ref[t, part] = deep[t]
            sums = sums + deep[t] * masks[t]
            mat_ref[t, part] = back * s0_ref[t, part]
        total_sum.append(sums)
        for i in range(3):
            held = sum(full[t + 2 - i] * acts[t] for t in range(sz.rows))
            acc_ref[3 * i, part] = held * right
            acc_ref[3 * i + 1, part] = held
            acc_ref[3 * i + 2, part] = held * left
    total_sum = jnp.concatenate(total_sum, axis=0)
    mean_own = lane_sum(total_sum) / jnp.maximum(count[:, 0:1], 1.0)
    square = 0.0
    for t in range(sz.rows):
        centred = (deep_ref[t] - mean_own) * masks[t]
        square = square + centred * centred
    send_block(out_pay, wide_rows(row_sums(total_sum), row_sums(square), half, count))
    part_ref[...] = placed_sums(acc_ref, 9, 3 * chans + 9)
    even, odd = pixel_product([mat_ref[t] for t in range(sz.rows)], pix_ref)
    held = even + pltpu.roll(odd, LANES - 2 * chans, 1)
    cells = [xc_ref[t].astype(F32)[:chans] * masks[t] for t in range(sz.rows)]
    x_sum = sum(cells)
    even, odd = pixel_product([cell.astype(BF16) for cell in cells], pix_ref)
    second = even[:, :chans] + odd[:, 2 * chans : 3 * chans]
    near_ref[...] = jnp.zeros(near_ref.shape, F32)
    buf_ref[...] = held
    for k in range(5):
        rows = min(32, sz.wide - 32 * k)
        near_ref[0:rows, chans * k : chans * (k + 1)] = buf_ref[32 * k : 32 * k + rows, 0:chans]
    near_ref[16:32, 4 * chans : 5 * chans] = second[0:16]
    near_ref[0:chans, 5 * chans : LANES] = second[:, 16:]
    x_row = row_sums(x_sum)
    for k in range(3):
        near_ref[chans + k : chans + k + 1, 5 * chans : LANES] = x_row[:, 8 * k : 8 * k + 8]
    squares = jnp.sum(squares.reshape(sz.wide // 8, 8, LANES), axis=0)
    squares = jnp.sum(lane_sum(squares), axis=0, keepdims=True)
    near_ref[chans + 3 : chans + 4, 5 * chans : 5 * chans + 1] = squares


def stage_two_kernel(
    sz,
    pay_ref,
    deep_ref,
    xc_ref,
    pix_ref,
    par_ref,
    tap_ref,
    unit_ref,
    info_ref,
    pw_ref,
    near_ref,
    act0_ref,
    s0_ref,
    part_ref,
    out_pay,
    act1_ref,
    dc_ref,
    s1_ref,
    proj_ref,
    gate_ref,
    seg_ref,
    row_ref,
    buf_ref,
    sq_ref,
    mat_ref,
    acc_ref,
    sh_ref,
):
    chans = sz.chans
    half = sz.wide - LANES
    mean1, inv1, _ = wide_moments(sz, pay_ref, half)
    row_ref[0:1] = mean1
    row_ref[1:2] = inv1
    info = info_ref[...]
    masks = mask_rows(sz, info)
    count = info[7:8]
    mean_c, slope_c, bias_c = spread_rows([mean1, inv1 * par_ref[2:3], par_ref[3:4]])
    pool = 0.0
    squares = 0.0
    fields = []
    for t in range(sz.rows):
        centred = deep_ref[t] - mean_c
        pre = centred * slope_c + bias_c
        gate = sigmoid(pre)
        held = pre * gate
        dc_ref[t] = centred
        s1_ref[t] = (gate + held * (1.0 - gate)) * masks[t]
        act = held * masks[t]
        act1_ref[t] = act
        pool = pool + act
        squares = squares + act * act
        fields.append(centred * masks[t])
    pooled = seg_sums(sz, pool) / info[8:16, 0:1]
    rw = par_ref[8:16]
    sw = par_ref[16:24]
    squeeze_pre = fine_dot(pooled, rw) + par_ref[7:8, 0:8]
    squeezed = squeeze_pre * sigmoid(squeeze_pre)
    gate = sigmoid(dot(squeezed, sw, 1, 0, True) + par_ref[4:5])
    seg_ref[0] = pooled
    seg_ref[1] = gate
    seg_ref[2, :, 0:8] = squeeze_pre
    gate_wide = seg_spread(sz, gate)
    gate_ref[...] = gate_wide
    sums = 0.0
    sum_g = 0.0
    gated = 0.0
    for t in range(sz.rows):
        act = (act1_ref[t] * gate_wide).astype(BF16)
        cells = dot(pw_ref[...], act, 1, 0)
        proj_ref[t] = cells
        sums = sums + cells * masks[t]
        sum_g = sum_g + xc_ref[t].astype(F32)[chans:] * masks[t]
        act = act.astype(F32)
        gated = gated + act * act
    sq_ref[0:8] = jnp.sum(squares.reshape(sz.wide // 8, 8, LANES), axis=0)
    sq_ref[8:16] = jnp.sum(gated.reshape(sz.wide // 8, 8, LANES), axis=0)
    mean_own = lane_sum(sums) / jnp.maximum(count[:, 0:1], 1.0)
    square = 0.0
    sum_gp = 0.0
    for t in range(sz.rows):
        centred = (proj_ref[t] - mean_own) * masks[t]
        square = square + centred * centred
        sum_gp = sum_gp + centred * xc_ref[t].astype(F32)[chans:]
    row = row_sums(jnp.concatenate([sums, square, sum_g, sum_gp], axis=0))
    row = jnp.concatenate([row, count[:, 4 * chans :]], axis=1)
    each = near_ref.shape[0] // sz.devices
    out_pay[pl.ds(0, sz.devices, stride=2), :] = jnp.broadcast_to(row, (sz.devices, LANES))
    out_pay[pl.ds(1, sz.devices, stride=2), :] = near_ref[...]
    field_shifts(sz, fields, sh_ref, unit_ref, False)
    for e in range(0, sz.wide, 8):
        part = slice(e, e + 8)
        acts = [half_of(act0_ref, t, e) for t in range(sz.rows)]
        back = backward_parts(sz, sh_ref, tap_ref, part, acts, acc_ref)
        for t in range(sz.rows):
            mat_ref[t, part] = back[t] * s0_ref[t, part]
    even, odd = pixel_product([mat_ref[t] for t in range(sz.rows)], pix_ref)
    lane = iota((1, LANES), 1)
    held = pltpu.roll(even, 2 * chans, 1) + odd
    held = jnp.where((lane >= 2 * chans) & (lane < 3 * chans), held, 0.0)
    buf_ref[...] = part_ref[...] + placed_sums(acc_ref, 9, 3 * chans + 18) + held


def stage_three_kernel(
    sz,
    pay_ref,
    proj_ref,
    xc_ref,
    pix_ref,
    act0_ref,
    act1_ref,
    s0_ref,
    dc_ref,
    s1_ref,
    gate_ref,
    seg_ref,
    par_ref,
    tap_ref,
    unit_ref,
    info_ref,
    pwt_ref,
    part_ref,
    sq_ref,
    row_ref,
    out_pay,
    res_ref,
    scaled_ref,
    bg2_ref,
    gg2_ref,
    ga_ref,
    mat_ref,
    acc_ref,
    sh_ref,
    buf_ref,
):
    chans = sz.chans
    half = sz.wide - LANES
    info = info_ref[...]
    masks = mask_rows(sz, info)
    parts = every(sz, pay_ref, 0, 2)
    near = every(sz, pay_ref, 1, 2)
    sums = jnp.sum(parts, axis=0, keepdims=True)
    counts = pltpu.roll(parts, LANES - 4 * chans, 1)
    shares = pltpu.roll(parts, LANES - 2 * chans, 1)
    total = sums[:, 4 * chans : 4 * chans + 1]
    mean_row = sums / total
    offset = parts - counts * mean_row
    scaled = offset / jnp.maximum(counts, 1.0)
    spare = jnp.sum(offset * scaled, axis=0, keepdims=True)
    cross = jnp.sum(scaled * shares, axis=0, keepdims=True)
    square = sums[:, chans : 2 * chans] + spare[:, :chans]
    inv2 = lax.rsqrt(square / total + EPSILON)
    bias_grad = sums[:, 2 * chans : 3 * chans]
    gain_grad = inv2 * (sums[:, 3 * chans : 4 * chans] + cross[:, :chans])
    bg2_ref[...] = bias_grad.reshape(chans)
    gg2_ref[...] = gain_grad.reshape(chans)
    rows = [mean_row[:, :chans], inv2, bias_grad / total, gain_grad / total]
    rows += [par_ref[5:6, :chans], par_ref[6:7, :chans]]
    columns = columns_of(rows)
    mean_c, inv_c, bg_c, gg_c, gain_c, bias_c = (
        spread(columns[:, at : at + 1]) for at in range(6)
    )
    scale = inv_c * gain_c
    gate_wide = gate_ref[...]
    branch_sq = 0.0
    result_sq = 0.0
    gate_sum = 0.0
    gated = []
    grads = []
    for t in range(sz.rows):
        both = xc_ref[t].astype(F32)
        normed = (proj_ref[t] - mean_c) * inv_c
        branch = (normed * gain_c + bias_c) * masks[t]
        result = both[:chans] + branch
        res_ref[t] = result
        branch_sq = branch_sq + branch * branch
        result_sq = result_sq + result * result * masks[t]
        grad = scale * (both[chans:] - (bg_c + normed * gg_c)) * masks[t]
        wide_grad = dot(pwt_ref[...], grad.astype(BF16), 1, 0)
        ga_ref[t] = wide_grad
        act = act1_ref[t]
        gate_sum = gate_sum + wide_grad * act
        gated.append((act * gate_wide).astype(BF16))
        grads.append(grad.astype(BF16))
    grads = dot(jnp.concatenate(gated, axis=1), jnp.concatenate(grads, axis=1), 1, 1)
    rw = par_ref[8:16]
    sw = par_ref[16:24]
    pooled = seg_ref[0]
    gate = seg_ref[1]
    squeeze_pre = seg_ref[2, :, 0:8]
    slope = sigmoid(squeeze_pre)
    squeezed = squeeze_pre * slope
    slope = slope + squeezed * (1.0 - slope)
    live = (iota((8, 1), 0) < sz.own).astype(F32)
    gate_pre = seg_sums(sz, gate_sum) * gate * (1.0 - gate)
    squeeze_grad = fine_dot(gate_pre, sw) * slope * live
    back = dot(squeeze_grad, rw, 1, 0, True) / info[8:16, 0:1]
    back_wide = seg_spread(sz, back)
    (scale_c,) = spread_rows([row_ref[1:2] * par_ref[2:3]])
    sum_b = 0.0
    sum_g = 0.0
    fields = []
    for t in range(sz.rows):
        grad = (ga_ref[t] * gate_wide + back_wide) * s1_ref[t]
        scaled_ref[t] = grad * scale_c
        sum_b = sum_b + grad
        sum_g = sum_g + grad * dc_ref[t]
        fields.append(grad)
    sum_b = row_sums(sum_b)
    sum_g = row_sums(sum_g) * row_ref[1:2]
    field_shifts(sz, fields, sh_ref, unit_ref, False)
    for e in range(0, sz.wide, 8):
        part = slice(e, e + 8)
        acts = [half_of(act0_ref, t, e) for t in range(sz.rows)]
        back = backward_parts(sz, sh_ref, tap_ref, part, acts, acc_ref)
        for t in range(sz.rows):
            mat_ref[t, part] = back[t] * s0_ref[t, part]
    even, odd = pixel_product([mat_ref[t] for t in range(sz.rows)], pix_ref)
    held = even + pltpu.roll(odd, LANES - 2 * chans, 1)
    held = jnp.where(iota((1, LANES), 1) < chans, held, 0.0)
    buf = part_ref[...] + placed_sums(acc_ref, 9, 3 * chans) + held
    at = 3 * chans + 27
    small = [dot(squeezed, gate_pre, 0, 0, True)[: sz.squeeze]]
    small.append(dot(squeeze_grad, pooled, 0, 0, True)[: sz.squeeze])
    small.append(jnp.sum(gate_pre, axis=0, keepdims=True))
    shape = (16, LANES)
    unit = jnp.where(iota(shape, 0) + at == iota(shape, 1), 1.0, 0.0).astype(BF16)
    buf_ref[...] = buf + spread_by(padded_rows(small, 16), unit)
    buf_ref[:, chans : 2 * chans] = grads
    at = at + 2 * sz.squeeze + 1
    spots = iota((8, 1), 0)
    held = jnp.sum(squeeze_grad, axis=0, keepdims=True)
    column = jnp.zeros((8, 1), F32)
    for k in range(sz.squeeze):
        column = jnp.where(spots == k, held[:, k : k + 1], column)
    buf_ref[0:8, at : at + 1] = column
    column = jnp.zeros((8, 1), F32)
    squares = [
        jnp.sum(result_sq.reshape(chans // 8, 8, LANES), axis=0),
        sq_ref[0:8],
        sq_ref[8:16],
        jnp.sum(branch_sq.reshape(chans // 8, 8, LANES), axis=0),
    ]
    for k, square in enumerate(squares):
        value = jnp.sum(lane_sum(square), axis=0, keepdims=True)
        column = jnp.where(spots == k, value, column)
    buf_ref[8:16, at : at + 1] = column
    used = at + 1
    piece = LANES - used
    for k in range(-(-used // piece)):
        take = min(piece, used - k * piece)
        buf_ref[k * half : (k + 1) * half, used : used + take] = buf_ref[
            LANES : LANES + half, k * piece : k * piece + take
        ]
    each = LANES // sz.devices
    last = jnp.sum(near, axis=0, keepdims=True)
    block = wide_rows(sum_b, sum_g, half, last)
    send_block(out_pay, jnp.concatenate([block, jnp.zeros((4, LANES), F32)], axis=0))
    for k in range(each):
        held = buf_ref[pl.ds(k, sz.devices, stride=each), :]
        out_pay[pl.ds(4 + k, sz.devices, stride=8), :] = held


def stage_four_kernel(
    sz, pay_ref, scaled_ref, dc_ref, ec_ref, s0_ref, row0_ref, row1_ref, par_ref, *refs
):
    tap_ref, unit_ref, info_ref, out_pay, gp0_ref, bg1_ref, gg1_ref, mid_ref, sh_ref = refs
    half = sz.wide - LANES
    masks = mask_rows(sz, info_ref[...])
    block = jnp.sum(pay_ref[...].reshape(sz.devices, 8, LANES), axis=0)
    bias_grad, gain_grad = wide_pair(block, half)
    bg1_ref[...] = bias_grad.reshape(sz.wide)
    gg1_ref[...] = gain_grad.reshape(sz.wide)
    mid_ref[0:1] = bias_grad
    mid_ref[1:2] = gain_grad
    inv1 = row1_ref[1:2]
    scale = inv1 * par_ref[2:3] / row0_ref[2:3]
    bg_c, gg_c = spread_rows([bias_grad * scale, gain_grad * inv1 * scale])
    fields = []
    for t in range(sz.rows):
        grad = scaled_ref[t] - masks[t] * (bg_c + dc_ref[t] * gg_c)
        fields.append(grad.astype(BF16).astype(F32))
    field_shifts(sz, fields, sh_ref, unit_ref, True)
    total_b = []
    total_g = []
    for e in range(0, sz.wide, 8):
        part = slice(e, e + 8)
        back = backward_parts(sz, sh_ref, tap_ref, part, None, None)
        sum_b = 0.0
        sum_g = 0.0
        for t in range(sz.rows):
            grad = back[t] * s0_ref[t, part]
            gp0_ref[t, part] = grad
            sum_b = sum_b + grad
            sum_g = sum_g + grad * ec_ref[t, part]
        total_b.append(sum_b)
        total_g.append(sum_g)
    sum_b = row_sums(jnp.concatenate(total_b, axis=0))
    sum_g = row_sums(jnp.concatenate(total_g, axis=0)) * row0_ref[1:2]
    top = wide_rows(sum_b, sum_g, half, jnp.zeros((1, LANES), F32))
    send_block(out_pay, jnp.concatenate([top, block[4:8]], axis=0))


def back_kernel(sz, gp0_ref, res_ref, row0_ref, par_ref, w_ref, *refs):
    out_refs, all_ref = refs[:-1], refs[-1]
    chans = sz.chans
    (scale,) = spread_rows([row0_ref[1:2] * par_ref[0:1]])
    weights = w_ref[...]
    for g in range(sz.rows // 2):
        pieces = []
        for par in range(2):
            t = 2 * g + par
            pieces += [res_ref[t], dot(weights, (gp0_ref[t] * scale).astype(BF16), 1, 0)]
        pieces.append(jnp.zeros((LANES - 4 * chans, LANES), F32))
        turned = jnp.concatenate(pieces, axis=0).T.astype(BF16)
        all_ref[:, :, g] = turned.reshape(sz.tiles, sz.own, sz.width, LANES)
    for step, out_ref in enumerate(out_refs):
        out_ref[...] = all_ref[partner(step)]


def far_kernel(sz, pay_ref, x_ref, far_info, row0_ref, w_ref, after_ref, *refs):
    del after_ref
    two_ref, wide_ref, misc_ref, live_ref, buf_ref, near_ref = refs
    chans = sz.chans
    near_ref[...] = every(sz, pay_ref, 3, 8)[0:32]
    buf_ref[...] = jnp.zeros(buf_ref.shape, F32)
    for k in range(5):
        rows = min(32, sz.wide - 32 * k)
        buf_ref[32 * k : 32 * k + rows, 0:chans] = near_ref[0:rows, chans * k : chans * (k + 1)]
    two_ref[...] = picked_rows(buf_ref[...], chans)
    x_row = [near_ref[chans + k : chans + k + 1, 5 * chans : LANES] for k in range(3)]
    x_row = jnp.concatenate(x_row, axis=1)
    x_column = columns_of([x_row])[:, 0:1]
    right = near_ref[0:chans, 5 * chans : LANES]
    below = jnp.concatenate([right.T[0:8, 0:16], right[16:chans]], axis=1)
    second = jnp.concatenate([near_ref[16:32, 4 * chans : 5 * chans], below], axis=0)
    second = second - x_column * x_row / row0_ref[2:3, :chans]
    wide_ref[...] = dot(second, w_ref[...].astype(F32), 1, 0, True) * row0_ref[1:2]
    misc_ref[0:chans] = spread(x_column)
    spot = chans + 3
    misc_ref[chans : chans + 8] = jnp.broadcast_to(
        near_ref[spot : spot + 1, 5 * chans : 5 * chans + 1], (8, LANES)
    )
    shape = (16, sz.rows * LANES)
    unit = jnp.where(iota(shape, 0) == lax.div(iota(shape, 1), LANES), 1.0, 0.0).astype(BF16)
    live = dot(far_info[...].astype(BF16), unit, 0, 0)
    lane = iota((1, 32), 1)
    for t in range(sz.rows):
        held = live[:, t * LANES : t * LANES + 32]
        cells = x_ref[:, t].reshape(sz.segs * sz.width, chans).astype(F32)
        cells = jnp.concatenate([cells, jnp.ones((LANES, 32 - chans), F32)], axis=1)
        live_ref[t] = (jnp.where(lane <= chans, cells, 0.0) * held).astype(BF16)


def picked_rows(columns, count):
    unit = eye(max(count, 16), LANES, BF16)
    return dot(jnp.concatenate([unit] * 3, axis=1), tripled(columns), 1, 1)[0:count]


def weights_kernel(
    sz,
    pay_ref,
    two_ref,
    wide_ref,
    misc_ref,
    live_ref,
    row0_ref,
    row1_ref,
    mid_ref,
    par_ref,
    w_ref,
    *refs,
):
    ew_ref, gg0_ref, bg0_ref, dw_ref, rw_ref, rb_ref, sw_ref, sb_ref, pw_ref, rms_ref = refs[:10]
    corr_ref, buf_ref = refs[10:]
    chans = sz.chans
    half = sz.wide - LANES
    each = LANES // sz.devices
    block = [jnp.sum(every(sz, pay_ref, at, 8), axis=0, keepdims=True) for at in range(3)]
    bias_grad, gain_grad = wide_pair(jnp.concatenate(block, axis=0), half)
    bg0_ref[...] = bias_grad.reshape(sz.wide)
    gg0_ref[...] = gain_grad.reshape(sz.wide)
    mean0 = row0_ref[0:1]
    inv0 = row0_ref[1:2]
    total = row0_ref[2:3]
    scale0 = inv0 * par_ref[0:1]
    bias_row = bias_grad / total
    gain_row = gain_grad / total
    weights = w_ref[...].astype(F32)
    factor = scale0 * gain_row * inv0
    matrix = dot(weights * factor, weights, 1, 1, True)
    offset = jnp.broadcast_to(scale0 * bias_row - factor * mean0, (8, sz.wide))
    offset = dot(offset, weights, 1, 1, True)[0:1]
    matrix = jnp.concatenate([matrix, offset, jnp.zeros((32 - chans - 1, chans), F32)], axis=0)
    high = matrix.astype(BF16)
    low = (matrix - high.astype(F32)).astype(BF16)
    for t in range(sz.rows):
        cells = live_ref[t]
        corr_ref[t] = dot(cells, high, 1, 0) + dot(cells, low, 1, 0)
    used = 3 * chans + 29 + 2 * sz.squeeze
    piece = LANES - used
    for k in range(each):
        buf_ref[pl.ds(k, sz.devices, stride=each), :] = every(sz, pay_ref, 4 + k, 8)
    buf_ref[LANES:] = jnp.zeros((half, LANES), F32)
    for k in range(-(-used // piece)):
        take = min(piece, used - k * piece)
        buf_ref[LANES : LANES + half, k * piece : k * piece + take] = buf_ref[
            k * half : (k + 1) * half, used : used + take
        ]
    rows = picked_rows(buf_ref[...], LANES)
    inv1 = row1_ref[1:2]
    scale1 = inv1 * par_ref[2:3]
    bias1 = mid_ref[0:1] / total
    gain1 = mid_ref[1:2] * inv1 / total
    inner = rows[0:chans] - two_ref[...] * bias1 - rows[2 * chans : 3 * chans] * gain1
    x_sum = misc_ref[0:chans, 0:1]
    ew_ref[...] = scale0 * (scale1 * inner - x_sum * bias_row - wide_ref[...] * gain_row)
    pw_ref[...] = rows[chans : 2 * chans]
    spot = 3 * chans
    held = rows[spot : spot + 9] - rows[spot + 9 : spot + 18] * bias1
    held = scale1 * (held - rows[spot + 18 : spot + 27] * gain1)
    for i in range(3):
        dw_ref[i] = held[3 * i : 3 * i + 3]
    spot = spot + 27
    sw_ref[...] = rows[spot : spot + sz.squeeze]
    spot = spot + sz.squeeze
    rw_ref[...] = rows[spot : spot + sz.squeeze]
    spot = spot + sz.squeeze
    sb_ref[...] = rows[spot : spot + 1].reshape(sz.wide)
    misc = rows[spot + 1 : spot + 2]
    rb_ref[...] = misc[:, : sz.squeeze].reshape(sz.squeeze)
    squares = jnp.concatenate(
        [misc[:, 8:9], misc_ref[chans : chans + 1, 0:1], misc[:, 9:10], misc[:, 10:11], misc[:, 11:12]], axis=1
    )
    chan_row = jnp.where(
        (iota((1, 5), 1) == 0) | (iota((1, 5), 1) == 4), float(chans), float(sz.wide)
    )
    rms_ref[...] = jnp.sqrt(squares / (total[:, :5] * chan_row)).reshape(5)


def return_kernel(sz, c_ref, corr_ref, *refs):
    got_refs = refs[: sz.tiles]
    out_ref, xg_ref = refs[sz.tiles :]
    chans = sz.chans
    shape = (LANES, 4 * LANES)
    column = iota(shape, 1)
    spot = lax.rem(column, LANES)
    source = spot + chans * lax.div(column, LANES)
    unit = jnp.where((iota(shape, 0) == source) & (spot < chans), 1.0, 0.0).astype(BF16)
    size = sz.own * sz.width
    shape = (sz.own, sz.width, chans)
    for step, ref in enumerate(got_refs):
        first = partner(step) * sz.own
        for g in range(sz.rows // 2):
            cells = dot(ref[:, g].reshape(size, LANES), unit, 1, 0)
            for par in range(2):
                t = 2 * g + par
                at = 2 * par * LANES
                held = cells[:, at : at + chans]
                out_ref[pl.ds(first, sz.own), t] = held.astype(BF16).reshape(shape)
                at = at + LANES
                held = cells[:, at : at + chans] - corr_ref[t, pl.ds(first * sz.width, size)]
                held = held.reshape(shape) + c_ref[pl.ds(first, sz.own), t].astype(F32)
                xg_ref[pl.ds(first, sz.own), t] = held.astype(BF16)


def call(kernel, sz, args, kinds, outs, scratch=(), cost=1.0, room=16):
    spaces = {"v": VMEM, "s": SMEM, "h": HBM, "a": pl.BlockSpec(memory_space=pl.ANY)}
    kinds = kinds + "v" * (len(args) - len(kinds))
    return pl.pallas_call(
        functools.partial(kernel, sz),
        out_shape=tuple(jax.ShapeDtypeStruct(shape, kind) for shape, kind in outs),
        in_specs=[spaces[kind] for kind in kinds],
        out_specs=tuple(VMEM for _ in outs),
        scratch_shapes=[pltpu.VMEM(*held) if isinstance(held, tuple) else held for held in scratch],
        compiler_params=pltpu.CompilerParams(vmem_limit_bytes=room * 1024 * 1024),
        cost_estimate=pl.CostEstimate(
            flops=int(cost * 1e9), bytes_accessed=int(cost * 3e6), transcendentals=0
        ),
        name=kernel.__name__,
    )(*args)


def everywhere(values):
    return lax.all_to_all(values, BOTH, 0, 0, tiled=True)


def passed(sz, parts):
    result = list(parts)
    for step in list(range(2, sz.tiles)) + [1]:
        pairs = [(i, i ^ step) for i in range(sz.tiles)]
        result[step] = lax.ppermute(parts[step], "tile", pairs)
    return result


def shards(
    x_input,
    expand_w,
    gain0,
    bias0,
    dw_kernel,
    gain1,
    bias1,
    reduce_w,
    reduce_b,
    restore_w,
    restore_b,
    project_w,
    gain2,
    bias2,
    cotangent,
    seg_count,
    seg_len,
):
    segs, rows, width, chans = x_input.shape
    wide, squeeze = reduce_w.shape
    tiles = lax.axis_size("tile")
    devices = lax.axis_size("seg") * tiles
    own = segs // tiles
    sz = Sizes(devices, tiles, segs, own, rows, width, chans, wide, squeeze)
    big = ((rows, wide, LANES), F32)
    small = ((rows, chans, LANES), F32)
    block = ((own, rows // 2, width, LANES), BF16)
    packed = ((rows, wide, LANES), BF16)
    both = ((rows, 2 * chans, LANES), BF16)
    column = ((wide, LANES), F32)
    taps = ((9, wide, LANES), F32)
    shifts = ((3, rows + 2, wide, LANES), F32)

    def pay_of(count):
        return ((devices * count, LANES), F32)

    pay, info, far_info = call(
        entry_kernel,
        sz,
        [x_input, expand_w, seg_len, seg_count],
        "hhhh",
        [pay_of(4), ((16, LANES), F32), ((16, LANES), F32)],
        [
            (x_input.shape, BF16),
            (expand_w.shape, BF16),
            pltpu.SMEM(seg_len.shape, jnp.int32),
            pltpu.SMEM(seg_count.shape, jnp.int32),
            pltpu.SemaphoreType.DMA((4,)),
        ],
        room=60,
    )
    parts = call(send_kernel, sz, [x_input, cotangent, pay], "vvh", [block] * tiles)
    par, tap, unit, pw_near, pw_turned, w_near, w_turned, info, far_info = call(
        setup_kernel,
        sz,
        [gain0, bias0, gain1, bias1, restore_b, gain2, bias2, reduce_b, dw_kernel, reduce_w.T]
        + [restore_w, project_w.T, expand_w, info, far_info],
        "",
        [
            ((24, wide), F32),
            taps,
            ((2 * LANES, 4 * LANES), BF16),
            ((chans, wide), BF16),
            ((wide, chans), BF16),
            ((chans, wide), BF16),
            ((wide, chans), BF16),
            ((16, LANES), F32),
            ((16, LANES), F32),
        ],
    )
    pay = everywhere(pay)
    parts = passed(sz, parts)
    row0, wide0 = call(
        moment_kernel, sz, [pay, par], "", [((3, wide), F32), ((3, wide, LANES), F32)]
    )
    pay, x_c, pix, act0, deep, ec, s0, near, part = call(
        stage_one_kernel,
        sz,
        [wide0] + parts + [w_turned, tap, unit, info],
        "",
        [pay_of(4), both, ((rows // 2, tiles, own * width, LANES), BF16), packed, big, big, big]
        + [((max(32, devices), LANES), F32), column],
        [big, taps, shifts, column],
    )
    pay = everywhere(pay)
    pay, act1, dc, s1, proj, gate, seg_rows, row1, part, squares = call(
        stage_two_kernel,
        sz,
        [pay, deep, x_c, pix, par, tap, unit, info, pw_near, near, act0, s0, part],
        "",
        [pay_of(2), big, big, big, small, column, ((3, 8, wide), F32), ((2, wide), F32)]
        + [column, ((16, LANES), F32)],
        [big, taps, shifts],
    )
    pay = everywhere(pay)
    pay, res, scaled, bg2, gg2 = call(
        stage_three_kernel,
        sz,
        [pay, proj, x_c, pix, act0, act1, s0, dc, s1, gate, seg_rows, par, tap, unit, info]
        + [pw_turned, part, squares, row1],
        "",
        [pay_of(8), small, big, ((chans,), F32), ((chans,), F32)],
        [big, big, taps, shifts, column],
    )
    far_pay = everywhere(pay)
    pay, gp0, bg1, gg1, mid = call(
        stage_four_kernel,
        sz,
        [far_pay, scaled, dc, ec, s0, row0, row1, par, tap, unit, info],
        "",
        [pay_of(8), big, ((wide,), F32), ((wide,), F32), ((2, wide), F32)],
        [shifts],
    )
    sent = call(
        back_kernel,
        sz,
        [gp0, res, row0, par, w_near],
        "",
        [block] * tiles,
        [((tiles,) + block[0], BF16)],
    )
    pay = everywhere(pay)
    sent = passed(sz, sent)
    far = call(
        far_kernel,
        sz,
        [far_pay, x_input, far_info, row0, w_near, gp0],
        "vvvvva",
        [((chans, wide), F32), ((chans, wide), F32), ((chans + 8, LANES), F32)]
        + [((rows, LANES, 32), BF16)],
        [column, ((32, LANES), F32)],
    )
    ew, gg0, bg0, dw, rw, rb, sw, sb, pw, rms, corr = call(
        weights_kernel,
        sz,
        [pay] + list(far) + [row0, row1, mid, par, w_near],
        "",
        [
            ((chans, wide), F32),
            ((wide,), F32),
            ((wide,), F32),
            (dw_kernel.shape, F32),
            ((squeeze, wide), F32),
            ((squeeze,), F32),
            ((squeeze, wide), F32),
            ((wide,), F32),
            ((chans, wide), F32),
            ((5,), F32),
            ((rows, LANES, chans), F32),
        ],
        [column],
    )
    block_out, x_grad = call(
        return_kernel,
        sz,
        [cotangent, corr] + sent,
        "",
        [(x_input.shape, BF16), (x_input.shape, BF16)],
    )
    return (
        block_out,
        x_grad,
        ew,
        gg0,
        bg0,
        dw,
        gg1,
        bg1,
        rw.T,
        rb,
        sw,
        sb,
        pw.T,
        gg2,
        bg2,
        rms,
    )


def solution(mesh):
    split = P("seg", "tile", None, None)
    return jax.shard_map(
        shards,
        mesh=mesh,
        in_specs=(split,) + (P(),) * 13 + (split, P("seg"), P("seg")),
        out_specs=(split, split) + (P(),) * 14,
        check_vma=False,
    )
```

```python
import functools
from typing import NamedTuple

import jax
import jax.numpy as jnp
from jax import lax
from jax.experimental import pallas as pl
from jax.experimental.pallas import tpu as pltpu
from jax.sharding import PartitionSpec as P

EPSILON = 0.001
BOTH = ("seg", "tile")
LANES = 128
F32 = jnp.float32
BF16 = jnp.bfloat16
VMEM = pl.BlockSpec(memory_space=pltpu.VMEM)
SMEM = pl.BlockSpec(memory_space=pltpu.SMEM)
HBM = pl.BlockSpec(memory_space=pltpu.HBM)


class Sizes(NamedTuple):
    devices: int
    tiles: int
    segs: int
    own: int
    rows: int
    width: int
    chans: int
    wide: int
    squeeze: int


def iota(shape, dim):
    return lax.broadcasted_iota(jnp.int32, shape, dim)


def dot(left, right, left_dim, right_dim, precise=False):
    return lax.dot_general(
        left,
        right,
        (((left_dim,), (right_dim,)), ((), ())),
        precision=lax.Precision.HIGHEST if precise else None,
        preferred_element_type=F32,
    )


def fine_dot(left, right):
    high = left.astype(BF16).astype(F32)
    left = jnp.concatenate([high, left - high, high], axis=0).astype(BF16)
    high = right.astype(BF16).astype(F32)
    right = jnp.concatenate([high, high, right - high], axis=0).astype(BF16)
    held = dot(left, right, 1, 1)
    return held[0:8, 0:8] + held[8:16, 8:16] + held[16:24, 16:24]


def eye(rows, cols, dtype=F32):
    return (iota((rows, cols), 0) == iota((rows, cols), 1)).astype(dtype)


def spread(column):
    return jnp.broadcast_to(column, (column.shape[0], LANES))


def lane_sum(values):
    return jnp.sum(values, axis=1, keepdims=True)


def sigmoid(values):
    return 0.5 * jnp.tanh(0.5 * values) + 0.5


def vector(ref):
    return ref[...].astype(F32).reshape(1, ref.shape[0])


def thirds(values):
    high = values.astype(BF16)
    rest = values - high.astype(F32)
    middle = rest.astype(BF16)
    return [high, middle, (rest - middle.astype(F32)).astype(BF16)]


def doubled(values):
    high = values.astype(BF16)
    return jnp.concatenate([high, (values - high.astype(F32)).astype(BF16)], axis=1)


def tripled(values):
    return jnp.concatenate(thirds(values), axis=1)


def row_sums(values):
    return dot(jnp.ones((8, 3 * LANES), BF16), tripled(values), 1, 1)[0:1]


def padded_rows(rows, count):
    spare = count - sum(row.shape[0] for row in rows)
    if spare:
        rows = rows + [jnp.zeros((spare, rows[0].shape[1]), F32)]
    return jnp.concatenate(rows, axis=0)


def spread_by(rows, unit):
    held = jnp.concatenate(thirds(rows), axis=0)
    return dot(held, jnp.concatenate([unit] * 3, axis=0), 0, 0)


def spread_rows(rows):
    count = len(rows)
    shape = (16, count * LANES)
    unit = jnp.where(iota(shape, 0) == lax.div(iota(shape, 1), LANES), 1.0, 0.0).astype(BF16)
    wide = spread_by(padded_rows(rows, 16), unit)
    return [wide[:, at * LANES : (at + 1) * LANES] for at in range(count)]


def columns_of(rows):
    held = padded_rows(rows, 8)
    width = held.shape[1]
    spare = (-width) % LANES
    if spare:
        held = jnp.concatenate([held, jnp.zeros((8, spare), F32)], axis=1)
    return held.T[:width]


def turned(cells):
    rows, width = cells.shape
    spare = (-width) % LANES
    held = jnp.concatenate([cells.astype(F32), jnp.zeros((rows, spare), F32)], axis=1)
    return held.T[:width].astype(cells.dtype)


def placed_sums(acc_ref, count, start):
    lane = iota((2 * LANES, LANES), 1)
    result = 0.0
    for at in range(count):
        unit = jnp.where(lane == start + at, 1.0, 0.0).astype(BF16)
        result = result + dot(doubled(acc_ref[at]), unit, 1, 0)
    return result


def lane_at(sz):
    lane = iota((1, LANES), 1)
    step = sz.width * sz.own
    return lax.rem(lane, sz.width), lax.rem(lax.div(lane, sz.width), sz.own), lax.div(lane, step)


def seg_lanes(sz, rows):
    slot = lax.rem(lax.div(iota((rows, LANES), 1), sz.width), sz.own)
    return jnp.where(slot == iota((rows, LANES), 0), 1.0, 0.0).astype(BF16)


def seg_sums(sz, values):
    lanes = seg_lanes(sz, 16)
    return dot(jnp.concatenate([lanes] * 3, axis=1), tripled(values), 1, 1)[0:8]


def seg_spread(sz, rows):
    return spread_by(padded_rows([rows], 16), seg_lanes(sz, 16))


def mask_rows(sz, info):
    return [info[t : t + 1] for t in range(sz.rows)]


def half_of(ref, t, e):
    first = e - e % 16
    return ref[t, first : first + 16].astype(F32)[e - first : e - first + 8]


def shift_unit(sz):
    source = iota((LANES, 2 * LANES), 0)
    column = iota((LANES, 2 * LANES), 1)
    lane = lax.rem(column, LANES)
    spot = lax.rem(lane, sz.width)
    left = jnp.where((source == lane - 1) & (spot != 0), 1.0, 0.0)
    right = jnp.where((source == lane + 1) & (spot != sz.width - 1), 1.0, 0.0)
    return jnp.where(column < LANES, left, right).astype(BF16)


def block_unit(sz):
    source = iota((LANES, 2 * LANES), 0)
    column = iota((LANES, 2 * LANES), 1)
    lane = lax.rem(column, LANES)
    step = sz.width * sz.own
    before = jnp.where(source == lane - step, 1.0, 0.0)
    after = jnp.where(source == lane + step, 1.0, 0.0)
    return jnp.where(column < LANES, before, after).astype(BF16)


def field_shifts(sz, fields, sh_ref, unit_ref, exact):
    deep = LANES if exact else 2 * LANES

    def parts(values):
        return values.astype(BF16) if exact else doubled(values)

    before = dot(parts(fields[-1]), unit_ref[0:deep, 2 * LANES : 3 * LANES], 1, 0)
    after = dot(parts(fields[0]), unit_ref[0:deep, 3 * LANES :], 1, 0)
    rows = [before] + fields + [after]
    cells = parts(jnp.concatenate(rows, axis=0))
    sides = dot(cells, unit_ref[0:deep, 0 : 2 * LANES], 1, 0)
    for t, row in enumerate(rows):
        part = slice(t * sz.wide, (t + 1) * sz.wide)
        sh_ref[0, t] = sides[part, :LANES]
        sh_ref[1, t] = row
        sh_ref[2, t] = sides[part, LANES:]


def pixel_product(values, pix_ref):
    cells = pix_ref[...].reshape(-1, LANES)
    even = jnp.concatenate(values[0::2], axis=1)
    odd = jnp.concatenate(values[1::2], axis=1)
    if even.dtype == F32:
        cells = jnp.concatenate([cells, cells], axis=0)
        even = doubled(even)
        odd = doubled(odd)
    return dot(even, cells, 1, 0), dot(odd, cells, 1, 0)


def backward_parts(sz, sh_ref, tap_ref, part, acts, acc_ref):
    result = [0.0] * sz.rows
    for j in range(3):
        taps = [tap_ref[3 * i + j, part] for i in range(3)]
        held = [0.0] * 3
        for at in range(sz.rows + 2):
            field = sh_ref[2 - j, at, part]
            for i in range(3):
                t = at - 2 + i
                if 0 <= t < sz.rows:
                    result[t] = result[t] + field * taps[i]
                    if acts is not None:
                        held[i] = held[i] + field * acts[t]
        if acts is not None:
            for i in range(3):
                acc_ref[3 * i + j, part] = held[i]
    return result


def every(sz, ref, first, step):
    return ref[pl.ds(first, sz.devices, stride=step), :]


def wide_rows(first, second, half, last):
    tail = [first[:, LANES:], second[:, LANES:], jnp.zeros((1, LANES - 2 * half), F32)]
    tail = jnp.concatenate(tail, axis=1)
    return jnp.concatenate([first[:, :LANES], second[:, :LANES], tail, last], axis=0)


def wide_pair(block, half):
    first = jnp.concatenate([block[0:1], block[2:3, :half]], axis=1)
    second = jnp.concatenate([block[1:2], block[2:3, half : 2 * half]], axis=1)
    return first, second


def wide_moments(sz, ref, half):
    sums, squares, tails, counts = (every(sz, ref, at, 4) for at in range(4))
    total = jnp.sum(counts, axis=0, keepdims=True)
    inverse = 1.0 / jnp.maximum(counts, 1.0)
    means = []
    spares = []
    for held in (sums, tails):
        mean_val = jnp.sum(held, axis=0, keepdims=True) / total
        offset = held - counts * mean_val
        means.append(mean_val)
        spares.append(jnp.sum(offset * offset * inverse, axis=0, keepdims=True))
    low = jnp.sum(squares, axis=0, keepdims=True) + spares[0]
    high = jnp.sum(tails, axis=0, keepdims=True)[:, half : 2 * half] + spares[1][:, :half]
    square = jnp.concatenate([low, high], axis=1)
    mean_row = jnp.concatenate([means[0], means[1][:, :half]], axis=1)
    total_row = jnp.concatenate([total, total[:, :half]], axis=1)
    return mean_row, lax.rsqrt(square / total_row + EPSILON), total_row


def send_block(ref, block):
    count = block.shape[0]
    if count < 8:
        block = jnp.concatenate([block] * (8 // count), axis=0)
    for at in range(0, ref.shape[0], 8):
        ref[at : at + 8] = block


def steps(sz):
    return [0] + list(range(2, sz.tiles)) + [1]


def partner(step):
    return lax.bitwise_xor(lax.axis_index("tile"), step)


def entry_kernel(sz, x_hbm, w_hbm, len_hbm, count_hbm, pay_ref, info_ref, far_info, *scratch):
    x_ref, w_ref, len_ref, count_ref, sems = scratch
    copies = [
        pltpu.make_async_copy(len_hbm, len_ref, sems.at[0]),
        pltpu.make_async_copy(count_hbm, count_ref, sems.at[1]),
        pltpu.make_async_copy(w_hbm, w_ref, sems.at[2]),
        pltpu.make_async_copy(x_hbm, x_ref, sems.at[3]),
    ]
    for copy in copies:
        copy.start()
    for copy in copies[:2]:
        copy.wait()
    tile_pos = lax.axis_index("tile")
    lane_seg = lax.div(iota((1, LANES), 1), sz.width)
    lengths = []
    far_length = jnp.zeros((1, LANES), jnp.int32)
    count = jnp.zeros((), jnp.int32)
    for s in range(sz.segs):
        held = jnp.where(s < count_ref[0], len_ref[s], 0)
        far_length = jnp.where(lane_seg == s, held, far_length)
        count = count + jnp.clip(held - tile_pos * sz.rows, 0, sz.rows)
    count = jnp.full((1, LANES), (count * sz.width).astype(F32))
    masks = [(tile_pos * sz.rows + t < far_length).astype(F32) for t in range(sz.rows)]
    far_info[...] = jnp.zeros(far_info.shape, F32)
    for t in range(sz.rows):
        far_info[t : t + 1] = masks[t]
    first = tile_pos * sz.own
    _, slot, block = lane_at(sz)
    length = jnp.zeros((1, LANES), jnp.int32)
    own_count = jnp.zeros((), jnp.int32)
    at = iota((8, LANES), 0)
    frames = jnp.ones((8, LANES), F32)
    for s in range(sz.own):
        held = jnp.where(first + s < count_ref[0], len_ref[first + s], 0)
        length = jnp.where(slot == s, held, length)
        own_count = own_count + jnp.minimum(held, sz.rows * sz.tiles)
        frame = jnp.maximum((held * sz.width).astype(F32), 1.0)
        frames = jnp.where(at == s, frame, frames)
    info_ref[...] = jnp.zeros(info_ref.shape, F32)
    for t in range(sz.rows):
        info_ref[t : t + 1] = (block * sz.rows + t < length).astype(F32)
    info_ref[7:8] = jnp.full((1, LANES), (own_count * sz.width).astype(F32))
    info_ref[8:16] = frames
    unit = eye(sz.chans, sz.chans, BF16)
    for copy in copies[2:]:
        copy.wait()
    weights = w_ref[...]
    cells = [dot(unit, x_ref[:, t].reshape(LANES, sz.chans), 1, 1) for t in range(sz.rows)]
    centre = cells[0][:, 0:1]
    cells = jnp.concatenate([(cells[t] - centre) * masks[t] for t in range(sz.rows)], axis=1)
    high = cells.astype(BF16)
    low = (cells - high.astype(F32)).astype(BF16)
    left = jnp.concatenate([high, low, high, low], axis=1)
    right = jnp.concatenate([high, high, low, low], axis=1)
    ones = jnp.ones((sz.chans, left.shape[1]), BF16)
    second = dot(left, right, 1, 1)
    halves = jnp.concatenate([high, low], axis=1)
    ones = ones[:, : halves.shape[1]]
    across = dot(ones, halves, 1, 1)
    down = dot(halves, ones, 1, 1)
    divided = jnp.maximum(count[:, : sz.chans], 1.0)
    spare = second - down * (across / divided)
    wide = sum(dot(held, weights, 1, 0) for held in thirds(spare))
    square = jnp.sum(wide * weights.astype(F32), axis=0, keepdims=True)
    total = down + centre * count[:, : sz.chans]
    wide_sum = jnp.concatenate([total[:, 0:1]] * 8, axis=1)
    wide_sum = dot(wide_sum, weights.astype(F32), 0, 0, True)[0:1]
    send_block(pay_ref, wide_rows(wide_sum, square, sz.wide - LANES, count))


def send_kernel(sz, x_ref, c_ref, after_ref, *out_refs):
    del after_ref
    for step, out_ref in zip(steps(sz), out_refs):
        first = partner(step) * sz.own
        out_ref[...] = jnp.zeros(out_ref.shape, BF16)
        for t in range(sz.rows):
            at = (t % 2) * 2 * sz.chans
            out_ref[:, t // 2, :, at : at + sz.chans] = x_ref[pl.ds(first, sz.own), t]
            at = at + sz.chans
            out_ref[:, t // 2, :, at : at + sz.chans] = c_ref[pl.ds(first, sz.own), t]


def setup_kernel(sz, *refs):
    wide_refs, small_refs, dw_ref, rw_ref, sw_ref, pw_in, w_in = (
        refs[0:5],
        refs[5:8],
        *refs[8:13],
    )
    info_in, far_in, par_ref, tap_ref, unit_ref, pw_ref, pwt_ref, w_ref, wt_ref = refs[13:22]
    info_ref, far_info = refs[22:]
    info_ref[...] = info_in[...]
    far_info[...] = far_in[...]
    par_ref[...] = jnp.zeros(par_ref.shape, F32)
    for at, ref in enumerate(wide_refs):
        par_ref[at : at + 1] = vector(ref)
    for at, ref in enumerate(small_refs):
        par_ref[5 + at : 6 + at, 0 : ref.shape[0]] = vector(ref)
    par_ref[8 : 8 + sz.squeeze] = rw_ref[...]
    par_ref[16 : 16 + sz.squeeze] = sw_ref[...]
    pw_ref[...] = pw_in[...]
    pwt_ref[...] = turned(pw_in[...])
    w_ref[...] = w_in[...]
    wt_ref[...] = turned(w_in[...])
    taps = spread_rows([dw_ref[i, j : j + 1].astype(F32) for i in range(3) for j in range(3)])
    for at in range(9):
        tap_ref[at] = taps[at]
    for at, unit in enumerate([shift_unit(sz), block_unit(sz)]):
        part = slice(at * 2 * LANES, (at + 1) * 2 * LANES)
        unit_ref[0:LANES, part] = unit
        unit_ref[LANES:, part] = unit


def moment_kernel(sz, pay_ref, par_ref, row_ref, wide_ref):
    mean0, inv0, total = wide_moments(sz, pay_ref, sz.wide - LANES)
    row_ref[0:1] = mean0
    row_ref[1:2] = inv0
    row_ref[2:3] = total
    for at, held in enumerate(spread_rows([mean0, inv0 * par_ref[0:1], par_ref[1:2]])):
        wide_ref[at] = held


def stage_one_kernel(sz, wide_ref, *refs):
    own_refs = refs[: sz.tiles]
    wt_ref, tap_ref, unit_ref, info_ref = refs[sz.tiles : sz.tiles + 4]
    refs = refs[sz.tiles + 4 :]
    out_pay, xc_ref, pix_ref, act0_ref, deep_ref, ec_ref, s0_ref, near_ref, part_ref = refs[:9]
    mat_ref, acc_ref, sh_ref, buf_ref = refs[9:]
    chans = sz.chans
    half = sz.wide - LANES
    size = sz.own * sz.width
    for step, ref in zip(steps(sz), own_refs):
        source = partner(step)
        for g in range(sz.rows // 2):
            pix_ref[g, source] = ref[:, g].reshape(size, LANES)
    unit = eye(LANES, LANES, BF16)
    expanded = []
    for g in range(sz.rows // 2):
        flat = dot(unit, pix_ref[g].reshape(LANES, LANES), 1, 1)
        for par in range(2):
            at = par * 2 * chans
            xc_ref[2 * g + par] = flat[at : at + 2 * chans].astype(BF16)
            cells = flat[at : at + chans].astype(BF16)
            expanded.append(dot(wt_ref[...], cells, 1, 0))
    info = info_ref[...]
    masks = mask_rows(sz, info)
    count = info[7:8]
    mean_c, slope_c, bias_c = (wide_ref[at] for at in range(3))
    acts = []
    squares = 0.0
    for t in range(sz.rows):
        centred = expanded[t] - mean_c
        pre = centred * slope_c + bias_c
        gate = sigmoid(pre)
        held = pre * gate
        ec_ref[t] = centred
        s0_ref[t] = (gate + held * (1.0 - gate)) * masks[t]
        act = (held * masks[t]).astype(BF16)
        act0_ref[t] = act
        act = act.astype(F32)
        squares = squares + act * act
        acts.append(act)
    field_shifts(sz, acts, sh_ref, unit_ref, True)
    step = sz.width * sz.own
    spot, _, block = lane_at(sz)
    full = [jnp.broadcast_to(mask, (8, LANES)) for mask in masks]
    before = jnp.where(block == 0, 0.0, pltpu.roll(full[-1], step, 1))
    after = jnp.where(block == sz.tiles - 1, 0.0, pltpu.roll(full[0], LANES - step, 1))
    full = [before] + full + [after]
    left = jnp.broadcast_to(jnp.where(spot == 0, 0.0, 1.0), (8, LANES))
    right = jnp.broadcast_to(jnp.where(spot == sz.width - 1, 0.0, 1.0), (8, LANES))
    total_sum = []
    for e in range(0, sz.wide, 8):
        part = slice(e, e + 8)
        taps = [tap_ref[at, part] for at in range(9)]
        acts = [half_of(act0_ref, t, e) for t in range(sz.rows)]
        sums = 0.0
        edged = [taps[3 * i] * right + taps[3 * i + 1] + taps[3 * i + 2] * left for i in range(3)]
        deep = [0.0] * sz.rows
        for j in range(3):
            for at in range(sz.rows + 2):
                field = sh_ref[j, at, part]
                for i in range(3):
                    if 0 <= at - i < sz.rows:
                        deep[at - i] = deep[at - i] + field * taps[3 * i + j]
        for t in range(sz.rows):
            back = 0.0
            for i in range(3):
                back = back + full[t + 2 - i] * edged[i]
            deep_ref[t, part] = deep[t]
            sums = sums + deep[t] * masks[t]
            mat_ref[t, part] = back * s0_ref[t, part]
        total_sum.append(sums)
        for i in range(3):
            held = sum(full[t + 2 - i] * acts[t] for t in range(sz.rows))
            acc_ref[3 * i, part] = held * right
            acc_ref[3 * i + 1, part] = held
            acc_ref[3 * i + 2, part] = held * left
    total_sum = jnp.concatenate(total_sum, axis=0)
    mean_own = lane_sum(total_sum) / jnp.maximum(count[:, 0:1], 1.0)
    square = 0.0
    for t in range(sz.rows):
        centred = (deep_ref[t] - mean_own) * masks[t]
        square = square + centred * centred
    send_block(out_pay, wide_rows(row_sums(total_sum), row_sums(square), half, count))
    part_ref[...] = placed_sums(acc_ref, 9, 3 * chans + 9)
    even, odd = pixel_product([mat_ref[t] for t in range(sz.rows)], pix_ref)
    held = even + pltpu.roll(odd, LANES - 2 * chans, 1)
    cells = [xc_ref[t].astype(F32)[:chans] * masks[t] for t in range(sz.rows)]
    x_sum = sum(cells)
    even, odd = pixel_product([cell.astype(BF16) for cell in cells], pix_ref)
    second = even[:, :chans] + odd[:, 2 * chans : 3 * chans]
    near_ref[...] = jnp.zeros(near_ref.shape, F32)
    buf_ref[...] = held
    for k in range(5):
        rows = min(32, sz.wide - 32 * k)
        near_ref[0:rows, chans * k : chans * (k + 1)] = buf_ref[32 * k : 32 * k + rows, 0:chans]
    near_ref[16:32, 4 * chans : 5 * chans] = second[0:16]
    near_ref[0:chans, 5 * chans : LANES] = second[:, 16:]
    x_row = row_sums(x_sum)
    for k in range(3):
        near_ref[chans + k : chans + k + 1, 5 * chans : LANES] = x_row[:, 8 * k : 8 * k + 8]
    squares = jnp.sum(squares.reshape(sz.wide // 8, 8, LANES), axis=0)
    squares = jnp.sum(lane_sum(squares), axis=0, keepdims=True)
    near_ref[chans + 3 : chans + 4, 5 * chans : 5 * chans + 1] = squares


def stage_two_kernel(
    sz,
    pay_ref,
    deep_ref,
    xc_ref,
    pix_ref,
    par_ref,
    tap_ref,
    unit_ref,
    info_ref,
    pw_ref,
    near_ref,
    act0_ref,
    s0_ref,
    part_ref,
    out_pay,
    act1_ref,
    dc_ref,
    s1_ref,
    proj_ref,
    gate_ref,
    seg_ref,
    row_ref,
    buf_ref,
    sq_ref,
    mat_ref,
    acc_ref,
    sh_ref,
):
    chans = sz.chans
    half = sz.wide - LANES
    mean1, inv1, _ = wide_moments(sz, pay_ref, half)
    row_ref[0:1] = mean1
    row_ref[1:2] = inv1
    info = info_ref[...]
    masks = mask_rows(sz, info)
    count = info[7:8]
    mean_c, slope_c, bias_c = spread_rows([mean1, inv1 * par_ref[2:3], par_ref[3:4]])
    pool = 0.0
    squares = 0.0
    fields = []
    for t in range(sz.rows):
        centred = deep_ref[t] - mean_c
        pre = centred * slope_c + bias_c
        gate = sigmoid(pre)
        held = pre * gate
        dc_ref[t] = centred
        s1_ref[t] = (gate + held * (1.0 - gate)) * masks[t]
        act = held * masks[t]
        act1_ref[t] = act
        pool = pool + act
        squares = squares + act * act
        fields.append(centred * masks[t])
    pooled = seg_sums(sz, pool) / info[8:16, 0:1]
    rw = par_ref[8:16]
    sw = par_ref[16:24]
    squeeze_pre = fine_dot(pooled, rw) + par_ref[7:8, 0:8]
    squeezed = squeeze_pre * sigmoid(squeeze_pre)
    gate = sigmoid(dot(squeezed, sw, 1, 0, True) + par_ref[4:5])
    seg_ref[0] = pooled
    seg_ref[1] = gate
    seg_ref[2, :, 0:8] = squeeze_pre
    gate_wide = seg_spread(sz, gate)
    gate_ref[...] = gate_wide
    sums = 0.0
    sum_g = 0.0
    gated = 0.0
    for t in range(sz.rows):
        act = (act1_ref[t] * gate_wide).astype(BF16)
        cells = dot(pw_ref[...], act, 1, 0)
        proj_ref[t] = cells
        sums = sums + cells * masks[t]
        sum_g = sum_g + xc_ref[t].astype(F32)[chans:] * masks[t]
        act = act.astype(F32)
        gated = gated + act * act
    sq_ref[0:8] = jnp.sum(squares.reshape(sz.wide // 8, 8, LANES), axis=0)
    sq_ref[8:16] = jnp.sum(gated.reshape(sz.wide // 8, 8, LANES), axis=0)
    mean_own = lane_sum(sums) / jnp.maximum(count[:, 0:1], 1.0)
    square = 0.0
    sum_gp = 0.0
    for t in range(sz.rows):
        centred = (proj_ref[t] - mean_own) * masks[t]
        square = square + centred * centred
        sum_gp = sum_gp + centred * xc_ref[t].astype(F32)[chans:]
    row = row_sums(jnp.concatenate([sums, square, sum_g, sum_gp], axis=0))
    row = jnp.concatenate([row, count[:, 4 * chans :]], axis=1)
    each = near_ref.shape[0] // sz.devices
    out_pay[pl.ds(0, sz.devices, stride=2), :] = jnp.broadcast_to(row, (sz.devices, LANES))
    out_pay[pl.ds(1, sz.devices, stride=2), :] = near_ref[...]
    field_shifts(sz, fields, sh_ref, unit_ref, False)
    for e in range(0, sz.wide, 8):
        part = slice(e, e + 8)
        acts = [half_of(act0_ref, t, e) for t in range(sz.rows)]
        back = backward_parts(sz, sh_ref, tap_ref, part, acts, acc_ref)
        for t in range(sz.rows):
            mat_ref[t, part] = back[t] * s0_ref[t, part]
    even, odd = pixel_product([mat_ref[t] for t in range(sz.rows)], pix_ref)
    lane = iota((1, LANES), 1)
    held = pltpu.roll(even, 2 * chans, 1) + odd
    held = jnp.where((lane >= 2 * chans) & (lane < 3 * chans), held, 0.0)
    buf_ref[...] = part_ref[...] + placed_sums(acc_ref, 9, 3 * chans + 18) + held


def stage_three_kernel(
    sz,
    pay_ref,
    proj_ref,
    xc_ref,
    pix_ref,
    act0_ref,
    act1_ref,
    s0_ref,
    dc_ref,
    s1_ref,
    gate_ref,
    seg_ref,
    par_ref,
    tap_ref,
    unit_ref,
    info_ref,
    pwt_ref,
    part_ref,
    sq_ref,
    row_ref,
    out_pay,
    res_ref,
    scaled_ref,
    bg2_ref,
    gg2_ref,
    ga_ref,
    mat_ref,
    acc_ref,
    sh_ref,
    buf_ref,
):
    chans = sz.chans
    half = sz.wide - LANES
    info = info_ref[...]
    masks = mask_rows(sz, info)
    parts = every(sz, pay_ref, 0, 2)
    near = every(sz, pay_ref, 1, 2)
    sums = jnp.sum(parts, axis=0, keepdims=True)
    counts = pltpu.roll(parts, LANES - 4 * chans, 1)
    shares = pltpu.roll(parts, LANES - 2 * chans, 1)
    total = sums[:, 4 * chans : 4 * chans + 1]
    mean_row = sums / total
    offset = parts - counts * mean_row
    scaled = offset / jnp.maximum(counts, 1.0)
    spare = jnp.sum(offset * scaled, axis=0, keepdims=True)
    cross = jnp.sum(scaled * shares, axis=0, keepdims=True)
    square = sums[:, chans : 2 * chans] + spare[:, :chans]
    inv2 = lax.rsqrt(square / total + EPSILON)
    bias_grad = sums[:, 2 * chans : 3 * chans]
    gain_grad = inv2 * (sums[:, 3 * chans : 4 * chans] + cross[:, :chans])
    bg2_ref[...] = bias_grad.reshape(chans)
    gg2_ref[...] = gain_grad.reshape(chans)
    rows = [mean_row[:, :chans], inv2, bias_grad / total, gain_grad / total]
    rows += [par_ref[5:6, :chans], par_ref[6:7, :chans]]
    columns = columns_of(rows)
    mean_c, inv_c, bg_c, gg_c, gain_c, bias_c = (
        spread(columns[:, at : at + 1]) for at in range(6)
    )
    scale = inv_c * gain_c
    gate_wide = gate_ref[...]
    branch_sq = 0.0
    result_sq = 0.0
    gate_sum = 0.0
    gated = []
    grads = []
    for t in range(sz.rows):
        both = xc_ref[t].astype(F32)
        normed = (proj_ref[t] - mean_c) * inv_c
        branch = (normed * gain_c + bias_c) * masks[t]
        result = both[:chans] + branch
        res_ref[t] = result
        branch_sq = branch_sq + branch * branch
        result_sq = result_sq + result * result * masks[t]
        grad = scale * (both[chans:] - (bg_c + normed * gg_c)) * masks[t]
        wide_grad = dot(pwt_ref[...], grad.astype(BF16), 1, 0)
        ga_ref[t] = wide_grad
        act = act1_ref[t]
        gate_sum = gate_sum + wide_grad * act
        gated.append((act * gate_wide).astype(BF16))
        grads.append(grad.astype(BF16))
    grads = dot(jnp.concatenate(gated, axis=1), jnp.concatenate(grads, axis=1), 1, 1)
    rw = par_ref[8:16]
    sw = par_ref[16:24]
    pooled = seg_ref[0]
    gate = seg_ref[1]
    squeeze_pre = seg_ref[2, :, 0:8]
    slope = sigmoid(squeeze_pre)
    squeezed = squeeze_pre * slope
    slope = slope + squeezed * (1.0 - slope)
    live = (iota((8, 1), 0) < sz.own).astype(F32)
    gate_pre = seg_sums(sz, gate_sum) * gate * (1.0 - gate)
    squeeze_grad = fine_dot(gate_pre, sw) * slope * live
    back = dot(squeeze_grad, rw, 1, 0, True) / info[8:16, 0:1]
    back_wide = seg_spread(sz, back)
    (scale_c,) = spread_rows([row_ref[1:2] * par_ref[2:3]])
    sum_b = 0.0
    sum_g = 0.0
    fields = []
    for t in range(sz.rows):
        grad = (ga_ref[t] * gate_wide + back_wide) * s1_ref[t]
        scaled_ref[t] = grad * scale_c
        sum_b = sum_b + grad
        sum_g = sum_g + grad * dc_ref[t]
        fields.append(grad)
    sum_b = row_sums(sum_b)
    sum_g = row_sums(sum_g) * row_ref[1:2]
    field_shifts(sz, fields, sh_ref, unit_ref, False)
    for e in range(0, sz.wide, 8):
        part = slice(e, e + 8)
        acts = [half_of(act0_ref, t, e) for t in range(sz.rows)]
        back = backward_parts(sz, sh_ref, tap_ref, part, acts, acc_ref)
        for t in range(sz.rows):
            mat_ref[t, part] = back[t] * s0_ref[t, part]
    even, odd = pixel_product([mat_ref[t] for t in range(sz.rows)], pix_ref)
    held = even + pltpu.roll(odd, LANES - 2 * chans, 1)
    held = jnp.where(iota((1, LANES), 1) < chans, held, 0.0)
    buf = part_ref[...] + placed_sums(acc_ref, 9, 3 * chans) + held
    at = 3 * chans + 27
    small = [dot(squeezed, gate_pre, 0, 0, True)[: sz.squeeze]]
    small.append(dot(squeeze_grad, pooled, 0, 0, True)[: sz.squeeze])
    small.append(jnp.sum(gate_pre, axis=0, keepdims=True))
    shape = (16, LANES)
    unit = jnp.where(iota(shape, 0) + at == iota(shape, 1), 1.0, 0.0).astype(BF16)
    buf_ref[...] = buf + spread_by(padded_rows(small, 16), unit)
    buf_ref[:, chans : 2 * chans] = grads
    at = at + 2 * sz.squeeze + 1
    spots = iota((8, 1), 0)
    held = jnp.sum(squeeze_grad, axis=0, keepdims=True)
    column = jnp.zeros((8, 1), F32)
    for k in range(sz.squeeze):
        column = jnp.where(spots == k, held[:, k : k + 1], column)
    buf_ref[0:8, at : at + 1] = column
    column = jnp.zeros((8, 1), F32)
    squares = [
        jnp.sum(result_sq.reshape(chans // 8, 8, LANES), axis=0),
        sq_ref[0:8],
        sq_ref[8:16],
        jnp.sum(branch_sq.reshape(chans // 8, 8, LANES), axis=0),
    ]
    for k, square in enumerate(squares):
        value = jnp.sum(lane_sum(square), axis=0, keepdims=True)
        column = jnp.where(spots == k, value, column)
    buf_ref[8:16, at : at + 1] = column
    used = at + 1
    piece = LANES - used
    for k in range(-(-used // piece)):
        take = min(piece, used - k * piece)
        buf_ref[k * half : (k + 1) * half, used : used + take] = buf_ref[
            LANES : LANES + half, k * piece : k * piece + take
        ]
    each = LANES // sz.devices
    last = jnp.sum(near, axis=0, keepdims=True)
    block = wide_rows(sum_b, sum_g, half, last)
    send_block(out_pay, jnp.concatenate([block, jnp.zeros((4, LANES), F32)], axis=0))
    for k in range(each):
        held = buf_ref[pl.ds(k, sz.devices, stride=each), :]
        out_pay[pl.ds(4 + k, sz.devices, stride=8), :] = held


def stage_four_kernel(
    sz, pay_ref, scaled_ref, dc_ref, ec_ref, s0_ref, row0_ref, row1_ref, par_ref, *refs
):
    tap_ref, unit_ref, info_ref, out_pay, gp0_ref, bg1_ref, gg1_ref, mid_ref, sh_ref = refs
    half = sz.wide - LANES
    masks = mask_rows(sz, info_ref[...])
    block = jnp.sum(pay_ref[...].reshape(sz.devices, 8, LANES), axis=0)
    bias_grad, gain_grad = wide_pair(block, half)
    bg1_ref[...] = bias_grad.reshape(sz.wide)
    gg1_ref[...] = gain_grad.reshape(sz.wide)
    mid_ref[0:1] = bias_grad
    mid_ref[1:2] = gain_grad
    inv1 = row1_ref[1:2]
    scale = inv1 * par_ref[2:3] / row0_ref[2:3]
    bg_c, gg_c = spread_rows([bias_grad * scale, gain_grad * inv1 * scale])
    fields = []
    for t in range(sz.rows):
        grad = scaled_ref[t] - masks[t] * (bg_c + dc_ref[t] * gg_c)
        fields.append(grad.astype(BF16).astype(F32))
    field_shifts(sz, fields, sh_ref, unit_ref, True)
    total_b = []
    total_g = []
    for e in range(0, sz.wide, 8):
        part = slice(e, e + 8)
        back = backward_parts(sz, sh_ref, tap_ref, part, None, None)
        sum_b = 0.0
        sum_g = 0.0
        for t in range(sz.rows):
            grad = back[t] * s0_ref[t, part]
            gp0_ref[t, part] = grad
            sum_b = sum_b + grad
            sum_g = sum_g + grad * ec_ref[t, part]
        total_b.append(sum_b)
        total_g.append(sum_g)
    sum_b = row_sums(jnp.concatenate(total_b, axis=0))
    sum_g = row_sums(jnp.concatenate(total_g, axis=0)) * row0_ref[1:2]
    top = wide_rows(sum_b, sum_g, half, jnp.zeros((1, LANES), F32))
    send_block(out_pay, jnp.concatenate([top, block[4:8]], axis=0))


def back_kernel(sz, gp0_ref, res_ref, row0_ref, par_ref, w_ref, *refs):
    out_refs, all_ref = refs[:-1], refs[-1]
    chans = sz.chans
    (scale,) = spread_rows([row0_ref[1:2] * par_ref[0:1]])
    weights = w_ref[...]
    for g in range(sz.rows // 2):
        pieces = []
        for par in range(2):
            t = 2 * g + par
            pieces += [res_ref[t], dot(weights, (gp0_ref[t] * scale).astype(BF16), 1, 0)]
        pieces.append(jnp.zeros((LANES - 4 * chans, LANES), F32))
        turned = jnp.concatenate(pieces, axis=0).T.astype(BF16)
        all_ref[:, :, g] = turned.reshape(sz.tiles, sz.own, sz.width, LANES)
    for step, out_ref in zip(steps(sz), out_refs):
        out_ref[...] = all_ref[partner(step)]


def far_kernel(sz, pay_ref, x_ref, far_info, row0_ref, w_ref, after_ref, *refs):
    del after_ref
    two_ref, wide_ref, misc_ref, live_ref, buf_ref, near_ref = refs
    chans = sz.chans
    near_ref[...] = every(sz, pay_ref, 3, 8)[0:32]
    buf_ref[...] = jnp.zeros(buf_ref.shape, F32)
    for k in range(5):
        rows = min(32, sz.wide - 32 * k)
        buf_ref[32 * k : 32 * k + rows, 0:chans] = near_ref[0:rows, chans * k : chans * (k + 1)]
    two_ref[...] = picked_rows(buf_ref[...], chans)
    x_row = [near_ref[chans + k : chans + k + 1, 5 * chans : LANES] for k in range(3)]
    x_row = jnp.concatenate(x_row, axis=1)
    x_column = columns_of([x_row])[:, 0:1]
    right = near_ref[0:chans, 5 * chans : LANES]
    below = jnp.concatenate([right.T[0:8, 0:16], right[16:chans]], axis=1)
    second = jnp.concatenate([near_ref[16:32, 4 * chans : 5 * chans], below], axis=0)
    second = second - x_column * x_row / row0_ref[2:3, :chans]
    wide_ref[...] = dot(second, w_ref[...].astype(F32), 1, 0, True) * row0_ref[1:2]
    misc_ref[0:chans] = spread(x_column)
    spot = chans + 3
    misc_ref[chans : chans + 8] = jnp.broadcast_to(
        near_ref[spot : spot + 1, 5 * chans : 5 * chans + 1], (8, LANES)
    )
    shape = (16, sz.rows * LANES)
    unit = jnp.where(iota(shape, 0) == lax.div(iota(shape, 1), LANES), 1.0, 0.0).astype(BF16)
    live = dot(far_info[...].astype(BF16), unit, 0, 0)
    lane = iota((1, 32), 1)
    for t in range(sz.rows):
        held = live[:, t * LANES : t * LANES + 32]
        cells = x_ref[:, t].reshape(sz.segs * sz.width, chans).astype(F32)
        cells = jnp.concatenate([cells, jnp.ones((LANES, 32 - chans), F32)], axis=1)
        live_ref[t] = (jnp.where(lane <= chans, cells, 0.0) * held).astype(BF16)


def picked_rows(columns, count):
    unit = eye(max(count, 16), LANES, BF16)
    return dot(jnp.concatenate([unit] * 3, axis=1), tripled(columns), 1, 1)[0:count]


def last_kernel(
    sz,
    pay_ref,
    two_ref,
    wide_ref,
    misc_ref,
    live_ref,
    row0_ref,
    row1_ref,
    mid_ref,
    par_ref,
    w_ref,
    c_ref,
    *refs,
):
    got_refs = refs[: sz.tiles]
    out_ref, xg_ref, ew_ref, gg0_ref, bg0_ref, dw_ref, rw_ref, rb_ref = refs[
        sz.tiles : sz.tiles + 8
    ]
    sw_ref, sb_ref, pw_ref, rms_ref, corr_ref, buf_ref = refs[sz.tiles + 8 :]
    chans = sz.chans
    half = sz.wide - LANES
    each = LANES // sz.devices
    block = [jnp.sum(every(sz, pay_ref, at, 8), axis=0, keepdims=True) for at in range(3)]
    bias_grad, gain_grad = wide_pair(jnp.concatenate(block, axis=0), half)
    bg0_ref[...] = bias_grad.reshape(sz.wide)
    gg0_ref[...] = gain_grad.reshape(sz.wide)
    mean0 = row0_ref[0:1]
    inv0 = row0_ref[1:2]
    total = row0_ref[2:3]
    scale0 = inv0 * par_ref[0:1]
    bias_row = bias_grad / total
    gain_row = gain_grad / total
    weights = w_ref[...].astype(F32)
    factor = scale0 * gain_row * inv0
    matrix = dot(weights * factor, weights, 1, 1, True)
    offset = jnp.broadcast_to(scale0 * bias_row - factor * mean0, (8, sz.wide))
    offset = dot(offset, weights, 1, 1, True)[0:1]
    matrix = jnp.concatenate([matrix, offset, jnp.zeros((32 - chans - 1, chans), F32)], axis=0)
    high = matrix.astype(BF16)
    low = (matrix - high.astype(F32)).astype(BF16)
    for t in range(sz.rows):
        cells = live_ref[t]
        corr_ref[t] = dot(cells, high, 1, 0) + dot(cells, low, 1, 0)
    shape = (LANES, 4 * LANES)
    column = iota(shape, 1)
    spot = lax.rem(column, LANES)
    source = spot + chans * lax.div(column, LANES)
    unit = jnp.where((iota(shape, 0) == source) & (spot < chans), 1.0, 0.0).astype(BF16)
    size = sz.own * sz.width
    shape = (sz.own, sz.width, chans)
    for step, ref in zip(steps(sz), got_refs):
        first = partner(step) * sz.own
        for g in range(sz.rows // 2):
            cells = dot(ref[:, g].reshape(size, LANES), unit, 1, 0)
            for par in range(2):
                t = 2 * g + par
                at = 2 * par * LANES
                held = cells[:, at : at + chans]
                out_ref[pl.ds(first, sz.own), t] = held.astype(BF16).reshape(shape)
                at = at + LANES
                held = cells[:, at : at + chans] - corr_ref[t, pl.ds(first * sz.width, size)]
                held = held.reshape(shape) + c_ref[pl.ds(first, sz.own), t].astype(F32)
                xg_ref[pl.ds(first, sz.own), t] = held.astype(BF16)
    used = 3 * chans + 29 + 2 * sz.squeeze
    piece = LANES - used
    for k in range(each):
        buf_ref[pl.ds(k, sz.devices, stride=each), :] = every(sz, pay_ref, 4 + k, 8)
    buf_ref[LANES:] = jnp.zeros((half, LANES), F32)
    for k in range(-(-used // piece)):
        take = min(piece, used - k * piece)
        buf_ref[LANES : LANES + half, k * piece : k * piece + take] = buf_ref[
            k * half : (k + 1) * half, used : used + take
        ]
    rows = picked_rows(buf_ref[...], LANES)
    inv1 = row1_ref[1:2]
    scale1 = inv1 * par_ref[2:3]
    bias1 = mid_ref[0:1] / total
    gain1 = mid_ref[1:2] * inv1 / total
    inner = rows[0:chans] - two_ref[...] * bias1 - rows[2 * chans : 3 * chans] * gain1
    x_sum = misc_ref[0:chans, 0:1]
    ew_ref[...] = scale0 * (scale1 * inner - x_sum * bias_row - wide_ref[...] * gain_row)
    pw_ref[...] = rows[chans : 2 * chans]
    spot = 3 * chans
    held = rows[spot : spot + 9] - rows[spot + 9 : spot + 18] * bias1
    held = scale1 * (held - rows[spot + 18 : spot + 27] * gain1)
    for i in range(3):
        dw_ref[i] = held[3 * i : 3 * i + 3]
    spot = spot + 27
    sw_ref[...] = rows[spot : spot + sz.squeeze]
    spot = spot + sz.squeeze
    rw_ref[...] = rows[spot : spot + sz.squeeze]
    spot = spot + sz.squeeze
    sb_ref[...] = rows[spot : spot + 1].reshape(sz.wide)
    misc = rows[spot + 1 : spot + 2]
    rb_ref[...] = misc[:, : sz.squeeze].reshape(sz.squeeze)
    squares = jnp.concatenate(
        [misc[:, 8:9], misc_ref[chans : chans + 1, 0:1], misc[:, 9:10], misc[:, 10:11], misc[:, 11:12]], axis=1
    )
    chan_row = jnp.where(
        (iota((1, 5), 1) == 0) | (iota((1, 5), 1) == 4), float(chans), float(sz.wide)
    )
    rms_ref[...] = jnp.sqrt(squares / (total[:, :5] * chan_row)).reshape(5)


def call(kernel, sz, args, kinds, outs, scratch=(), cost=1.0, room=16):
    spaces = {"v": VMEM, "s": SMEM, "h": HBM, "a": pl.BlockSpec(memory_space=pl.ANY)}
    kinds = kinds + "v" * (len(args) - len(kinds))
    return pl.pallas_call(
        functools.partial(kernel, sz),
        out_shape=tuple(jax.ShapeDtypeStruct(shape, kind) for shape, kind in outs),
        in_specs=[spaces[kind] for kind in kinds],
        out_specs=tuple(VMEM for _ in outs),
        scratch_shapes=[pltpu.VMEM(*held) if isinstance(held, tuple) else held for held in scratch],
        compiler_params=pltpu.CompilerParams(vmem_limit_bytes=room * 1024 * 1024),
        cost_estimate=pl.CostEstimate(
            flops=int(cost * 1e9), bytes_accessed=int(cost * 3e6), transcendentals=0
        ),
        name=kernel.__name__,
    )(*args)


def everywhere(values):
    return lax.all_to_all(values, BOTH, 0, 0, tiled=True)


def passed(sz, parts):
    result = [parts[0]]
    for step, part in zip(steps(sz)[1:], parts[1:]):
        pairs = [(i, i ^ step) for i in range(sz.tiles)]
        result.append(lax.ppermute(part, "tile", pairs))
    return result


def shards(
    x_input,
    expand_w,
    gain0,
    bias0,
    dw_kernel,
    gain1,
    bias1,
    reduce_w,
    reduce_b,
    restore_w,
    restore_b,
    project_w,
    gain2,
    bias2,
    cotangent,
    seg_count,
    seg_len,
):
    segs, rows, width, chans = x_input.shape
    wide, squeeze = reduce_w.shape
    tiles = lax.axis_size("tile")
    devices = lax.axis_size("seg") * tiles
    own = segs // tiles
    sz = Sizes(devices, tiles, segs, own, rows, width, chans, wide, squeeze)
    big = ((rows, wide, LANES), F32)
    small = ((rows, chans, LANES), F32)
    block = ((own, rows // 2, width, LANES), BF16)
    packed = ((rows, wide, LANES), BF16)
    both = ((rows, 2 * chans, LANES), BF16)
    column = ((wide, LANES), F32)
    taps = ((9, wide, LANES), F32)
    shifts = ((3, rows + 2, wide, LANES), F32)

    def pay_of(count):
        return ((devices * count, LANES), F32)

    pay, info, far_info = call(
        entry_kernel,
        sz,
        [x_input, expand_w, seg_len, seg_count],
        "hhhh",
        [pay_of(4), ((16, LANES), F32), ((16, LANES), F32)],
        [
            (x_input.shape, BF16),
            (expand_w.shape, BF16),
            pltpu.SMEM(seg_len.shape, jnp.int32),
            pltpu.SMEM(seg_count.shape, jnp.int32),
            pltpu.SemaphoreType.DMA((4,)),
        ],
        room=60,
    )
    parts = call(send_kernel, sz, [x_input, cotangent, pay], "vvh", [block] * tiles)
    par, tap, unit, pw_near, pw_turned, w_near, w_turned, info, far_info = call(
        setup_kernel,
        sz,
        [gain0, bias0, gain1, bias1, restore_b, gain2, bias2, reduce_b, dw_kernel, reduce_w.T]
        + [restore_w, project_w.T, expand_w, info, far_info],
        "",
        [
            ((24, wide), F32),
            taps,
            ((2 * LANES, 4 * LANES), BF16),
            ((chans, wide), BF16),
            ((wide, chans), BF16),
            ((chans, wide), BF16),
            ((wide, chans), BF16),
            ((16, LANES), F32),
            ((16, LANES), F32),
        ],
    )
    pay = everywhere(pay)
    parts = passed(sz, parts)
    row0, wide0 = call(
        moment_kernel, sz, [pay, par], "", [((3, wide), F32), ((3, wide, LANES), F32)]
    )
    pay, x_c, pix, act0, deep, ec, s0, near, part = call(
        stage_one_kernel,
        sz,
        [wide0] + parts + [w_turned, tap, unit, info],
        "",
        [pay_of(4), both, ((rows // 2, tiles, own * width, LANES), BF16), packed, big, big, big]
        + [((max(32, devices), LANES), F32), column],
        [big, taps, shifts, column],
    )
    pay = everywhere(pay)
    pay, act1, dc, s1, proj, gate, seg_rows, row1, part, squares = call(
        stage_two_kernel,
        sz,
        [pay, deep, x_c, pix, par, tap, unit, info, pw_near, near, act0, s0, part],
        "",
        [pay_of(2), big, big, big, small, column, ((3, 8, wide), F32), ((2, wide), F32)]
        + [column, ((16, LANES), F32)],
        [big, taps, shifts],
    )
    pay = everywhere(pay)
    pay, res, scaled, bg2, gg2 = call(
        stage_three_kernel,
        sz,
        [pay, proj, x_c, pix, act0, act1, s0, dc, s1, gate, seg_rows, par, tap, unit, info]
        + [pw_turned, part, squares, row1],
        "",
        [pay_of(8), small, big, ((chans,), F32), ((chans,), F32)],
        [big, big, taps, shifts, column],
    )
    far_pay = everywhere(pay)
    pay, gp0, bg1, gg1, mid = call(
        stage_four_kernel,
        sz,
        [far_pay, scaled, dc, ec, s0, row0, row1, par, tap, unit, info],
        "",
        [pay_of(8), big, ((wide,), F32), ((wide,), F32), ((2, wide), F32)],
        [shifts],
    )
    sent = call(
        back_kernel,
        sz,
        [gp0, res, row0, par, w_near],
        "",
        [block] * tiles,
        [((tiles,) + block[0], BF16)],
    )
    pay = everywhere(pay)
    sent = passed(sz, sent)
    far = call(
        far_kernel,
        sz,
        [far_pay, x_input, far_info, row0, w_near, gp0],
        "vvvvva",
        [((chans, wide), F32), ((chans, wide), F32), ((chans + 8, LANES), F32)]
        + [((rows, LANES, 32), BF16)],
        [column, ((32, LANES), F32)],
    )
    block_out, x_grad, ew, gg0, bg0, dw, rw, rb, sw, sb, pw, rms = call(
        last_kernel,
        sz,
        [pay] + list(far) + [row0, row1, mid, par, w_near, cotangent] + sent,
        "",
        [
            (x_input.shape, BF16),
            (x_input.shape, BF16),
            ((chans, wide), F32),
            ((wide,), F32),
            ((wide,), F32),
            (dw_kernel.shape, F32),
            ((squeeze, wide), F32),
            ((squeeze,), F32),
            ((squeeze, wide), F32),
            ((wide,), F32),
            ((chans, wide), F32),
            ((5,), F32),
        ],
        [((rows, LANES, chans), F32), column],
    )
    return (
        block_out,
        x_grad,
        ew,
        gg0,
        bg0,
        dw,
        gg1,
        bg1,
        rw.T,
        rb,
        sw,
        sb,
        pw.T,
        gg2,
        bg2,
        rms,
    )


def solution(mesh):
    split = P("seg", "tile", None, None)
    return jax.shard_map(
        shards,
        mesh=mesh,
        in_specs=(split,) + (P(),) * 13 + (split, P("seg"), P("seg")),
        out_specs=(split, split) + (P(),) * 14,
        check_vma=False,
    )
```

```python
import functools
from typing import NamedTuple

import jax
import jax.numpy as jnp
from jax import lax
from jax.experimental import pallas as pl
from jax.experimental.pallas import tpu as pltpu
from jax.sharding import PartitionSpec as P

EPSILON = 0.001
BOTH = ("seg", "tile")
LANES = 128
F32 = jnp.float32
BF16 = jnp.bfloat16
VMEM = pl.BlockSpec(memory_space=pltpu.VMEM)
SMEM = pl.BlockSpec(memory_space=pltpu.SMEM)
HBM = pl.BlockSpec(memory_space=pltpu.HBM)


class Sizes(NamedTuple):
    devices: int
    tiles: int
    segs: int
    own: int
    rows: int
    width: int
    chans: int
    wide: int
    squeeze: int


def iota(shape, dim):
    return lax.broadcasted_iota(jnp.int32, shape, dim)


def dot(left, right, left_dim, right_dim, precise=False):
    return lax.dot_general(
        left,
        right,
        (((left_dim,), (right_dim,)), ((), ())),
        precision=lax.Precision.HIGHEST if precise else None,
        preferred_element_type=F32,
    )


def fine_dot(left, right):
    high = left.astype(BF16).astype(F32)
    left = jnp.concatenate([high, left - high, high], axis=0).astype(BF16)
    high = right.astype(BF16).astype(F32)
    right = jnp.concatenate([high, high, right - high], axis=0).astype(BF16)
    held = dot(left, right, 1, 1)
    return held[0:8, 0:8] + held[8:16, 8:16] + held[16:24, 16:24]


def eye(rows, cols, dtype=F32):
    return (iota((rows, cols), 0) == iota((rows, cols), 1)).astype(dtype)


def spread(column):
    return jnp.broadcast_to(column, (column.shape[0], LANES))


def lane_sum(values):
    return jnp.sum(values, axis=1, keepdims=True)


def sigmoid(values):
    return 0.5 * jnp.tanh(0.5 * values) + 0.5


def vector(ref):
    return ref[...].astype(F32).reshape(1, ref.shape[0])


def thirds(values):
    high = values.astype(BF16)
    rest = values - high.astype(F32)
    middle = rest.astype(BF16)
    return [high, middle, (rest - middle.astype(F32)).astype(BF16)]


def doubled(values):
    high = values.astype(BF16)
    return jnp.concatenate([high, (values - high.astype(F32)).astype(BF16)], axis=1)


def tripled(values):
    return jnp.concatenate(thirds(values), axis=1)


def row_sums(values):
    return dot(jnp.ones((8, 3 * LANES), BF16), tripled(values), 1, 1)[0:1]


def padded_rows(rows, count):
    spare = count - sum(row.shape[0] for row in rows)
    if spare:
        rows = rows + [jnp.zeros((spare, rows[0].shape[1]), F32)]
    return jnp.concatenate(rows, axis=0)


def spread_by(rows, unit):
    held = jnp.concatenate(thirds(rows), axis=0)
    return dot(held, jnp.concatenate([unit] * 3, axis=0), 0, 0)


def spread_rows(rows):
    count = len(rows)
    shape = (16, count * LANES)
    unit = jnp.where(iota(shape, 0) == lax.div(iota(shape, 1), LANES), 1.0, 0.0).astype(BF16)
    wide = spread_by(padded_rows(rows, 16), unit)
    return [wide[:, at * LANES : (at + 1) * LANES] for at in range(count)]


def columns_of(rows):
    held = padded_rows(rows, 8)
    width = held.shape[1]
    spare = (-width) % LANES
    if spare:
        held = jnp.concatenate([held, jnp.zeros((8, spare), F32)], axis=1)
    return held.T[:width]


def turned(cells):
    rows, width = cells.shape
    spare = (-width) % LANES
    held = jnp.concatenate([cells.astype(F32), jnp.zeros((rows, spare), F32)], axis=1)
    return held.T[:width].astype(cells.dtype)


def placed_sums(acc_ref, count, start):
    lane = iota((2 * LANES, LANES), 1)
    result = 0.0
    for at in range(count):
        unit = jnp.where(lane == start + at, 1.0, 0.0).astype(BF16)
        result = result + dot(doubled(acc_ref[at]), unit, 1, 0)
    return result


def lane_at(sz):
    lane = iota((1, LANES), 1)
    step = sz.width * sz.own
    return lax.rem(lane, sz.width), lax.rem(lax.div(lane, sz.width), sz.own), lax.div(lane, step)


def seg_lanes(sz, rows):
    slot = lax.rem(lax.div(iota((rows, LANES), 1), sz.width), sz.own)
    return jnp.where(slot == iota((rows, LANES), 0), 1.0, 0.0).astype(BF16)


def seg_sums(sz, values):
    lanes = seg_lanes(sz, 16)
    return dot(jnp.concatenate([lanes] * 3, axis=1), tripled(values), 1, 1)[0:8]


def seg_spread(sz, rows):
    return spread_by(padded_rows([rows], 16), seg_lanes(sz, 16))


def mask_rows(sz, info):
    return [info[t : t + 1] for t in range(sz.rows)]


def half_of(ref, t, e):
    first = e - e % 16
    return ref[t, first : first + 16].astype(F32)[e - first : e - first + 8]


def shift_unit(sz):
    source = iota((LANES, 2 * LANES), 0)
    column = iota((LANES, 2 * LANES), 1)
    lane = lax.rem(column, LANES)
    spot = lax.rem(lane, sz.width)
    left = jnp.where((source == lane - 1) & (spot != 0), 1.0, 0.0)
    right = jnp.where((source == lane + 1) & (spot != sz.width - 1), 1.0, 0.0)
    return jnp.where(column < LANES, left, right).astype(BF16)


def block_unit(sz):
    source = iota((LANES, 2 * LANES), 0)
    column = iota((LANES, 2 * LANES), 1)
    lane = lax.rem(column, LANES)
    step = sz.width * sz.own
    before = jnp.where(source == lane - step, 1.0, 0.0)
    after = jnp.where(source == lane + step, 1.0, 0.0)
    return jnp.where(column < LANES, before, after).astype(BF16)


def field_shifts(sz, fields, sh_ref, unit_ref, exact):
    deep = LANES if exact else 2 * LANES

    def parts(values):
        return values.astype(BF16) if exact else doubled(values)

    before = dot(parts(fields[-1]), unit_ref[0:deep, 2 * LANES : 3 * LANES], 1, 0)
    after = dot(parts(fields[0]), unit_ref[0:deep, 3 * LANES :], 1, 0)
    rows = [before] + fields + [after]
    cells = parts(jnp.concatenate(rows, axis=0))
    sides = dot(cells, unit_ref[0:deep, 0 : 2 * LANES], 1, 0)
    for t, row in enumerate(rows):
        part = slice(t * sz.wide, (t + 1) * sz.wide)
        sh_ref[0, t] = sides[part, :LANES]
        sh_ref[1, t] = row
        sh_ref[2, t] = sides[part, LANES:]


def pixel_product(values, pix_ref):
    cells = pix_ref[...].reshape(-1, LANES)
    even = jnp.concatenate(values[0::2], axis=1)
    odd = jnp.concatenate(values[1::2], axis=1)
    if even.dtype == F32:
        cells = jnp.concatenate([cells, cells], axis=0)
        even = doubled(even)
        odd = doubled(odd)
    return dot(even, cells, 1, 0), dot(odd, cells, 1, 0)


def backward_parts(sz, sh_ref, tap_ref, part, acts, acc_ref):
    result = [0.0] * sz.rows
    for j in range(3):
        taps = [tap_ref[3 * i + j, part] for i in range(3)]
        held = [0.0] * 3
        for at in range(sz.rows + 2):
            field = sh_ref[2 - j, at, part]
            for i in range(3):
                t = at - 2 + i
                if 0 <= t < sz.rows:
                    result[t] = result[t] + field * taps[i]
                    if acts is not None:
                        held[i] = held[i] + field * acts[t]
        if acts is not None:
            for i in range(3):
                acc_ref[3 * i + j, part] = held[i]
    return result


def every(sz, ref, first, step):
    return ref[pl.ds(first, sz.devices, stride=step), :]


def wide_rows(first, second, half, last):
    tail = [first[:, LANES:], second[:, LANES:], jnp.zeros((1, LANES - 2 * half), F32)]
    tail = jnp.concatenate(tail, axis=1)
    return jnp.concatenate([first[:, :LANES], second[:, :LANES], tail, last], axis=0)


def wide_pair(block, half):
    first = jnp.concatenate([block[0:1], block[2:3, :half]], axis=1)
    second = jnp.concatenate([block[1:2], block[2:3, half : 2 * half]], axis=1)
    return first, second


def wide_moments(sz, ref, half):
    sums, squares, tails, counts = (every(sz, ref, at, 4) for at in range(4))
    total = jnp.sum(counts, axis=0, keepdims=True)
    inverse = 1.0 / jnp.maximum(counts, 1.0)
    means = []
    spares = []
    for held in (sums, tails):
        mean_val = jnp.sum(held, axis=0, keepdims=True) / total
        offset = held - counts * mean_val
        means.append(mean_val)
        spares.append(jnp.sum(offset * offset * inverse, axis=0, keepdims=True))
    low = jnp.sum(squares, axis=0, keepdims=True) + spares[0]
    high = jnp.sum(tails, axis=0, keepdims=True)[:, half : 2 * half] + spares[1][:, :half]
    square = jnp.concatenate([low, high], axis=1)
    mean_row = jnp.concatenate([means[0], means[1][:, :half]], axis=1)
    total_row = jnp.concatenate([total, total[:, :half]], axis=1)
    return mean_row, lax.rsqrt(square / total_row + EPSILON), total_row


def send_block(ref, block):
    count = block.shape[0]
    if count < 8:
        block = jnp.concatenate([block] * (8 // count), axis=0)
    for at in range(0, ref.shape[0], 8):
        ref[at : at + 8] = block


def steps(sz):
    return [0] + list(range(2, sz.tiles)) + [1]


def partner(step):
    return lax.bitwise_xor(lax.axis_index("tile"), step)


def entry_kernel(sz, x_hbm, w_hbm, len_hbm, count_hbm, pay_ref, info_ref, far_info, *scratch):
    x_ref, w_ref, len_ref, count_ref, sems = scratch
    copies = [
        pltpu.make_async_copy(len_hbm, len_ref, sems.at[0]),
        pltpu.make_async_copy(count_hbm, count_ref, sems.at[1]),
        pltpu.make_async_copy(w_hbm, w_ref, sems.at[2]),
        pltpu.make_async_copy(x_hbm, x_ref, sems.at[3]),
    ]
    for copy in copies:
        copy.start()
    for copy in copies[:2]:
        copy.wait()
    tile_pos = lax.axis_index("tile")
    lane_seg = lax.div(iota((1, LANES), 1), sz.width)
    lengths = []
    far_length = jnp.zeros((1, LANES), jnp.int32)
    count = jnp.zeros((), jnp.int32)
    for s in range(sz.segs):
        held = jnp.where(s < count_ref[0], len_ref[s], 0)
        far_length = jnp.where(lane_seg == s, held, far_length)
        count = count + jnp.clip(held - tile_pos * sz.rows, 0, sz.rows)
    count = jnp.full((1, LANES), (count * sz.width).astype(F32))
    masks = [(tile_pos * sz.rows + t < far_length).astype(F32) for t in range(sz.rows)]
    far_info[...] = jnp.zeros(far_info.shape, F32)
    for t in range(sz.rows):
        far_info[t : t + 1] = masks[t]
    first = tile_pos * sz.own
    _, slot, block = lane_at(sz)
    length = jnp.zeros((1, LANES), jnp.int32)
    own_count = jnp.zeros((), jnp.int32)
    at = iota((8, LANES), 0)
    frames = jnp.ones((8, LANES), F32)
    for s in range(sz.own):
        held = jnp.where(first + s < count_ref[0], len_ref[first + s], 0)
        length = jnp.where(slot == s, held, length)
        own_count = own_count + jnp.minimum(held, sz.rows * sz.tiles)
        frame = jnp.maximum((held * sz.width).astype(F32), 1.0)
        frames = jnp.where(at == s, frame, frames)
    info_ref[...] = jnp.zeros(info_ref.shape, F32)
    for t in range(sz.rows):
        info_ref[t : t + 1] = (block * sz.rows + t < length).astype(F32)
    info_ref[7:8] = jnp.full((1, LANES), (own_count * sz.width).astype(F32))
    info_ref[8:16] = frames
    unit = eye(sz.chans, sz.chans, BF16)
    for copy in copies[2:]:
        copy.wait()
    weights = w_ref[...]
    cells = [dot(unit, x_ref[:, t].reshape(LANES, sz.chans), 1, 1) for t in range(sz.rows)]
    centre = cells[0][:, 0:1]
    cells = jnp.concatenate([(cells[t] - centre) * masks[t] for t in range(sz.rows)], axis=1)
    high = cells.astype(BF16)
    low = (cells - high.astype(F32)).astype(BF16)
    left = jnp.concatenate([high, low, high, low], axis=1)
    right = jnp.concatenate([high, high, low, low], axis=1)
    ones = jnp.ones((sz.chans, left.shape[1]), BF16)
    second = dot(left, right, 1, 1)
    halves = jnp.concatenate([high, low], axis=1)
    ones = ones[:, : halves.shape[1]]
    across = dot(ones, halves, 1, 1)
    down = dot(halves, ones, 1, 1)
    divided = jnp.maximum(count[:, : sz.chans], 1.0)
    spare = second - down * (across / divided)
    wide = sum(dot(held, weights, 1, 0) for held in thirds(spare))
    square = jnp.sum(wide * weights.astype(F32), axis=0, keepdims=True)
    total = down + centre * count[:, : sz.chans]
    wide_sum = jnp.concatenate([total[:, 0:1]] * 8, axis=1)
    wide_sum = dot(wide_sum, weights.astype(F32), 0, 0, True)[0:1]
    send_block(pay_ref, wide_rows(wide_sum, square, sz.wide - LANES, count))


def send_kernel(sz, x_ref, c_ref, after_ref, *out_refs):
    del after_ref
    for step, out_ref in zip(steps(sz), out_refs):
        first = partner(step) * sz.own
        out_ref[...] = jnp.zeros(out_ref.shape, BF16)
        for t in range(sz.rows):
            at = (t % 2) * 2 * sz.chans
            out_ref[:, t // 2, :, at : at + sz.chans] = x_ref[pl.ds(first, sz.own), t]
            at = at + sz.chans
            out_ref[:, t // 2, :, at : at + sz.chans] = c_ref[pl.ds(first, sz.own), t]


def setup_kernel(sz, *refs):
    wide_refs, small_refs, dw_ref, rw_ref, sw_ref, pw_in, w_in = (
        refs[0:5],
        refs[5:8],
        *refs[8:13],
    )
    info_in, far_in, par_ref, tap_ref, unit_ref, pw_ref, pwt_ref, w_ref, wt_ref = refs[13:22]
    info_ref, far_info = refs[22:]
    info_ref[...] = info_in[...]
    far_info[...] = far_in[...]
    par_ref[...] = jnp.zeros(par_ref.shape, F32)
    for at, ref in enumerate(wide_refs):
        par_ref[at : at + 1] = vector(ref)
    for at, ref in enumerate(small_refs):
        par_ref[5 + at : 6 + at, 0 : ref.shape[0]] = vector(ref)
    par_ref[8 : 8 + sz.squeeze] = rw_ref[...]
    par_ref[16 : 16 + sz.squeeze] = sw_ref[...]
    pw_ref[...] = pw_in[...]
    pwt_ref[...] = turned(pw_in[...])
    w_ref[...] = w_in[...]
    wt_ref[...] = turned(w_in[...])
    taps = spread_rows([dw_ref[i, j : j + 1].astype(F32) for i in range(3) for j in range(3)])
    for at in range(9):
        tap_ref[at] = taps[at]
    for at, unit in enumerate([shift_unit(sz), block_unit(sz)]):
        part = slice(at * 2 * LANES, (at + 1) * 2 * LANES)
        unit_ref[0:LANES, part] = unit
        unit_ref[LANES:, part] = unit


def moment_kernel(sz, pay_ref, par_ref, row_ref, wide_ref):
    mean0, inv0, total = wide_moments(sz, pay_ref, sz.wide - LANES)
    row_ref[0:1] = mean0
    row_ref[1:2] = inv0
    row_ref[2:3] = total
    for at, held in enumerate(spread_rows([mean0, inv0 * par_ref[0:1], par_ref[1:2]])):
        wide_ref[at] = held


def stage_one_kernel(sz, wide_ref, *refs):
    own_refs = refs[: sz.tiles]
    wt_ref, tap_ref, unit_ref, info_ref = refs[sz.tiles : sz.tiles + 4]
    refs = refs[sz.tiles + 4 :]
    out_pay, xc_ref, pix_ref, act0_ref, deep_ref, ec_ref, s0_ref, near_ref, part_ref = refs[:9]
    mat_ref, acc_ref, sh_ref, buf_ref = refs[9:]
    chans = sz.chans
    half = sz.wide - LANES
    size = sz.own * sz.width
    for step, ref in zip(steps(sz), own_refs):
        source = partner(step)
        for g in range(sz.rows // 2):
            pix_ref[g, source] = ref[:, g].reshape(size, LANES)
    unit = eye(LANES, LANES, BF16)
    expanded = []
    for g in range(sz.rows // 2):
        flat = dot(unit, pix_ref[g].reshape(LANES, LANES), 1, 1)
        for par in range(2):
            at = par * 2 * chans
            xc_ref[2 * g + par] = flat[at : at + 2 * chans].astype(BF16)
            cells = flat[at : at + chans].astype(BF16)
            expanded.append(dot(wt_ref[...], cells, 1, 0))
    info = info_ref[...]
    masks = mask_rows(sz, info)
    count = info[7:8]
    mean_c, slope_c, bias_c = (wide_ref[at] for at in range(3))
    acts = []
    squares = 0.0
    for t in range(sz.rows):
        centred = expanded[t] - mean_c
        pre = centred * slope_c + bias_c
        gate = sigmoid(pre)
        held = pre * gate
        ec_ref[t] = centred
        s0_ref[t] = (gate + held * (1.0 - gate)) * masks[t]
        act = (held * masks[t]).astype(BF16)
        act0_ref[t] = act
        act = act.astype(F32)
        squares = squares + act * act
        acts.append(act)
    field_shifts(sz, acts, sh_ref, unit_ref, True)
    step = sz.width * sz.own
    spot, _, block = lane_at(sz)
    full = [jnp.broadcast_to(mask, (8, LANES)) for mask in masks]
    before = jnp.where(block == 0, 0.0, pltpu.roll(full[-1], step, 1))
    after = jnp.where(block == sz.tiles - 1, 0.0, pltpu.roll(full[0], LANES - step, 1))
    full = [before] + full + [after]
    left = jnp.broadcast_to(jnp.where(spot == 0, 0.0, 1.0), (8, LANES))
    right = jnp.broadcast_to(jnp.where(spot == sz.width - 1, 0.0, 1.0), (8, LANES))
    total_sum = []
    for e in range(0, sz.wide, 8):
        part = slice(e, e + 8)
        taps = [tap_ref[at, part] for at in range(9)]
        acts = [half_of(act0_ref, t, e) for t in range(sz.rows)]
        sums = 0.0
        edged = [taps[3 * i] * right + taps[3 * i + 1] + taps[3 * i + 2] * left for i in range(3)]
        deep = [0.0] * sz.rows
        for j in range(3):
            for at in range(sz.rows + 2):
                field = sh_ref[j, at, part]
                for i in range(3):
                    if 0 <= at - i < sz.rows:
                        deep[at - i] = deep[at - i] + field * taps[3 * i + j]
        for t in range(sz.rows):
            back = 0.0
            for i in range(3):
                back = back + full[t + 2 - i] * edged[i]
            deep_ref[t, part] = deep[t]
            sums = sums + deep[t] * masks[t]
            mat_ref[t, part] = back * s0_ref[t, part]
        total_sum.append(sums)
        for i in range(3):
            held = sum(full[t + 2 - i] * acts[t] for t in range(sz.rows))
            acc_ref[3 * i, part] = held * right
            acc_ref[3 * i + 1, part] = held
            acc_ref[3 * i + 2, part] = held * left
    total_sum = jnp.concatenate(total_sum, axis=0)
    mean_own = lane_sum(total_sum) / jnp.maximum(count[:, 0:1], 1.0)
    square = 0.0
    for t in range(sz.rows):
        centred = (deep_ref[t] - mean_own) * masks[t]
        square = square + centred * centred
    send_block(out_pay, wide_rows(row_sums(total_sum), row_sums(square), half, count))
    part_ref[...] = placed_sums(acc_ref, 9, 3 * chans + 9)
    even, odd = pixel_product([mat_ref[t] for t in range(sz.rows)], pix_ref)
    held = even + pltpu.roll(odd, LANES - 2 * chans, 1)
    cells = [xc_ref[t].astype(F32)[:chans] * masks[t] for t in range(sz.rows)]
    x_sum = sum(cells)
    even, odd = pixel_product([cell.astype(BF16) for cell in cells], pix_ref)
    second = even[:, :chans] + odd[:, 2 * chans : 3 * chans]
    near_ref[...] = jnp.zeros(near_ref.shape, F32)
    buf_ref[...] = held
    for k in range(5):
        rows = min(32, sz.wide - 32 * k)
        near_ref[0:rows, chans * k : chans * (k + 1)] = buf_ref[32 * k : 32 * k + rows, 0:chans]
    near_ref[16:32, 4 * chans : 5 * chans] = second[0:16]
    near_ref[0:chans, 5 * chans : LANES] = second[:, 16:]
    x_row = row_sums(x_sum)
    for k in range(3):
        near_ref[chans + k : chans + k + 1, 5 * chans : LANES] = x_row[:, 8 * k : 8 * k + 8]
    squares = jnp.sum(squares.reshape(sz.wide // 8, 8, LANES), axis=0)
    squares = jnp.sum(lane_sum(squares), axis=0, keepdims=True)
    near_ref[chans + 3 : chans + 4, 5 * chans : 5 * chans + 1] = squares


def stage_two_kernel(
    sz,
    pay_ref,
    deep_ref,
    xc_ref,
    pix_ref,
    par_ref,
    tap_ref,
    unit_ref,
    info_ref,
    pw_ref,
    near_ref,
    act0_ref,
    s0_ref,
    part_ref,
    out_pay,
    act1_ref,
    dc_ref,
    s1_ref,
    proj_ref,
    gate_ref,
    seg_ref,
    row_ref,
    buf_ref,
    sq_ref,
    slope_ref,
    mat_ref,
    acc_ref,
    sh_ref,
):
    chans = sz.chans
    half = sz.wide - LANES
    mean1, inv1, _ = wide_moments(sz, pay_ref, half)
    row_ref[0:1] = mean1
    row_ref[1:2] = inv1
    info = info_ref[...]
    masks = mask_rows(sz, info)
    count = info[7:8]
    mean_c, slope_c, bias_c = spread_rows([mean1, inv1 * par_ref[2:3], par_ref[3:4]])
    slope_ref[...] = slope_c
    pool = 0.0
    squares = 0.0
    fields = []
    for t in range(sz.rows):
        centred = deep_ref[t] - mean_c
        pre = centred * slope_c + bias_c
        gate = sigmoid(pre)
        held = pre * gate
        dc_ref[t] = centred
        s1_ref[t] = (gate + held * (1.0 - gate)) * masks[t]
        act = held * masks[t]
        act1_ref[t] = act
        pool = pool + act
        squares = squares + act * act
        fields.append(centred * masks[t])
    pooled = seg_sums(sz, pool) / info[8:16, 0:1]
    rw = par_ref[8:16]
    sw = par_ref[16:24]
    squeeze_pre = fine_dot(pooled, rw) + par_ref[7:8, 0:8]
    squeezed = squeeze_pre * sigmoid(squeeze_pre)
    gate = sigmoid(dot(squeezed, sw, 1, 0, True) + par_ref[4:5])
    seg_ref[0] = pooled
    seg_ref[1] = gate
    seg_ref[2, :, 0:8] = squeeze_pre
    gate_wide = seg_spread(sz, gate)
    gate_ref[...] = gate_wide
    sums = 0.0
    sum_g = 0.0
    gated = 0.0
    for t in range(sz.rows):
        act = (act1_ref[t] * gate_wide).astype(BF16)
        cells = dot(pw_ref[...], act, 1, 0)
        proj_ref[t] = cells
        sums = sums + cells * masks[t]
        sum_g = sum_g + xc_ref[t].astype(F32)[chans:] * masks[t]
        act = act.astype(F32)
        gated = gated + act * act
    sq_ref[0:8] = jnp.sum(squares.reshape(sz.wide // 8, 8, LANES), axis=0)
    sq_ref[8:16] = jnp.sum(gated.reshape(sz.wide // 8, 8, LANES), axis=0)
    mean_own = lane_sum(sums) / jnp.maximum(count[:, 0:1], 1.0)
    square = 0.0
    sum_gp = 0.0
    for t in range(sz.rows):
        centred = (proj_ref[t] - mean_own) * masks[t]
        square = square + centred * centred
        sum_gp = sum_gp + centred * xc_ref[t].astype(F32)[chans:]
    row = row_sums(jnp.concatenate([sums, square, sum_g, sum_gp], axis=0))
    row = jnp.concatenate([row, count[:, 4 * chans :]], axis=1)
    each = near_ref.shape[0] // sz.devices
    out_pay[pl.ds(0, sz.devices, stride=2), :] = jnp.broadcast_to(row, (sz.devices, LANES))
    out_pay[pl.ds(1, sz.devices, stride=2), :] = near_ref[...]
    field_shifts(sz, fields, sh_ref, unit_ref, False)
    for e in range(0, sz.wide, 8):
        part = slice(e, e + 8)
        acts = [half_of(act0_ref, t, e) for t in range(sz.rows)]
        back = backward_parts(sz, sh_ref, tap_ref, part, acts, acc_ref)
        for t in range(sz.rows):
            mat_ref[t, part] = back[t] * s0_ref[t, part]
    even, odd = pixel_product([mat_ref[t] for t in range(sz.rows)], pix_ref)
    lane = iota((1, LANES), 1)
    held = pltpu.roll(even, 2 * chans, 1) + odd
    held = jnp.where((lane >= 2 * chans) & (lane < 3 * chans), held, 0.0)
    buf_ref[...] = part_ref[...] + placed_sums(acc_ref, 9, 3 * chans + 18) + held


def stage_three_kernel(
    sz,
    pay_ref,
    proj_ref,
    xc_ref,
    pix_ref,
    act0_ref,
    act1_ref,
    s0_ref,
    dc_ref,
    s1_ref,
    gate_ref,
    seg_ref,
    par_ref,
    tap_ref,
    unit_ref,
    info_ref,
    pwt_ref,
    part_ref,
    sq_ref,
    row_ref,
    slope_ref,
    out_pay,
    res_ref,
    scaled_ref,
    bg2_ref,
    gg2_ref,
    ga_ref,
    mat_ref,
    acc_ref,
    sh_ref,
    buf_ref,
):
    chans = sz.chans
    half = sz.wide - LANES
    info = info_ref[...]
    masks = mask_rows(sz, info)
    parts = every(sz, pay_ref, 0, 2)
    near = every(sz, pay_ref, 1, 2)
    sums = jnp.sum(parts, axis=0, keepdims=True)
    counts = pltpu.roll(parts, LANES - 4 * chans, 1)
    shares = pltpu.roll(parts, LANES - 2 * chans, 1)
    total = sums[:, 4 * chans : 4 * chans + 1]
    mean_row = sums / total
    offset = parts - counts * mean_row
    scaled = offset / jnp.maximum(counts, 1.0)
    spare = jnp.sum(offset * scaled, axis=0, keepdims=True)
    cross = jnp.sum(scaled * shares, axis=0, keepdims=True)
    square = sums[:, chans : 2 * chans] + spare[:, :chans]
    inv2 = lax.rsqrt(square / total + EPSILON)
    bias_grad = sums[:, 2 * chans : 3 * chans]
    gain_grad = inv2 * (sums[:, 3 * chans : 4 * chans] + cross[:, :chans])
    bg2_ref[...] = bias_grad.reshape(chans)
    gg2_ref[...] = gain_grad.reshape(chans)
    rows = [mean_row[:, :chans], inv2, bias_grad / total, gain_grad / total]
    rows += [par_ref[5:6, :chans], par_ref[6:7, :chans]]
    columns = columns_of(rows)
    mean_c, inv_c, bg_c, gg_c, gain_c, bias_c = (
        spread(columns[:, at : at + 1]) for at in range(6)
    )
    scale = inv_c * gain_c
    gate_wide = gate_ref[...]
    branch_sq = 0.0
    result_sq = 0.0
    gate_sum = 0.0
    gated = []
    grads = []
    for t in range(sz.rows):
        both = xc_ref[t].astype(F32)
        normed = (proj_ref[t] - mean_c) * inv_c
        branch = (normed * gain_c + bias_c) * masks[t]
        result = both[:chans] + branch
        res_ref[t] = result
        branch_sq = branch_sq + branch * branch
        result_sq = result_sq + result * result * masks[t]
        grad = scale * (both[chans:] - (bg_c + normed * gg_c)) * masks[t]
        wide_grad = dot(pwt_ref[...], grad.astype(BF16), 1, 0)
        ga_ref[t] = wide_grad
        act = act1_ref[t]
        gate_sum = gate_sum + wide_grad * act
        gated.append((act * gate_wide).astype(BF16))
        grads.append(grad.astype(BF16))
    grads = dot(jnp.concatenate(gated, axis=1), jnp.concatenate(grads, axis=1), 1, 1)
    rw = par_ref[8:16]
    sw = par_ref[16:24]
    pooled = seg_ref[0]
    gate = seg_ref[1]
    squeeze_pre = seg_ref[2, :, 0:8]
    slope = sigmoid(squeeze_pre)
    squeezed = squeeze_pre * slope
    slope = slope + squeezed * (1.0 - slope)
    live = (iota((8, 1), 0) < sz.own).astype(F32)
    gate_pre = seg_sums(sz, gate_sum) * gate * (1.0 - gate)
    squeeze_grad = fine_dot(gate_pre, sw) * slope * live
    back = dot(squeeze_grad, rw, 1, 0, True) / info[8:16, 0:1]
    back_wide = seg_spread(sz, back)
    scale_c = slope_ref[...]
    sum_b = 0.0
    sum_g = 0.0
    fields = []
    for t in range(sz.rows):
        grad = (ga_ref[t] * gate_wide + back_wide) * s1_ref[t]
        scaled_ref[t] = grad * scale_c
        sum_b = sum_b + grad
        sum_g = sum_g + grad * dc_ref[t]
        fields.append(grad)
    sum_b = row_sums(sum_b)
    sum_g = row_sums(sum_g) * row_ref[1:2]
    field_shifts(sz, fields, sh_ref, unit_ref, False)
    for e in range(0, sz.wide, 8):
        part = slice(e, e + 8)
        acts = [half_of(act0_ref, t, e) for t in range(sz.rows)]
        back = backward_parts(sz, sh_ref, tap_ref, part, acts, acc_ref)
        for t in range(sz.rows):
            mat_ref[t, part] = back[t] * s0_ref[t, part]
    even, odd = pixel_product([mat_ref[t] for t in range(sz.rows)], pix_ref)
    held = even + pltpu.roll(odd, LANES - 2 * chans, 1)
    held = jnp.where(iota((1, LANES), 1) < chans, held, 0.0)
    buf = part_ref[...] + placed_sums(acc_ref, 9, 3 * chans) + held
    at = 3 * chans + 27
    small = [dot(squeezed, gate_pre, 0, 0, True)[: sz.squeeze]]
    small.append(dot(squeeze_grad, pooled, 0, 0, True)[: sz.squeeze])
    small.append(jnp.sum(gate_pre, axis=0, keepdims=True))
    shape = (16, LANES)
    unit = jnp.where(iota(shape, 0) + at == iota(shape, 1), 1.0, 0.0).astype(BF16)
    buf_ref[...] = buf + spread_by(padded_rows(small, 16), unit)
    buf_ref[:, chans : 2 * chans] = grads
    at = at + 2 * sz.squeeze + 1
    spots = iota((8, 1), 0)
    held = jnp.sum(squeeze_grad, axis=0, keepdims=True)
    column = jnp.zeros((8, 1), F32)
    for k in range(sz.squeeze):
        column = jnp.where(spots == k, held[:, k : k + 1], column)
    buf_ref[0:8, at : at + 1] = column
    column = jnp.zeros((8, 1), F32)
    squares = [
        jnp.sum(result_sq.reshape(chans // 8, 8, LANES), axis=0),
        sq_ref[0:8],
        sq_ref[8:16],
        jnp.sum(branch_sq.reshape(chans // 8, 8, LANES), axis=0),
    ]
    for k, square in enumerate(squares):
        value = jnp.sum(lane_sum(square), axis=0, keepdims=True)
        column = jnp.where(spots == k, value, column)
    buf_ref[8:16, at : at + 1] = column
    used = at + 1
    piece = LANES - used
    for k in range(-(-used // piece)):
        take = min(piece, used - k * piece)
        buf_ref[k * half : (k + 1) * half, used : used + take] = buf_ref[
            LANES : LANES + half, k * piece : k * piece + take
        ]
    each = LANES // sz.devices
    last = jnp.sum(near, axis=0, keepdims=True)
    block = wide_rows(sum_b, sum_g, half, last)
    send_block(out_pay, jnp.concatenate([block, jnp.zeros((4, LANES), F32)], axis=0))
    for k in range(each):
        held = buf_ref[pl.ds(k, sz.devices, stride=each), :]
        out_pay[pl.ds(4 + k, sz.devices, stride=8), :] = held


def stage_four_kernel(
    sz, pay_ref, scaled_ref, dc_ref, ec_ref, s0_ref, row0_ref, row1_ref, par_ref, *refs
):
    tap_ref, unit_ref, info_ref, out_pay, gp0_ref, bg1_ref, gg1_ref, mid_ref, sh_ref = refs
    half = sz.wide - LANES
    masks = mask_rows(sz, info_ref[...])
    block = jnp.sum(pay_ref[...].reshape(sz.devices, 8, LANES), axis=0)
    bias_grad, gain_grad = wide_pair(block, half)
    bg1_ref[...] = bias_grad.reshape(sz.wide)
    gg1_ref[...] = gain_grad.reshape(sz.wide)
    mid_ref[0:1] = bias_grad
    mid_ref[1:2] = gain_grad
    inv1 = row1_ref[1:2]
    scale = inv1 * par_ref[2:3] / row0_ref[2:3]
    bg_c, gg_c = spread_rows([bias_grad * scale, gain_grad * inv1 * scale])
    fields = []
    for t in range(sz.rows):
        grad = scaled_ref[t] - masks[t] * (bg_c + dc_ref[t] * gg_c)
        fields.append(grad.astype(BF16).astype(F32))
    field_shifts(sz, fields, sh_ref, unit_ref, True)
    total_b = []
    total_g = []
    for e in range(0, sz.wide, 8):
        part = slice(e, e + 8)
        back = backward_parts(sz, sh_ref, tap_ref, part, None, None)
        sum_b = 0.0
        sum_g = 0.0
        for t in range(sz.rows):
            grad = back[t] * s0_ref[t, part]
            gp0_ref[t, part] = grad
            sum_b = sum_b + grad
            sum_g = sum_g + grad * ec_ref[t, part]
        total_b.append(sum_b)
        total_g.append(sum_g)
    sum_b = row_sums(jnp.concatenate(total_b, axis=0))
    sum_g = row_sums(jnp.concatenate(total_g, axis=0)) * row0_ref[1:2]
    top = wide_rows(sum_b, sum_g, half, jnp.zeros((1, LANES), F32))
    send_block(out_pay, jnp.concatenate([top, block[4:8]], axis=0))


def back_kernel(sz, gp0_ref, res_ref, wide_ref, w_ref, *refs):
    out_refs, all_ref = refs[:-1], refs[-1]
    chans = sz.chans
    scale = wide_ref[1]
    weights = w_ref[...]
    for g in range(sz.rows // 2):
        pieces = []
        for par in range(2):
            t = 2 * g + par
            pieces += [res_ref[t], dot(weights, (gp0_ref[t] * scale).astype(BF16), 1, 0)]
        pieces.append(jnp.zeros((LANES - 4 * chans, LANES), F32))
        turned = jnp.concatenate(pieces, axis=0).T.astype(BF16)
        all_ref[:, :, g] = turned.reshape(sz.tiles, sz.own, sz.width, LANES)
    for step, out_ref in zip(steps(sz), out_refs):
        out_ref[...] = all_ref[partner(step)]


def far_kernel(sz, pay_ref, x_ref, far_info, row0_ref, w_ref, after_ref, *refs):
    del after_ref
    two_ref, wide_ref, misc_ref, live_ref, buf_ref, near_ref = refs
    chans = sz.chans
    near_ref[...] = every(sz, pay_ref, 3, 8)[0:32]
    buf_ref[...] = jnp.zeros(buf_ref.shape, F32)
    for k in range(5):
        rows = min(32, sz.wide - 32 * k)
        buf_ref[32 * k : 32 * k + rows, 0:chans] = near_ref[0:rows, chans * k : chans * (k + 1)]
    two_ref[...] = picked_rows(buf_ref[...], chans)
    x_row = [near_ref[chans + k : chans + k + 1, 5 * chans : LANES] for k in range(3)]
    x_row = jnp.concatenate(x_row, axis=1)
    x_column = columns_of([x_row])[:, 0:1]
    right = near_ref[0:chans, 5 * chans : LANES]
    below = jnp.concatenate([right.T[0:8, 0:16], right[16:chans]], axis=1)
    second = jnp.concatenate([near_ref[16:32, 4 * chans : 5 * chans], below], axis=0)
    second = second - x_column * x_row / row0_ref[2:3, :chans]
    wide_ref[...] = dot(second, w_ref[...].astype(F32), 1, 0, True) * row0_ref[1:2]
    misc_ref[0:chans] = spread(x_column)
    spot = chans + 3
    misc_ref[chans : chans + 8] = jnp.broadcast_to(
        near_ref[spot : spot + 1, 5 * chans : 5 * chans + 1], (8, LANES)
    )
    shape = (16, sz.rows * LANES)
    unit = jnp.where(iota(shape, 0) == lax.div(iota(shape, 1), LANES), 1.0, 0.0).astype(BF16)
    live = dot(far_info[...].astype(BF16), unit, 0, 0)
    lane = iota((1, 32), 1)
    for t in range(sz.rows):
        held = live[:, t * LANES : t * LANES + 32]
        cells = x_ref[:, t].reshape(sz.segs * sz.width, chans).astype(F32)
        cells = jnp.concatenate([cells, jnp.ones((LANES, 32 - chans), F32)], axis=1)
        live_ref[t] = (jnp.where(lane <= chans, cells, 0.0) * held).astype(BF16)


def picked_rows(columns, count):
    unit = eye(max(count, 16), LANES, BF16)
    return dot(jnp.concatenate([unit] * 3, axis=1), tripled(columns), 1, 1)[0:count]


def last_kernel(
    sz,
    pay_ref,
    two_ref,
    wide_ref,
    misc_ref,
    live_ref,
    row0_ref,
    row1_ref,
    mid_ref,
    par_ref,
    w_ref,
    c_ref,
    *refs,
):
    got_refs = refs[: sz.tiles]
    out_ref, xg_ref, ew_ref, gg0_ref, bg0_ref, dw_ref, rw_ref, rb_ref = refs[
        sz.tiles : sz.tiles + 8
    ]
    sw_ref, sb_ref, pw_ref, rms_ref, corr_ref, buf_ref = refs[sz.tiles + 8 :]
    chans = sz.chans
    half = sz.wide - LANES
    each = LANES // sz.devices
    block = [jnp.sum(every(sz, pay_ref, at, 8), axis=0, keepdims=True) for at in range(3)]
    bias_grad, gain_grad = wide_pair(jnp.concatenate(block, axis=0), half)
    bg0_ref[...] = bias_grad.reshape(sz.wide)
    gg0_ref[...] = gain_grad.reshape(sz.wide)
    mean0 = row0_ref[0:1]
    inv0 = row0_ref[1:2]
    total = row0_ref[2:3]
    scale0 = inv0 * par_ref[0:1]
    bias_row = bias_grad / total
    gain_row = gain_grad / total
    weights = w_ref[...].astype(F32)
    factor = scale0 * gain_row * inv0
    matrix = dot(weights * factor, weights, 1, 1, True)
    offset = jnp.broadcast_to(scale0 * bias_row - factor * mean0, (8, sz.wide))
    offset = dot(offset, weights, 1, 1, True)[0:1]
    matrix = jnp.concatenate([matrix, offset, jnp.zeros((32 - chans - 1, chans), F32)], axis=0)
    high = matrix.astype(BF16)
    low = (matrix - high.astype(F32)).astype(BF16)
    for t in range(sz.rows):
        cells = live_ref[t]
        corr_ref[t] = dot(cells, high, 1, 0) + dot(cells, low, 1, 0)
    shape = (LANES, 4 * LANES)
    column = iota(shape, 1)
    spot = lax.rem(column, LANES)
    source = spot + chans * lax.div(column, LANES)
    unit = jnp.where((iota(shape, 0) == source) & (spot < chans), 1.0, 0.0).astype(BF16)
    size = sz.own * sz.width
    shape = (sz.own, sz.width, chans)
    for step, ref in zip(steps(sz), got_refs):
        first = partner(step) * sz.own
        for g in range(sz.rows // 2):
            cells = dot(ref[:, g].reshape(size, LANES), unit, 1, 0)
            for par in range(2):
                t = 2 * g + par
                at = 2 * par * LANES
                held = cells[:, at : at + chans]
                out_ref[pl.ds(first, sz.own), t] = held.astype(BF16).reshape(shape)
                at = at + LANES
                held = cells[:, at : at + chans] - corr_ref[t, pl.ds(first * sz.width, size)]
                held = held.reshape(shape) + c_ref[pl.ds(first, sz.own), t].astype(F32)
                xg_ref[pl.ds(first, sz.own), t] = held.astype(BF16)
    used = 3 * chans + 29 + 2 * sz.squeeze
    piece = LANES - used
    for k in range(each):
        buf_ref[pl.ds(k, sz.devices, stride=each), :] = every(sz, pay_ref, 4 + k, 8)
    buf_ref[LANES:] = jnp.zeros((half, LANES), F32)
    for k in range(-(-used // piece)):
        take = min(piece, used - k * piece)
        buf_ref[LANES : LANES + half, k * piece : k * piece + take] = buf_ref[
            k * half : (k + 1) * half, used : used + take
        ]
    rows = picked_rows(buf_ref[...], LANES)
    inv1 = row1_ref[1:2]
    scale1 = inv1 * par_ref[2:3]
    bias1 = mid_ref[0:1] / total
    gain1 = mid_ref[1:2] * inv1 / total
    inner = rows[0:chans] - two_ref[...] * bias1 - rows[2 * chans : 3 * chans] * gain1
    x_sum = misc_ref[0:chans, 0:1]
    ew_ref[...] = scale0 * (scale1 * inner - x_sum * bias_row - wide_ref[...] * gain_row)
    pw_ref[...] = rows[chans : 2 * chans]
    spot = 3 * chans
    held = rows[spot : spot + 9] - rows[spot + 9 : spot + 18] * bias1
    held = scale1 * (held - rows[spot + 18 : spot + 27] * gain1)
    for i in range(3):
        dw_ref[i] = held[3 * i : 3 * i + 3]
    spot = spot + 27
    sw_ref[...] = rows[spot : spot + sz.squeeze]
    spot = spot + sz.squeeze
    rw_ref[...] = rows[spot : spot + sz.squeeze]
    spot = spot + sz.squeeze
    sb_ref[...] = rows[spot : spot + 1].reshape(sz.wide)
    misc = rows[spot + 1 : spot + 2]
    rb_ref[...] = misc[:, : sz.squeeze].reshape(sz.squeeze)
    squares = jnp.concatenate(
        [misc[:, 8:9], misc_ref[chans : chans + 1, 0:1], misc[:, 9:10], misc[:, 10:11], misc[:, 11:12]], axis=1
    )
    chan_row = jnp.where(
        (iota((1, 5), 1) == 0) | (iota((1, 5), 1) == 4), float(chans), float(sz.wide)
    )
    rms_ref[...] = jnp.sqrt(squares / (total[:, :5] * chan_row)).reshape(5)


def call(kernel, sz, args, kinds, outs, scratch=(), cost=1.0, room=16):
    spaces = {"v": VMEM, "s": SMEM, "h": HBM, "a": pl.BlockSpec(memory_space=pl.ANY)}
    kinds = kinds + "v" * (len(args) - len(kinds))
    return pl.pallas_call(
        functools.partial(kernel, sz),
        out_shape=tuple(jax.ShapeDtypeStruct(shape, kind) for shape, kind in outs),
        in_specs=[spaces[kind] for kind in kinds],
        out_specs=tuple(VMEM for _ in outs),
        scratch_shapes=[pltpu.VMEM(*held) if isinstance(held, tuple) else held for held in scratch],
        compiler_params=pltpu.CompilerParams(vmem_limit_bytes=room * 1024 * 1024),
        cost_estimate=pl.CostEstimate(
            flops=int(cost * 1e9), bytes_accessed=int(cost * 3e6), transcendentals=0
        ),
        name=kernel.__name__,
    )(*args)


def everywhere(values):
    return lax.all_to_all(values, BOTH, 0, 0, tiled=True)


def passed(sz, parts):
    result = [parts[0]]
    for step, part in zip(steps(sz)[1:], parts[1:]):
        pairs = [(i, i ^ step) for i in range(sz.tiles)]
        result.append(lax.ppermute(part, "tile", pairs))
    return result


def shards(
    x_input,
    expand_w,
    gain0,
    bias0,
    dw_kernel,
    gain1,
    bias1,
    reduce_w,
    reduce_b,
    restore_w,
    restore_b,
    project_w,
    gain2,
    bias2,
    cotangent,
    seg_count,
    seg_len,
):
    segs, rows, width, chans = x_input.shape
    wide, squeeze = reduce_w.shape
    tiles = lax.axis_size("tile")
    devices = lax.axis_size("seg") * tiles
    own = segs // tiles
    sz = Sizes(devices, tiles, segs, own, rows, width, chans, wide, squeeze)
    big = ((rows, wide, LANES), F32)
    small = ((rows, chans, LANES), F32)
    block = ((own, rows // 2, width, LANES), BF16)
    packed = ((rows, wide, LANES), BF16)
    both = ((rows, 2 * chans, LANES), BF16)
    column = ((wide, LANES), F32)
    taps = ((9, wide, LANES), F32)
    shifts = ((3, rows + 2, wide, LANES), F32)

    def pay_of(count):
        return ((devices * count, LANES), F32)

    pay, info, far_info = call(
        entry_kernel,
        sz,
        [x_input, expand_w, seg_len, seg_count],
        "hhhh",
        [pay_of(4), ((16, LANES), F32), ((16, LANES), F32)],
        [
            (x_input.shape, BF16),
            (expand_w.shape, BF16),
            pltpu.SMEM(seg_len.shape, jnp.int32),
            pltpu.SMEM(seg_count.shape, jnp.int32),
            pltpu.SemaphoreType.DMA((4,)),
        ],
        room=60,
    )
    parts = call(send_kernel, sz, [x_input, cotangent, pay], "vvh", [block] * tiles)
    par, tap, unit, pw_near, pw_turned, w_near, w_turned, info, far_info = call(
        setup_kernel,
        sz,
        [gain0, bias0, gain1, bias1, restore_b, gain2, bias2, reduce_b, dw_kernel, reduce_w.T]
        + [restore_w, project_w.T, expand_w, info, far_info],
        "",
        [
            ((24, wide), F32),
            taps,
            ((2 * LANES, 4 * LANES), BF16),
            ((chans, wide), BF16),
            ((wide, chans), BF16),
            ((chans, wide), BF16),
            ((wide, chans), BF16),
            ((16, LANES), F32),
            ((16, LANES), F32),
        ],
    )
    pay = everywhere(pay)
    parts = passed(sz, parts)
    row0, wide0 = call(
        moment_kernel, sz, [pay, par], "", [((3, wide), F32), ((3, wide, LANES), F32)]
    )
    pay, x_c, pix, act0, deep, ec, s0, near, part = call(
        stage_one_kernel,
        sz,
        [wide0] + parts + [w_turned, tap, unit, info],
        "",
        [pay_of(4), both, ((rows // 2, tiles, own * width, LANES), BF16), packed, big, big, big]
        + [((max(32, devices), LANES), F32), column],
        [big, taps, shifts, column],
    )
    pay = everywhere(pay)
    pay, act1, dc, s1, proj, gate, seg_rows, row1, part, squares, slope1 = call(
        stage_two_kernel,
        sz,
        [pay, deep, x_c, pix, par, tap, unit, info, pw_near, near, act0, s0, part],
        "",
        [pay_of(2), big, big, big, small, column, ((3, 8, wide), F32), ((2, wide), F32)]
        + [column, ((16, LANES), F32), column],
        [big, taps, shifts],
    )
    pay = everywhere(pay)
    pay, res, scaled, bg2, gg2 = call(
        stage_three_kernel,
        sz,
        [pay, proj, x_c, pix, act0, act1, s0, dc, s1, gate, seg_rows, par, tap, unit, info]
        + [pw_turned, part, squares, row1, slope1],
        "",
        [pay_of(8), small, big, ((chans,), F32), ((chans,), F32)],
        [big, big, taps, shifts, column],
    )
    far_pay = everywhere(pay)
    pay, gp0, bg1, gg1, mid = call(
        stage_four_kernel,
        sz,
        [far_pay, scaled, dc, ec, s0, row0, row1, par, tap, unit, info],
        "",
        [pay_of(8), big, ((wide,), F32), ((wide,), F32), ((2, wide), F32)],
        [shifts],
    )
    sent = call(
        back_kernel,
        sz,
        [gp0, res, wide0, w_near],
        "",
        [block] * tiles,
        [((tiles,) + block[0], BF16)],
    )
    pay = everywhere(pay)
    sent = passed(sz, sent)
    far = call(
        far_kernel,
        sz,
        [far_pay, x_input, far_info, row0, w_near, gp0],
        "vvvvva",
        [((chans, wide), F32), ((chans, wide), F32), ((chans + 8, LANES), F32)]
        + [((rows, LANES, 32), BF16)],
        [column, ((32, LANES), F32)],
    )
    block_out, x_grad, ew, gg0, bg0, dw, rw, rb, sw, sb, pw, rms = call(
        last_kernel,
        sz,
        [pay] + list(far) + [row0, row1, mid, par, w_near, cotangent] + sent,
        "",
        [
            (x_input.shape, BF16),
            (x_input.shape, BF16),
            ((chans, wide), F32),
            ((wide,), F32),
            ((wide,), F32),
            (dw_kernel.shape, F32),
            ((squeeze, wide), F32),
            ((squeeze,), F32),
            ((squeeze, wide), F32),
            ((wide,), F32),
            ((chans, wide), F32),
            ((5,), F32),
        ],
        [((rows, LANES, chans), F32), column],
    )
    return (
        block_out,
        x_grad,
        ew,
        gg0,
        bg0,
        dw,
        gg1,
        bg1,
        rw.T,
        rb,
        sw,
        sb,
        pw.T,
        gg2,
        bg2,
        rms,
    )


def solution(mesh):
    split = P("seg", "tile", None, None)
    return jax.shard_map(
        shards,
        mesh=mesh,
        in_specs=(split,) + (P(),) * 13 + (split, P("seg"), P("seg")),
        out_specs=(split, split) + (P(),) * 14,
        check_vma=False,
    )
```
